128 devices in a mesh: pipe: 8 (over x, y_hi), dp: 16 (over z, y_lo, core).
Axes of the slice: x: 4, y: 4 (y_hi: 2, y_lo: 2; y = y_hi * 2 + y_lo), z: 4, core: 2. Of those that a mesh axis runs over, the one named last changes fastest.
Arguments:
- hidden_in: bfloat16 [8, 8192, 7168], P('pipe', 'dp'), may hold values from -6 to 6
- weight: bfloat16 [8, 7168, 576], P('pipe'), may hold values from -0.0625 to 0.0625
- gain: float32 [8, 512], P('pipe'), may hold values from 0.25 to 1.75
- latent_cot: bfloat16 [8, 8192, 512], P('pipe', 'dp'), may hold values from -0.06591797 to 0.06591797
- rope_cot: bfloat16 [8, 8192, 64], P('pipe', 'dp'), may hold values from -0.06591797 to 0.06591797
- master_weight: float32 [8, 7168, 576], P('pipe', 'dp'), may hold values from -0.0625 to 0.0625
- first_moment: float32 [8, 7168, 576], P('pipe', 'dp'), may hold values from -2 to 2
- second_moment: float32 [8, 7168, 576], P('pipe', 'dp'), may hold values from 0.01 to 1
- gain_master: float32 [8, 512], P('pipe', 'dp'), may hold values from 0.25 to 1.75
- gain_first: float32 [8, 512], P('pipe', 'dp'), may hold values from -2 to 2
- gain_second: float32 [8, 512], P('pipe', 'dp'), may hold values from 0.01 to 1
Outputs:
- received_grad: bfloat16 [8, 8192, 7168], P('pipe', 'dp')
- next_master: float32 [8, 7168, 576], P('pipe', 'dp')
- next_first: float32 [8, 7168, 576], P('pipe', 'dp')
- next_second: float32 [8, 7168, 576], P('pipe', 'dp')
- next_gain_master: float32 [8, 512], P('pipe', 'dp')
- next_gain_first: float32 [8, 512], P('pipe', 'dp')
- next_gain_second: float32 [8, 512], P('pipe', 'dp')
The draws below stay inside these ranges and needn't reach their ends.
All inputs are finite; a program needn't handle non-finite values.
Results may differ from the reference program's by a relative error of at most 0.0049.
Values may be sent and summed in bfloat16 or wider, within the bound.
No kernel may reach another device: no remote copies, remote signals or barrier semaphores. Data moves between devices by JAX's collectives and lax.ppermute only.
A program may use at most 192 MiB of HBM per device.

```python
import math
import jax
import jax.numpy as jnp
from jax import lax

D = 7168
LAT = 512
ROPE = 64
TOK_DEV = 512
RANKS = 8
TOKENS = 8192
WID = 576
N_DP = 16


def block_levels(key, extent, shards, low, top_value):
    factor_of, own = 1.0, jax.random.fold_in(key, 6)
    for axis_at, parts in shards:
        steps = jnp.exp(jax.random.uniform(jax.random.fold_in(own, axis_at), (parts,), jnp.float32, low / len(shards), top_value / len(shards)))
        factor_of = factor_of * jnp.repeat(steps, extent[axis_at] // parts).reshape([-1 if axis == axis_at else 1 for axis in range(len(extent))])
    return factor_of


def bell_draw(own_key, extent, deviation, limit, shards=(), held_as=jnp.bfloat16):
    entries = jax.random.normal(own_key, extent, jnp.float32) * deviation
    if len(shards) > 0:
        entries = block_levels(own_key, extent, shards, -0.22, 0.18) * entries
    return jnp.clip(entries, min=-limit, max=limit).astype(held_as)


def setup_inputs(seed: int = 0) -> dict:
    splits = jax.random.split(jax.random.key(seed), 12)
    return {
        "hidden_in": bell_draw(splits[0], (RANKS, TOKENS, D), 1.0, 6.0, ((0, 8), (1, 16))),
        "weight": bell_draw(splits[1], (RANKS, D, WID), D ** -0.5, 0.0625, ((0, 8),)),
        "gain": jnp.clip(1.0 + 0.15 * jax.random.normal(splits[2], (RANKS, LAT), jnp.float32), 0.25, 1.75),
        "latent_cot": bell_draw(splits[3], (RANKS, TOKENS, LAT), (1.0 / (TOK_DEV * N_DP) ** 0.5), 0.06591797, ((0, 8), (1, 16))),
        "rope_cot": bell_draw(splits[4], (RANKS, TOKENS, ROPE), (1.0 / (TOK_DEV * N_DP) ** 0.5), 0.06591797, ((0, 8), (1, 16))),
        "master_weight": bell_draw(splits[5], (RANKS, D, WID), D ** -0.5, 0.0625, ((0, 8), (1, 16)), jnp.float32),
        "first_moment": bell_draw(splits[6], (RANKS, D, WID), 0.3, 2.0, ((0, 8), (1, 16)), jnp.float32),
        "second_moment": jnp.clip(jnp.exp(math.log(1.0) - 4.6051702 * jax.random.uniform(splits[7], (RANKS, D, WID), jnp.float32) ** block_levels(splits[7], (RANKS, D, WID), ((0, 8), (1, 16)), -0.2, 0.2)), 0.01, 1.0),
        "gain_master": jnp.clip(1.0 + 0.15 * jax.random.normal(splits[8], (RANKS, LAT), jnp.float32), 0.25, 1.75),
        "gain_first": bell_draw(splits[9], (RANKS, LAT), 0.3, 2.0, ((0, 8), (1, 16)), jnp.float32),
        "gain_second": jnp.clip(jnp.exp(math.log(1.0) - 4.6051702 * jax.random.uniform(splits[10], (RANKS, LAT), jnp.float32) ** block_levels(splits[10], (RANKS, LAT), ((0, 8), (1, 16)), -0.2, 0.2)), 0.01, 1.0),
    }


beta_one = 0.9
beta_two = 0.95
adam_count = 10
learn_rate = 0.00022
adam_eps = 1e-08
decay_rate = 0.1

def section_grads(hidden_in, weight, gain, latent_cot, rope_cot):
    rows = hidden_in.shape[0]
    latent = jnp.dot(hidden_in, weight[:, :LAT], preferred_element_type=jnp.float32)
    inv = lax.rsqrt(lax.optimization_barrier(jnp.mean(latent * latent, axis=-1, keepdims=True)) + 1e-06)
    normed = latent * inv
    cot = latent_cot.astype(jnp.float32)
    scaled = cot * gain[None, :]
    latent_grad = inv * (scaled - normed * lax.optimization_barrier(jnp.mean(scaled * normed, axis=-1, keepdims=True)))
    gain_part = lax.optimization_barrier(jnp.sum(cot * normed, axis=0))
    half = ROPE // 2
    position = (jnp.arange(rows) % TOK_DEV).astype(jnp.float32)
    freqs = 10000.0 ** (-2.0 * jnp.arange(half).astype(jnp.float32) / ROPE)
    angle = position[:, None] * freqs[None, :]
    cosine = jnp.cos(angle)
    sine = jnp.sin(angle)
    rope = rope_cot.astype(jnp.float32)
    first = rope[:, :half]
    second = rope[:, half:]
    out_grad = jnp.concatenate([latent_grad, first * cosine + second * sine, second * cosine - first * sine], axis=-1).astype(jnp.bfloat16)
    input_grad = lax.dot_general(out_grad, weight, (((1,), (1,)), ((), ())), preferred_element_type=jnp.float32).astype(jnp.bfloat16)
    weight_part = lax.dot_general(hidden_in, out_grad, (((0,), (0,)), ((), ())), preferred_element_type=jnp.float32)
    return (input_grad, weight_part, gain_part)

def adamw(master, first, second, grad):
    new_first = beta_one * first + (1.0 - beta_one) * grad
    new_second = beta_two * second + (1.0 - beta_two) * grad * grad
    first_hat = new_first / (1.0 - beta_one ** adam_count)
    second_hat = new_second / (1.0 - beta_two ** adam_count)
    new_master = master - learn_rate * (first_hat / (jnp.sqrt(second_hat) + adam_eps) + decay_rate * master)
    return (new_master, new_first, new_second)

def reference(hidden_in, weight, gain, latent_cot, rope_cot, master_weight, first_moment, second_moment, gain_master, gain_first, gain_second):

    def one_rank(items):
        return section_grads(items[0], items[1], items[2], items[3], items[4])
    input_grad, weight_part, gain_part = lax.map(one_rank, (hidden_in, weight, gain, latent_cot, rope_cot))
    total = weight_part + weight_part[::-1]
    gain_total = gain_part + gain_part[::-1]
    received_grad = jnp.concatenate([input_grad[1:], jnp.zeros_like(input_grad[:1])], axis=0)
    next_master, next_first, next_second = adamw(master_weight, first_moment, second_moment, total)
    next_gain_master, next_gain_first, next_gain_second = adamw(gain_master, gain_first, gain_second, gain_total)
    return (received_grad, next_master, next_first, next_second, next_gain_master, next_gain_first, next_gain_second)
```

```python
import jax
import jax.numpy as jnp
from jax import lax
from jax.experimental import pallas as pl
from jax.experimental.pallas import tpu as pltpu
from jax.sharding import PartitionSpec as P

beta_one = 0.9
beta_two = 0.95
adam_count = 10
learn_rate = 0.00022
adam_eps = 1e-08
decay_rate = 0.1

RANKS, SHARDS = 8, 16
TOK, WIDTH, LAT, ROPE = 512, 7168, 512, 64
COLS = LAT + ROPE
BLOCK = WIDTH // 8
TILE = 512
HALF = COLS // 2
ROWS_A = 3 * HALF + HALF // 2
ROWS_B = ROWS_A + 16
EXT = COLS + 16
BF, F32 = jnp.bfloat16, jnp.float32
MIB = 1 << 20


def params(mib):
    return pltpu.CompilerParams(vmem_limit_bytes=mib * MIB)


def cost(flops, moved):
    return pl.CostEstimate(flops=flops, bytes_accessed=moved, transcendentals=0)


def moved(value, target):
    pairs = []
    for r in range(RANKS):
        for d in range(SHARDS):
            to = target(r, d)
            if 0 <= to[0] < RANKS:
                pairs.append((r * SHARDS + d, to[0] * SHARDS + to[1]))
    return lax.ppermute(value, ("pipe", "dp"), pairs)


def to_core(r, d):
    return r, d ^ 1


def to_ylo(r, d):
    return r, d ^ 2


def to_z(steps):
    return lambda r, d: (r, (d + 4 * steps) % SHARDS)


def to_mirror(r, d):
    return RANKS - 1 - r, d


def to_before(r, d):
    return r - 1, d


def to_before_near(r, d):
    return r - 1, d ^ 2


def cut_kernel(s, hidden, weight, part, piece):
    part[...] = hidden[:, pl.ds(pl.multiple_of(384 * (1 - s[2]), 128), TILE)]

    @pl.when(pl.program_id(0) == 0)
    def _():
        piece[...] = weight[...]


def cut(s, hidden, weight):
    return pl.pallas_call(
        cut_kernel,
        grid_spec=pltpu.PrefetchScalarGridSpec(
            num_scalar_prefetch=1,
            grid=(8,),
            in_specs=[
                pl.BlockSpec((TOK, BLOCK), lambda b, s: (0, b)),
                pl.BlockSpec((HALF, BLOCK), lambda b, s: (s[2], 2 * s[0] + 1 - s[1])),
            ],
            out_specs=[
                pl.BlockSpec((TOK, TILE), lambda b, s: (0, b)),
                pl.BlockSpec((HALF, BLOCK), lambda b, s: (0, 0)),
            ],
        ),
        out_shape=[
            jax.ShapeDtypeStruct((TOK, 8 * TILE), BF),
            jax.ShapeDtypeStruct((HALF, BLOCK), BF),
        ],
        compiler_params=params(24),
        cost_estimate=cost(0, 12_500_000),
        name="cut",
    )(s, hidden, weight)


def latent_kernel(hidden, weight, cot, gain, rope, out, total):
    k = pl.program_id(0)
    part = lax.dot_general(
        hidden[...], weight[...], (((1,), (1,)), ((), ())), preferred_element_type=F32
    )

    @pl.when(k == 0)
    def _():
        total[...] = part

    @pl.when(k > 0)
    def _():
        total[...] += part

    @pl.when(k == pl.num_programs(0) - 1)
    def _():
        latent = total[...]
        inv = lax.rsqrt(jnp.mean(latent * latent, axis=-1, keepdims=True) + 1e-06)
        normed = latent * inv
        c = cot[...].astype(F32)
        scaled = c * gain[...]
        grad = inv * (scaled - normed * jnp.mean(scaled * normed, axis=-1, keepdims=True))
        gain_part = jnp.sum(c * normed, axis=0, keepdims=True)
        out[0:LAT, :] = grad.T.astype(BF)
        out[LAT:COLS, :] = rope[...]
        high = gain_part.astype(BF)
        low = (gain_part - high.astype(F32)).astype(BF)
        row = lax.broadcasted_iota(jnp.int32, (16, LAT), 0)
        high = jnp.broadcast_to(high.astype(F32), (16, LAT))
        low = jnp.broadcast_to(low.astype(F32), (16, LAT))
        both = jnp.where(row == 0, high, jnp.where(row == 1, low, 0.0))
        out[COLS:EXT, :] = both.astype(BF)


def latent_step(hidden, weight, cot, gain, rope):
    width = 1024
    return pl.pallas_call(
        latent_kernel,
        grid=(WIDTH // width,),
        in_specs=[
            pl.BlockSpec((TOK, width), lambda k: (0, k)),
            pl.BlockSpec((LAT, width), lambda k: (0, k)),
            pl.BlockSpec((TOK, LAT), lambda k: (0, 0)),
            pl.BlockSpec((1, LAT), lambda k: (0, 0)),
            pl.BlockSpec((ROPE, TOK), lambda k: (0, 0)),
        ],
        out_specs=pl.BlockSpec((EXT, TOK), lambda k: (0, 0)),
        out_shape=jax.ShapeDtypeStruct((EXT, TOK), BF),
        scratch_shapes=[pltpu.VMEM((TOK, LAT), F32)],
        compiler_params=params(32),
        cost_estimate=cost(2 * TOK * WIDTH * LAT, 16_000_000),
        name="latent_grad",
    )(hidden, weight, cot, gain, rope)


def weight_kernel(
    s, hidden, other, grad, grad_other, own_a, z1, z2, z3, own_b, send_b, gain
):
    g = pl.program_id(0)
    k, e = g // 2, g % 2
    core = s[2]

    @pl.when(g == 0)
    def _():
        sums = jnp.zeros((1, LAT), F32)
        for ref in (grad, grad_other):
            pair = ref[COLS:EXT, :].astype(F32)
            sums = sums + pair[0:1] + pair[1:2]
        gain[...] = jnp.zeros_like(gain)
        for i in range(4):
            gain[i : i + 1, :] = sums[:, 128 * i : 128 * i + 128]

    own = hidden[:, pl.ds(pl.multiple_of(384 * core, 128), TILE)]
    lane = lax.broadcasted_iota(jnp.int32, (HALF // 2, 128), 1)
    first = core == 0

    def packed(h):
        rows = slice(h * HALF, h * HALF + HALF)
        full = jnp.dot(grad[rows, :], own, preferred_element_type=F32)
        full += jnp.dot(grad_other[rows, :], other[...], preferred_element_type=F32)
        col = [full[:, 128 * j : 128 * j + 128] for j in range(4)]
        edge = jnp.where(first, col[3], col[0])
        top, low = edge[: HALF // 2], edge[HALF // 2 :]
        left = jnp.where(first, top, pltpu.roll(top, 64, 1))
        right = jnp.where(first, pltpu.roll(low, 64, 1), low)
        return [jnp.where(first, col[i], col[i + 1]) for i in range(3)] + [
            jnp.where(lane < 64, left, right)
        ]

    a, b = packed(0), packed(1)

    def put(ref, parts, with_gain):
        at = 0
        for part in parts:
            n = part.shape[0]
            ref[0, at : at + n, :] = part.astype(ref.dtype)
            at += n
        if with_gain:
            ref[0, at : at + 16, :] = gain[...].astype(ref.dtype)

    for number, ref in enumerate((own_a, z1, z2, z3)):
        pl.when(k == number)(lambda ref=ref: put(ref, a, False))
    pl.when(e == 0)(lambda: put(own_b, b, True))
    pl.when(e == 1)(lambda: put(send_b, b, True))


def weight_step(s, hidden, other, grad, grad_other):
    def at(k):
        return lambda g, s: (jnp.clip(g - 2 * k, 0, 1), 0, 0)

    def block(g, s):
        z = lax.rem(s[0] + g // 2, 4)
        return 2 * z + lax.rem(s[1] + g % 2, 2)

    return pl.pallas_call(
        weight_kernel,
        grid_spec=pltpu.PrefetchScalarGridSpec(
            num_scalar_prefetch=1,
            grid=(8,),
            in_specs=[
                pl.BlockSpec((TOK, BLOCK), lambda g, s: (0, block(g, s))),
                pl.BlockSpec((TOK, TILE), lambda g, s: (0, block(g, s))),
                pl.BlockSpec((EXT, TOK), lambda g, s: (0, 0)),
                pl.BlockSpec((EXT, TOK), lambda g, s: (0, 0)),
            ],
            out_specs=[pl.BlockSpec((1, ROWS_A, 128), at(k)) for k in range(4)]
            + [pl.BlockSpec((1, ROWS_B, 128), lambda g, s: (g // 2, 0, 0))] * 2,
            scratch_shapes=[pltpu.VMEM((16, 128), F32)],
        ),
        out_shape=[jax.ShapeDtypeStruct((2, ROWS_A, 128), F32)]
        + [jax.ShapeDtypeStruct((2, ROWS_A, 128), BF)] * 3
        + [
            jax.ShapeDtypeStruct((4, ROWS_B, 128), F32),
            jax.ShapeDtypeStruct((4, ROWS_B, 128), BF),
        ],
        compiler_params=params(40),
        cost_estimate=cost(2 * 2 * TOK * 8 * TILE * COLS, 20_000_000),
        name="weight_grad",
    )(s, hidden, other, grad, grad_other)


def sum_a_kernel(own, r1, r2, r3, keep, send):
    total = own[0] + r1[0].astype(F32) + r2[0].astype(F32) + r3[0].astype(F32)

    @pl.when(pl.program_id(0) == 0)
    def _():
        keep[...] = total

    @pl.when(pl.program_id(0) == 1)
    def _():
        send[...] = total.astype(BF)


def sum_a(own, r1, r2, r3):
    return pl.pallas_call(
        sum_a_kernel,
        grid=(2,),
        in_specs=[pl.BlockSpec((1, ROWS_A, 128), lambda e: (e, 0, 0))] * 4,
        out_specs=[pl.BlockSpec((ROWS_A, 128), lambda e: (0, 0))] * 2,
        out_shape=[
            jax.ShapeDtypeStruct((ROWS_A, 128), F32),
            jax.ShapeDtypeStruct((ROWS_A, 128), BF),
        ],
        compiler_params=params(16),
        cost_estimate=cost(0, 3_500_000),
        name="sum_z",
    )(own, r1, r2, r3)


def sum_b_kernel(own, r, keep, s1, s2, s3):
    total = own[0] + r[0].astype(F32)
    k = pl.program_id(0)
    for number, ref in enumerate((keep, s1, s2, s3)):

        def put(ref=ref):
            ref[...] = total.astype(ref.dtype)

        pl.when(k == number)(put)


def sum_b(own, r):
    return pl.pallas_call(
        sum_b_kernel,
        grid=(4,),
        in_specs=[pl.BlockSpec((1, ROWS_B, 128), lambda k: (k, 0, 0))] * 2,
        out_specs=[pl.BlockSpec((ROWS_B, 128), lambda k: (0, 0))] * 4,
        out_shape=[jax.ShapeDtypeStruct((ROWS_B, 128), F32)]
        + [jax.ShapeDtypeStruct((ROWS_B, 128), BF)] * 3,
        compiler_params=params(16),
        cost_estimate=cost(0, 4_500_000),
        name="sum_y",
    )(own, r)


def sum_all_kernel(keep_a, ra, keep_b, r1, r2, r3, total, send):
    a = keep_a[...] + ra[...].astype(F32)
    b = keep_b[...] + r1[...].astype(F32) + r2[...].astype(F32) + r3[...].astype(F32)
    total[:ROWS_A, :] = a
    total[ROWS_A:, :] = b
    send[:ROWS_A, :] = a.astype(BF)
    send[ROWS_A:, :] = b.astype(BF)


def sum_all(*parts):
    return pl.pallas_call(
        sum_all_kernel,
        out_shape=[
            jax.ShapeDtypeStruct((ROWS_A + ROWS_B, 128), F32),
            jax.ShapeDtypeStruct((ROWS_A + ROWS_B, 128), BF),
        ],
        compiler_params=params(16),
        cost_estimate=cost(0, 4_000_000),
        name="sum_shard",
    )(*parts)


def adamw(master, first, second, grad):
    new_first = beta_one * first + (1.0 - beta_one) * grad
    new_second = beta_two * second + (1.0 - beta_two) * grad * grad
    first_hat = new_first / (1.0 - beta_one**adam_count)
    second_hat = new_second / (1.0 - beta_two**adam_count)
    new_master = master - learn_rate * (
        first_hat / (jnp.sqrt(second_hat) + adam_eps) + decay_rate * master
    )
    return (new_master, new_first, new_second)


def adam_kernel(s, own, far, master, first, second, n_master, n_first, n_second, gain, grad):
    total = own[...] + far[...].astype(F32)
    core = s[2]
    gain[...] = total[2 * ROWS_A : 2 * ROWS_A + 8]

    def both(lo, n):
        return [total[h * ROWS_A + lo : h * ROWS_A + lo + n] for h in range(2)]

    for i in range(3):
        block = jnp.concatenate(both(i * HALF, HALF), axis=0)
        grad[pl.ds(pl.multiple_of(64 * core + 128 * i, 64), 128), :] = block.T
    edge = []
    for part in both(3 * HALF, HALF // 2):
        edge += [part, pltpu.roll(part, 64, 1)]
    block = jnp.concatenate(edge, axis=0)
    grad[pl.ds(pl.multiple_of(384 * (1 - core), 64), 64), :] = block.T[:64]
    n_master[...], n_first[...], n_second[...] = adamw(
        master[...], first[...], second[...], grad[...]
    )


def adam_step(s, own, far, master, first, second):
    shape = jax.ShapeDtypeStruct(master.shape, F32)
    spec = pl.BlockSpec(memory_space=pltpu.VMEM)
    return pl.pallas_call(
        adam_kernel,
        in_specs=[pl.BlockSpec(memory_space=pltpu.SMEM)] + [spec] * 5,
        out_specs=[spec] * 4,
        out_shape=[shape] * 3 + [jax.ShapeDtypeStruct((8, 128), F32)],
        scratch_shapes=[pltpu.VMEM(master.shape, F32)],
        compiler_params=params(32),
        cost_estimate=cost(0, 9_000_000),
        name="adamw",
    )(s, own, far, master, first, second)


def input_kernel(grad, weight, out, turned):
    @pl.when(pl.program_id(0) == 0)
    def _():
        turned[...] = grad[:COLS, :].astype(F32).T.astype(BF)

    block = weight[...].reshape(COLS, BLOCK)
    out[...] = jnp.dot(turned[...], block, preferred_element_type=F32).astype(BF)


def input_step(grad, weight):
    return pl.pallas_call(
        input_kernel,
        grid=(8,),
        in_specs=[
            pl.BlockSpec((EXT, TOK), lambda b: (0, 0)),
            pl.BlockSpec((2, HALF, BLOCK), lambda b: (b, 0, 0)),
        ],
        out_specs=pl.BlockSpec((TOK, BLOCK), lambda b: (0, b)),
        out_shape=jax.ShapeDtypeStruct((TOK, WIDTH), BF),
        scratch_shapes=[pltpu.VMEM((TOK, COLS), BF)],
        compiler_params=params(32),
        cost_estimate=cost(2 * TOK * WIDTH * COLS, 16_000_000),
        name="input_grad",
    )(grad, weight)


def rope_step(rope_cot):
    half = ROPE // 2
    position = jnp.arange(TOK).astype(F32)
    freqs = 10000.0 ** (-2.0 * jnp.arange(half).astype(F32) / ROPE)
    angle = freqs[:, None] * position[None, :]
    cosine = jnp.cos(angle)
    sine = jnp.sin(angle)
    rope = rope_cot.T.astype(F32)
    first, second = rope[:half], rope[half:]
    return jnp.concatenate(
        [first * cosine + second * sine, second * cosine - first * sine], axis=0
    ).astype(BF)


def on_device(
    hidden_in,
    weight,
    gain,
    latent_cot,
    rope_cot,
    master_weight,
    first_moment,
    second_moment,
    gain_master,
    gain_first,
    gain_second,
):
    shard = lax.axis_index("dp")
    s = jnp.stack([shard // 4, (shard // 2) % 2, shard % 2]).astype(jnp.int32)
    hidden = hidden_in[0]
    turned = weight[0].T
    part, piece = cut(s, hidden, turned)
    piece_next = moved(piece, to_before_near)
    other = moved(part, to_core)
    weight_next = lax.all_gather(piece_next, "dp")
    grad = latent_step(hidden, turned, latent_cot[0], gain, rope_step(rope_cot[0]))
    grad_other = moved(grad, to_core)
    grad_next = moved(grad, to_before)
    own_a, z1, z2, z3, own_b, send_b = weight_step(s, hidden, other, grad, grad_other)
    r1, r2, r3 = moved(z1, to_z(1)), moved(z2, to_z(2)), moved(z3, to_z(3))
    rb = moved(send_b, to_ylo)
    keep_a, send_a = sum_a(own_a, r1, r2, r3)
    keep_b, s1, s2, s3 = sum_b(own_b, rb)
    ra = moved(send_a, to_ylo)
    r1, r2, r3 = moved(s1, to_z(1)), moved(s2, to_z(2)), moved(s3, to_z(3))
    total, send = sum_all(keep_a, ra, keep_b, r1, r2, r3)
    far = moved(send, to_mirror)
    received = input_step(grad_next, weight_next)
    next_master, next_first, next_second, gain_rows = adam_step(
        s, total, far, master_weight[0], first_moment[0], second_moment[0]
    )
    gain_total = lax.dynamic_slice(gain_rows[:4].reshape(LAT), (shard * 32,), (32,))
    next_gain = adamw(gain_master[0], gain_first[0], gain_second[0], gain_total)
    return (
        received[None],
        next_master[None],
        next_first[None],
        next_second[None],
        *(value[None] for value in next_gain),
    )


def solution(mesh):
    tokens, shared = P("pipe", "dp", None), P("pipe", None)
    split = P("pipe", "dp")
    return jax.shard_map(
        on_device,
        mesh=mesh,
        in_specs=(tokens, P("pipe", None, None), shared) + (tokens,) * 5 + (split,) * 3,
        out_specs=(tokens,) * 4 + (split,) * 3,
        check_vma=False,
    )
```

```python
import jax
import jax.numpy as jnp
from jax import lax
from jax.experimental import pallas as pl
from jax.experimental.pallas import tpu as pltpu
from jax.sharding import PartitionSpec as P

beta_one = 0.9
beta_two = 0.95
adam_count = 10
learn_rate = 0.00022
adam_eps = 1e-08
decay_rate = 0.1

RANKS, SHARDS = 8, 16
TOK, WIDTH, LAT, ROPE = 512, 7168, 512, 64
COLS = LAT + ROPE
BLOCK = WIDTH // 8
TILE = 512
HALF = COLS // 2
ROWS_A = 3 * HALF + HALF // 2
ROWS_B = ROWS_A + 16
EXT = COLS + 16
BF, F32 = jnp.bfloat16, jnp.float32
MIB = 1 << 20


def params(mib):
    return pltpu.CompilerParams(vmem_limit_bytes=mib * MIB)


def cost(flops, moved):
    return pl.CostEstimate(flops=flops, bytes_accessed=moved, transcendentals=0)


def moved(value, target):
    pairs = []
    for r in range(RANKS):
        for d in range(SHARDS):
            to = target(r, d)
            if 0 <= to[0] < RANKS:
                pairs.append((r * SHARDS + d, to[0] * SHARDS + to[1]))
    return lax.ppermute(value, ("pipe", "dp"), pairs)


def to_core(r, d):
    return r, d ^ 1


def to_ylo(r, d):
    return r, d ^ 2


def to_z(steps):
    return lambda r, d: (r, (d + 4 * steps) % SHARDS)


def to_mirror(r, d):
    return RANKS - 1 - r, d


def to_before(r, d):
    return r - 1, d


def to_before_near(r, d):
    return r - 1, d ^ 2


FLAG = jax.ShapeDtypeStruct((8, 128), F32)
ANYWHERE = pl.BlockSpec(memory_space=pl.ANY)


def after_kernel(value, *rest):
    pass


def after(value, *earlier):
    return pl.pallas_call(
        after_kernel,
        in_specs=[ANYWHERE] * (1 + len(earlier)),
        out_specs=ANYWHERE,
        out_shape=jax.ShapeDtypeStruct(value.shape, value.dtype),
        input_output_aliases={0: 0},
        cost_estimate=cost(0, 0),
        name="after",
    )(value, *earlier)


def copy_kernel(s, value, out):
    out[...] = value[...]


def cut_weight(s, weight):
    return pl.pallas_call(
        copy_kernel,
        grid_spec=pltpu.PrefetchScalarGridSpec(
            num_scalar_prefetch=1,
            grid=(1,),
            in_specs=[pl.BlockSpec((HALF, BLOCK), lambda b, s: (s[2], 2 * s[0] + 1 - s[1]))],
            out_specs=pl.BlockSpec((HALF, BLOCK), lambda b, s: (0, 0)),
        ),
        out_shape=jax.ShapeDtypeStruct((HALF, BLOCK), BF),
        compiler_params=params(60),
        cost_estimate=cost(0, 1_000_000),
        name="cut_weight",
    )(s, weight)


def cut_kernel(s, hidden, earlier, part, flag):
    part[...] = hidden[:, pl.ds(pl.multiple_of(384 * (1 - s[2]), 128), TILE)]
    flag[...] = jnp.zeros_like(flag)


def cut(s, hidden, earlier):
    return pl.pallas_call(
        cut_kernel,
        grid_spec=pltpu.PrefetchScalarGridSpec(
            num_scalar_prefetch=1,
            grid=(8,),
            in_specs=[
                pl.BlockSpec((TOK, BLOCK), lambda b, s: (0, b)),
                ANYWHERE,
            ],
            out_specs=[
                pl.BlockSpec((TOK, TILE), lambda b, s: (0, b)),
                pl.BlockSpec((8, 128), lambda b, s: (0, 0)),
            ],
        ),
        out_shape=[jax.ShapeDtypeStruct((TOK, 8 * TILE), BF), FLAG],
        compiler_params=params(60),
        cost_estimate=cost(0, 12_500_000),
        name="cut_hidden",
    )(s, hidden, earlier)


def latent_kernel(hidden, weight, cot, gain, rope, earlier, out, total):
    k = pl.program_id(0)
    part = lax.dot_general(
        hidden[...], weight[...], (((1,), (1,)), ((), ())), preferred_element_type=F32
    )

    @pl.when(k == 0)
    def _():
        total[...] = part

    @pl.when(k > 0)
    def _():
        total[...] += part

    @pl.when(k == pl.num_programs(0) - 1)
    def _():
        latent = total[...]
        inv = lax.rsqrt(jnp.mean(latent * latent, axis=-1, keepdims=True) + 1e-06)
        normed = latent * inv
        c = cot[...].astype(F32)
        scaled = c * gain[...]
        grad = inv * (scaled - normed * jnp.mean(scaled * normed, axis=-1, keepdims=True))
        gain_part = jnp.sum(c * normed, axis=0, keepdims=True)
        out[0:LAT, :] = grad.T.astype(BF)
        out[LAT:COLS, :] = rope[...]
        high = gain_part.astype(BF)
        low = (gain_part - high.astype(F32)).astype(BF)
        row = lax.broadcasted_iota(jnp.int32, (16, LAT), 0)
        high = jnp.broadcast_to(high.astype(F32), (16, LAT))
        low = jnp.broadcast_to(low.astype(F32), (16, LAT))
        both = jnp.where(row == 0, high, jnp.where(row == 1, low, 0.0))
        out[COLS:EXT, :] = both.astype(BF)


def latent_step(hidden, weight, cot, gain, rope, earlier):
    width = 1024
    return pl.pallas_call(
        latent_kernel,
        grid=(WIDTH // width,),
        in_specs=[
            pl.BlockSpec((TOK, width), lambda k: (0, k)),
            pl.BlockSpec((LAT, width), lambda k: (0, k)),
            pl.BlockSpec((TOK, LAT), lambda k: (0, 0)),
            pl.BlockSpec((1, LAT), lambda k: (0, 0)),
            pl.BlockSpec((ROPE, TOK), lambda k: (0, 0)),
            ANYWHERE,
        ],
        out_specs=pl.BlockSpec((EXT, TOK), lambda k: (0, 0)),
        out_shape=jax.ShapeDtypeStruct((EXT, TOK), BF),
        scratch_shapes=[pltpu.VMEM((TOK, LAT), F32)],
        compiler_params=params(60),
        cost_estimate=cost(2 * TOK * WIDTH * LAT, 16_000_000),
        name="latent_grad",
    )(hidden, weight, cot, gain, rope, earlier)


def weight_kernel(
    s, hidden, other, grad, grad_other, own_a, z1, z2, z3, own_b, send_b, gain
):
    g = pl.program_id(0)
    k, e = g // 2, g % 2
    core = s[2]

    @pl.when(g == 0)
    def _():
        sums = jnp.zeros((1, LAT), F32)
        for ref in (grad, grad_other):
            pair = ref[COLS:EXT, :].astype(F32)
            sums = sums + pair[0:1] + pair[1:2]
        gain[...] = jnp.zeros_like(gain)
        for i in range(4):
            gain[i : i + 1, :] = sums[:, 128 * i : 128 * i + 128]

    own = hidden[:, pl.ds(pl.multiple_of(384 * core, 128), TILE)]
    lane = lax.broadcasted_iota(jnp.int32, (HALF // 2, 128), 1)
    first = core == 0

    whole = jnp.dot(grad[:COLS, :], own, preferred_element_type=F32)
    whole += jnp.dot(grad_other[:COLS, :], other[...], preferred_element_type=F32)

    def packed(h):
        full = whole[h * HALF : h * HALF + HALF]
        col = [full[:, 128 * j : 128 * j + 128] for j in range(4)]
        edge = jnp.where(first, col[3], col[0])
        top, low = edge[: HALF // 2], edge[HALF // 2 :]
        left = jnp.where(first, top, pltpu.roll(top, 64, 1))
        right = jnp.where(first, pltpu.roll(low, 64, 1), low)
        return [jnp.where(first, col[i], col[i + 1]) for i in range(3)] + [
            jnp.where(lane < 64, left, right)
        ]

    a, b = packed(0), packed(1)

    def put(ref, parts, with_gain):
        at = 0
        for part in parts:
            n = part.shape[0]
            ref[0, at : at + n, :] = part.astype(ref.dtype)
            at += n
        if with_gain:
            ref[0, at : at + 16, :] = gain[...].astype(ref.dtype)

    for number, ref in enumerate((own_a, z1, z2, z3)):
        pl.when(k == number)(lambda ref=ref: put(ref, a, False))
    pl.when(e == 0)(lambda: put(own_b, b, True))
    pl.when(e == 1)(lambda: put(send_b, b, True))


def weight_step(s, hidden, other, grad, grad_other):
    def at(k):
        return lambda g, s: (jnp.clip(g - 2 * k, 0, 1), 0, 0)

    def block(g, s):
        z = lax.rem(s[0] + g // 2, 4)
        return 2 * z + lax.rem(s[1] + g % 2, 2)

    return pl.pallas_call(
        weight_kernel,
        grid_spec=pltpu.PrefetchScalarGridSpec(
            num_scalar_prefetch=1,
            grid=(8,),
            in_specs=[
                pl.BlockSpec((TOK, BLOCK), lambda g, s: (0, block(g, s))),
                pl.BlockSpec((TOK, TILE), lambda g, s: (0, block(g, s))),
                pl.BlockSpec((EXT, TOK), lambda g, s: (0, 0)),
                pl.BlockSpec((EXT, TOK), lambda g, s: (0, 0)),
            ],
            out_specs=[pl.BlockSpec((1, ROWS_A, 128), at(k)) for k in range(4)]
            + [pl.BlockSpec((1, ROWS_B, 128), lambda g, s: (g // 2, 0, 0))] * 2,
            scratch_shapes=[pltpu.VMEM((16, 128), F32)],
        ),
        out_shape=[jax.ShapeDtypeStruct((2, ROWS_A, 128), F32)]
        + [jax.ShapeDtypeStruct((2, ROWS_A, 128), BF)] * 3
        + [
            jax.ShapeDtypeStruct((4, ROWS_B, 128), F32),
            jax.ShapeDtypeStruct((4, ROWS_B, 128), BF),
        ],
        compiler_params=params(60),
        cost_estimate=cost(2 * 2 * TOK * 8 * TILE * COLS, 20_000_000),
        name="weight_grad",
    )(s, hidden, other, grad, grad_other)


def sum_a_kernel(own, r1, r2, r3, keep, send):
    total = own[0] + r1[0].astype(F32) + r2[0].astype(F32) + r3[0].astype(F32)

    @pl.when(pl.program_id(0) == 0)
    def _():
        keep[...] = total

    @pl.when(pl.program_id(0) == 1)
    def _():
        send[...] = total.astype(BF)


def sum_a(own, r1, r2, r3):
    return pl.pallas_call(
        sum_a_kernel,
        grid=(2,),
        in_specs=[pl.BlockSpec((1, ROWS_A, 128), lambda e: (e, 0, 0))] * 4,
        out_specs=[pl.BlockSpec((ROWS_A, 128), lambda e: (0, 0))] * 2,
        out_shape=[
            jax.ShapeDtypeStruct((ROWS_A, 128), F32),
            jax.ShapeDtypeStruct((ROWS_A, 128), BF),
        ],
        compiler_params=params(16),
        cost_estimate=cost(0, 3_500_000),
        name="sum_z",
    )(own, r1, r2, r3)


def sum_b_kernel(own, r, keep, s1, s2, s3):
    total = own[0] + r[0].astype(F32)
    k = pl.program_id(0)
    for number, ref in enumerate((keep, s1, s2, s3)):

        def put(ref=ref):
            ref[...] = total.astype(ref.dtype)

        pl.when(k == number)(put)


def sum_b(own, r):
    return pl.pallas_call(
        sum_b_kernel,
        grid=(4,),
        in_specs=[pl.BlockSpec((1, ROWS_B, 128), lambda k: (k, 0, 0))] * 2,
        out_specs=[pl.BlockSpec((ROWS_B, 128), lambda k: (0, 0))] * 4,
        out_shape=[jax.ShapeDtypeStruct((ROWS_B, 128), F32)]
        + [jax.ShapeDtypeStruct((ROWS_B, 128), BF)] * 3,
        compiler_params=params(16),
        cost_estimate=cost(0, 4_500_000),
        name="sum_y",
    )(own, r)


def sum_all_kernel(keep_a, ra, keep_b, r1, r2, r3, total, send, flag):
    a = keep_a[...] + ra[...].astype(F32)
    b = keep_b[...] + r1[...].astype(F32) + r2[...].astype(F32) + r3[...].astype(F32)
    total[:ROWS_A, :] = a
    total[ROWS_A:, :] = b
    send[:ROWS_A, :] = a.astype(BF)
    send[ROWS_A:, :] = b.astype(BF)
    flag[...] = jnp.zeros_like(flag)


def sum_all(*parts):
    return pl.pallas_call(
        sum_all_kernel,
        out_shape=[
            jax.ShapeDtypeStruct((ROWS_A + ROWS_B, 128), F32),
            jax.ShapeDtypeStruct((ROWS_A + ROWS_B, 128), BF),
            FLAG,
        ],
        compiler_params=params(16),
        cost_estimate=cost(0, 4_000_000),
        name="sum_shard",
    )(*parts)


def adamw(master, first, second, grad):
    new_first = beta_one * first + (1.0 - beta_one) * grad
    new_second = beta_two * second + (1.0 - beta_two) * grad * grad
    first_hat = new_first / (1.0 - beta_one**adam_count)
    second_hat = new_second / (1.0 - beta_two**adam_count)
    new_master = master - learn_rate * (
        first_hat / (jnp.sqrt(second_hat) + adam_eps) + decay_rate * master
    )
    return (new_master, new_first, new_second)


def adam_kernel(s, own, far, master, first, second, earlier, n_master, n_first, n_second, gain, grad):
    total = own[...] + far[...].astype(F32)
    core = s[2]
    gain[...] = total[2 * ROWS_A : 2 * ROWS_A + 8]

    def both(lo, n):
        return [total[h * ROWS_A + lo : h * ROWS_A + lo + n] for h in range(2)]

    for i in range(3):
        block = jnp.concatenate(both(i * HALF, HALF), axis=0)
        grad[pl.ds(pl.multiple_of(64 * core + 128 * i, 64), 128), :] = block.T
    edge = []
    for part in both(3 * HALF, HALF // 2):
        edge += [part, pltpu.roll(part, 64, 1)]
    block = jnp.concatenate(edge, axis=0)
    grad[pl.ds(pl.multiple_of(384 * (1 - core), 64), 64), :] = block.T[:64]
    n_master[...], n_first[...], n_second[...] = adamw(
        master[...], first[...], second[...], grad[...]
    )


def adam_step(s, own, far, master, first, second, earlier):
    shape = jax.ShapeDtypeStruct(master.shape, F32)
    spec = pl.BlockSpec(memory_space=pltpu.VMEM)
    return pl.pallas_call(
        adam_kernel,
        in_specs=[pl.BlockSpec(memory_space=pltpu.SMEM)]
        + [spec] * 5
        + [ANYWHERE],
        out_specs=[spec] * 4,
        out_shape=[shape] * 3 + [jax.ShapeDtypeStruct((8, 128), F32)],
        scratch_shapes=[pltpu.VMEM(master.shape, F32)],
        compiler_params=params(32),
        cost_estimate=cost(0, 9_000_000),
        name="adamw",
    )(s, own, far, master, first, second, earlier)


def input_kernel(grad, weight, earlier, out, flag, turned):
    @pl.when(pl.program_id(0) == 0)
    def _():
        turned[...] = grad[:COLS, :].astype(F32).T.astype(BF)
        flag[...] = jnp.zeros_like(flag)

    block = weight[...].reshape(COLS, BLOCK)
    out[...] = jnp.dot(turned[...], block, preferred_element_type=F32).astype(BF)


def input_step(grad, weight, earlier):
    return pl.pallas_call(
        input_kernel,
        grid=(8,),
        in_specs=[
            pl.BlockSpec((EXT, TOK), lambda b: (0, 0)),
            pl.BlockSpec((2, HALF, BLOCK), lambda b: (b, 0, 0)),
            ANYWHERE,
        ],
        out_specs=[
            pl.BlockSpec((TOK, BLOCK), lambda b: (0, b)),
            pl.BlockSpec((8, 128), lambda b: (0, 0)),
        ],
        out_shape=[jax.ShapeDtypeStruct((TOK, WIDTH), BF), FLAG],
        scratch_shapes=[pltpu.VMEM((TOK, COLS), BF)],
        compiler_params=params(60),
        cost_estimate=cost(2 * TOK * WIDTH * COLS, 16_000_000),
        name="input_grad",
    )(grad, weight, earlier)


def rope_step(rope_cot):
    half = ROPE // 2
    position = jnp.arange(TOK).astype(F32)
    freqs = 10000.0 ** (-2.0 * jnp.arange(half).astype(F32) / ROPE)
    angle = freqs[:, None] * position[None, :]
    cosine = jnp.cos(angle)
    sine = jnp.sin(angle)
    rope = rope_cot.T.astype(F32)
    first, second = rope[:half], rope[half:]
    return jnp.concatenate(
        [first * cosine + second * sine, second * cosine - first * sine], axis=0
    ).astype(BF)


def on_device(
    hidden_in,
    weight,
    gain,
    latent_cot,
    rope_cot,
    master_weight,
    first_moment,
    second_moment,
    gain_master,
    gain_first,
    gain_second,
):
    shard = lax.axis_index("dp")
    s = jnp.stack([shard >> 2, (shard >> 1) & 1, shard & 1]).astype(jnp.int32)
    hidden = hidden_in[0]
    turned = weight[0].T
    piece = cut_weight(s, turned)
    piece_next = moved(piece, to_before_near)
    part, is_cut = cut(s, hidden, piece)
    rope = rope_step(rope_cot[0])
    other = moved(part, to_core)
    grad = latent_step(hidden, turned, latent_cot[0], gain, rope, is_cut)
    grad_other = moved(grad, to_core)
    grad_next = moved(grad, to_before)
    weight_next = lax.all_gather(after(piece_next, grad, other), "dp")
    own_a, z1, z2, z3, own_b, send_b = weight_step(s, hidden, other, grad, grad_other)
    r1, r2, r3 = moved(z1, to_z(1)), moved(z2, to_z(2)), moved(z3, to_z(3))
    rb = moved(send_b, to_ylo)
    keep_a, send_a = sum_a(own_a, r1, r2, r3)
    keep_b, s1, s2, s3 = sum_b(own_b, rb)
    ra = moved(send_a, to_ylo)
    r1, r2, r3 = moved(s1, to_z(1)), moved(s2, to_z(2)), moved(s3, to_z(3))
    total, send, is_summed = sum_all(keep_a, ra, keep_b, r1, r2, r3)
    far = moved(send, to_mirror)
    received, is_received = input_step(grad_next, weight_next, is_summed)
    next_master, next_first, next_second, gain_rows = adam_step(
        s, total, far, master_weight[0], first_moment[0], second_moment[0], is_received
    )
    gain_total = lax.dynamic_slice(gain_rows[:4].reshape(LAT), (shard * 32,), (32,))
    next_gain = adamw(gain_master[0], gain_first[0], gain_second[0], gain_total)
    return (
        received[None],
        next_master[None],
        next_first[None],
        next_second[None],
        *(value[None] for value in next_gain),
    )


def solution(mesh):
    tokens, shared = P("pipe", "dp", None), P("pipe", None)
    split = P("pipe", "dp")
    return jax.shard_map(
        on_device,
        mesh=mesh,
        in_specs=(tokens, P("pipe", None, None), shared) + (tokens,) * 5 + (split,) * 3,
        out_specs=(tokens,) * 4 + (split,) * 3,
        check_vma=False,
    )
```

```python
import jax
import jax.numpy as jnp
from jax import lax
from jax.experimental import pallas as pl
from jax.experimental.pallas import tpu as pltpu
from jax.sharding import PartitionSpec as P

beta_one = 0.9
beta_two = 0.95
adam_count = 10
learn_rate = 0.00022
adam_eps = 1e-08
decay_rate = 0.1

RANKS, SHARDS = 8, 16
TOK, WIDTH, LAT, ROPE = 512, 7168, 512, 64
COLS = LAT + ROPE
BLOCK = WIDTH // 8
TILE = 512
HALF = COLS // 2
ROWS_A = 3 * HALF + HALF // 2
ROWS_B = ROWS_A + 16
EXT = COLS + 16
BF, F32 = jnp.bfloat16, jnp.float32
MIB = 1 << 20


def params(mib):
    return pltpu.CompilerParams(vmem_limit_bytes=mib * MIB)


def cost(flops, moved):
    return pl.CostEstimate(flops=flops, bytes_accessed=moved, transcendentals=0)


def moved(value, target):
    pairs = []
    for r in range(RANKS):
        for d in range(SHARDS):
            to = target(r, d)
            if 0 <= to[0] < RANKS:
                pairs.append((r * SHARDS + d, to[0] * SHARDS + to[1]))
    return lax.ppermute(value, ("pipe", "dp"), pairs)


def to_core(r, d):
    return r, d ^ 1


def to_ylo(r, d):
    return r, d ^ 2


def to_z(steps):
    return lambda r, d: (r, (d + 4 * steps) % SHARDS)


def to_mirror(r, d):
    return RANKS - 1 - r, d


def to_before(r, d):
    return r - 1, d


def to_before_near(r, d):
    return r - 1, d ^ 2


FLAG = jax.ShapeDtypeStruct((8, 128), F32)
ANYWHERE = pl.BlockSpec(memory_space=pltpu.HBM)
LATER = pl.BlockSpec(memory_space=pl.ANY)


def place():
    shard = lax.axis_index("dp")
    return shard >> 2, (shard >> 1) & 1, shard & 1


def columns(block, core):
    return pl.ds(pl.multiple_of(block * BLOCK + 384 * core, 128), TILE)


def start_all(copies):
    for copy in copies:
        copy.start()


def wait_all(copies):
    for copy in copies:
        copy.wait()


def after(value, *earlier):
    def kernel(*refs):
        pass

    return pl.pallas_call(
        kernel,
        in_specs=[ANYWHERE] + [LATER] * len(earlier),
        out_specs=ANYWHERE,
        out_shape=jax.ShapeDtypeStruct(value.shape, value.dtype),
        input_output_aliases={0: 0},
        cost_estimate=cost(0, 0),
        name="after",
    )(value, *earlier)


def cut_weight(weight, blocks, *earlier):
    def kernel(weight, *rest):
        out, sems = rest[-2:]
        z, y, core = place()
        rows = pl.ds(pl.multiple_of(core * HALF, HALF), HALF)
        copies = []
        for i, (dz, e) in enumerate(blocks):
            block = 2 * ((z + dz) & 3) + ((1 - y) ^ e)
            cols = pl.ds(pl.multiple_of(block * BLOCK, BLOCK), BLOCK)
            copies.append(pltpu.make_async_copy(weight.at[rows, cols], out.at[i], sems.at[i]))
        start_all(copies)
        wait_all(copies)

    count = len(blocks)
    return pl.pallas_call(
        kernel,
        in_specs=[ANYWHERE] + [LATER] * len(earlier),
        out_shape=jax.ShapeDtypeStruct((count, HALF, BLOCK), BF),
        scratch_shapes=[pltpu.SemaphoreType.DMA((count,))],
        compiler_params=params(60),
        cost_estimate=cost(0, 1_000),
        name="cut_weight",
    )(weight, *earlier)


PARTS = 7
PART = WIDTH // PARTS


def latent_kernel(hidden, weight, cot, gain, rope, earlier, out, tokens, matrix, sems):
    copies = []
    for i in range(PARTS):
        cols = pl.ds(i * PART, PART)
        copies.append(
            (
                pltpu.make_async_copy(hidden.at[:, cols], tokens.at[:, cols], sems.at[0, i]),
                pltpu.make_async_copy(
                    weight.at[pl.ds(0, LAT), cols], matrix.at[:, cols], sems.at[1, i]
                ),
            )
        )
    for pair in copies:
        start_all(pair)
    latent = jnp.zeros((TOK, LAT), F32)
    for i in range(PARTS):
        wait_all(copies[i])
        cols = slice(i * PART, i * PART + PART)
        latent += lax.dot_general(
            tokens[:, cols],
            matrix[:, cols],
            (((1,), (1,)), ((), ())),
            preferred_element_type=F32,
        )
    inv = lax.rsqrt(jnp.mean(latent * latent, axis=-1, keepdims=True) + 1e-06)
    normed = latent * inv
    c = cot[...].astype(F32)
    scaled = c * gain[...]
    grad = inv * (scaled - normed * jnp.mean(scaled * normed, axis=-1, keepdims=True))
    gain_part = jnp.sum(c * normed, axis=0, keepdims=True)
    out[0:LAT, :] = grad.T.astype(BF)
    out[LAT:COLS, :] = rope[...]
    high = gain_part.astype(BF)
    low = (gain_part - high.astype(F32)).astype(BF)
    row = lax.broadcasted_iota(jnp.int32, (16, LAT), 0)
    high = jnp.broadcast_to(high.astype(F32), (16, LAT))
    low = jnp.broadcast_to(low.astype(F32), (16, LAT))
    both = jnp.where(row == 0, high, jnp.where(row == 1, low, 0.0))
    out[COLS:EXT, :] = both.astype(BF)


def latent_step(hidden, weight, cot, gain, rope, earlier):
    inside = pl.BlockSpec(memory_space=pltpu.VMEM)
    return pl.pallas_call(
        latent_kernel,
        in_specs=[ANYWHERE, ANYWHERE, inside, inside, inside, LATER],
        out_shape=jax.ShapeDtypeStruct((EXT, TOK), BF),
        scratch_shapes=[
            pltpu.VMEM((TOK, WIDTH), BF),
            pltpu.VMEM((LAT, WIDTH), BF),
            pltpu.SemaphoreType.DMA((2, PARTS)),
        ],
        compiler_params=params(60),
        cost_estimate=cost(0, 1_000),
        name="latent_grad",
    )(hidden, weight, cot, gain, rope, earlier)


def weight_kernel(
    hidden,
    other,
    grad,
    grad_other,
    earlier,
    own_a,
    send_a,
    own_b,
    send_b,
    tiles,
    tiles_other,
    turned,
    turned_other,
    first_a,
    rest_a,
    keep_b,
    give_b,
    gain,
    in_sems,
    out_sems,
    grad_sems,
):
    z, y, core = place()
    steps = [(k, e) for k in (1, 2, 3, 0) for e in (1, 0)]
    incoming = []
    for i, (k, e) in enumerate(steps):
        cols = columns(2 * ((z + k) & 3) + (y ^ e), core)
        incoming.append(
            (
                pltpu.make_async_copy(hidden.at[:, cols], tiles.at[i], in_sems.at[0, i]),
                pltpu.make_async_copy(other.at[:, cols], tiles_other.at[i], in_sems.at[1, i]),
            )
        )
    grads = [
        pltpu.make_async_copy(grad, turned, grad_sems.at[0]),
        pltpu.make_async_copy(grad_other, turned_other, grad_sems.at[1]),
    ]
    start_all(grads)
    for pair in incoming:
        start_all(pair)
    wait_all(grads)

    sums = jnp.zeros((1, LAT), F32)
    for ref in (turned, turned_other):
        pair = ref[COLS:EXT, :].astype(F32)
        sums = sums + pair[0:1] + pair[1:2]
    gain[...] = jnp.zeros_like(gain)
    for i in range(4):
        gain[i : i + 1, :] = sums[:, 128 * i : 128 * i + 128]

    lane = lax.broadcasted_iota(jnp.int32, (HALF // 2, 128), 1)
    first = core == 0

    def packed(full):
        col = [full[:, 128 * j : 128 * j + 128] for j in range(4)]
        edge = jnp.where(first, col[3], col[0])
        top, low = edge[: HALF // 2], edge[HALF // 2 :]
        left = jnp.where(first, top, pltpu.roll(top, 64, 1))
        right = jnp.where(first, pltpu.roll(low, 64, 1), low)
        return [jnp.where(first, col[i], col[i + 1]) for i in range(3)] + [
            jnp.where(lane < 64, left, right)
        ]

    def put(ref, parts):
        at = 0
        for part in parts:
            n = part.shape[0]
            ref[at : at + n, :] = part.astype(ref.dtype)
            at += n

    outgoing = []
    for i, (k, e) in enumerate(steps):
        wait_all(incoming[i])
        whole = jnp.dot(turned[:COLS, :], tiles[i], preferred_element_type=F32)
        whole += jnp.dot(turned_other[:COLS, :], tiles_other[i], preferred_element_type=F32)
        buffer_a = first_a.at[e] if k == 0 else rest_a.at[2 * (k - 1) + e]
        buffer_b = keep_b.at[k] if e == 0 else give_b.at[k]
        put(buffer_a, packed(whole[:HALF]))
        put(buffer_b, packed(whole[HALF:]) + [gain[...]])
        to_a = own_a.at[e] if k == 0 else send_a.at[(z + k) & 3, e]
        to_b = (own_b, send_b)[e].at[k]
        outgoing.append(pltpu.make_async_copy(buffer_a, to_a, out_sems.at[0, i]))
        outgoing.append(pltpu.make_async_copy(buffer_b, to_b, out_sems.at[1, i]))
        start_all(outgoing[-2:])
    wait_all(outgoing)


def weight_step(hidden, other, grad, grad_other, earlier):
    return pl.pallas_call(
        weight_kernel,
        in_specs=[ANYWHERE] * 4 + [LATER],
        out_specs=[ANYWHERE] * 4,
        out_shape=[
            jax.ShapeDtypeStruct((2, ROWS_A, 128), F32),
            jax.ShapeDtypeStruct((4, 2, ROWS_A, 128), BF),
            jax.ShapeDtypeStruct((4, ROWS_B, 128), F32),
            jax.ShapeDtypeStruct((4, ROWS_B, 128), BF),
        ],
        scratch_shapes=[
            pltpu.VMEM((8, TOK, TILE), BF),
            pltpu.VMEM((8, TOK, TILE), BF),
            pltpu.VMEM((EXT, TOK), BF),
            pltpu.VMEM((EXT, TOK), BF),
            pltpu.VMEM((2, ROWS_A, 128), F32),
            pltpu.VMEM((6, ROWS_A, 128), BF),
            pltpu.VMEM((4, ROWS_B, 128), F32),
            pltpu.VMEM((4, ROWS_B, 128), BF),
            pltpu.VMEM((16, 128), F32),
            pltpu.SemaphoreType.DMA((2, 8)),
            pltpu.SemaphoreType.DMA((2, 8)),
            pltpu.SemaphoreType.DMA((2,)),
        ],
        compiler_params=params(60),
        cost_estimate=cost(0, 1_000),
        name="weight_grad",
    )(hidden, other, grad, grad_other, earlier)


def received_sum(ref, own, z):
    for other in range(4):
        own = own + jnp.where(z == other, 0.0, ref[other].astype(F32))
    return own


def whole(shape):
    return pl.BlockSpec(shape, lambda k: (0,) * len(shape))


FLAGGED = whole((8, 128))


def sum_a_kernel(own, r, *rest):
    keep, send, flag = rest[-3:]
    z, _, _ = place()
    total = received_sum(r.at[:, 0], own[0], z)

    @pl.when(pl.program_id(0) == 0)
    def _():
        keep[...] = total
        flag[...] = jnp.zeros_like(flag)

    @pl.when(pl.program_id(0) == 1)
    def _():
        send[...] = total.astype(BF)


def sum_a(own, r, *earlier):
    return pl.pallas_call(
        sum_a_kernel,
        grid=(2,),
        in_specs=[
            pl.BlockSpec((1, ROWS_A, 128), lambda e: (e, 0, 0)),
            pl.BlockSpec((4, 1, ROWS_A, 128), lambda e: (0, e, 0, 0)),
        ]
        + [LATER] * len(earlier),
        out_specs=[whole((ROWS_A, 128))] * 2 + [FLAGGED],
        out_shape=[
            jax.ShapeDtypeStruct((ROWS_A, 128), F32),
            jax.ShapeDtypeStruct((ROWS_A, 128), BF),
            FLAG,
        ],
        compiler_params=params(16),
        cost_estimate=cost(0, 3_500_000),
        name="sum_z",
    )(own, r, *earlier)


def sum_b_kernel(own, r, keep, send, flag):
    z, _, _ = place()
    k = pl.program_id(0)
    total = own[0] + r[0].astype(F32)
    send[(z + k) & 3] = total.astype(BF)

    @pl.when(k == 0)
    def _():
        keep[...] = total
        flag[...] = jnp.zeros_like(flag)


def sum_b(own, r):
    return pl.pallas_call(
        sum_b_kernel,
        grid=(4,),
        in_specs=[pl.BlockSpec((1, ROWS_B, 128), lambda k: (k, 0, 0))] * 2,
        out_specs=[whole((ROWS_B, 128)), whole((4, ROWS_B, 128)), FLAGGED],
        out_shape=[
            jax.ShapeDtypeStruct((ROWS_B, 128), F32),
            jax.ShapeDtypeStruct((4, ROWS_B, 128), BF),
            FLAG,
        ],
        compiler_params=params(16),
        cost_estimate=cost(0, 4_500_000),
        name="sum_y",
    )(own, r)


def sum_all_kernel(keep_a, ra, keep_b, rb, earlier, total, send, flag):
    z, _, _ = place()
    a = keep_a[...] + ra[...].astype(F32)
    b = received_sum(rb, keep_b[...], z)
    total[:ROWS_A, :] = a
    total[ROWS_A:, :] = b
    send[:ROWS_A, :] = a.astype(BF)
    send[ROWS_A:, :] = b.astype(BF)
    flag[...] = jnp.zeros_like(flag)


def sum_all(*parts):
    rows = ROWS_A + ROWS_B
    return pl.pallas_call(
        sum_all_kernel,
        grid=(1,),
        in_specs=[whole(part.shape) for part in parts[:-1]] + [LATER],
        out_specs=[whole((rows, 128)), whole((rows, 128)), FLAGGED],
        out_shape=[
            jax.ShapeDtypeStruct((rows, 128), F32),
            jax.ShapeDtypeStruct((rows, 128), BF),
            FLAG,
        ],
        compiler_params=params(16),
        cost_estimate=cost(0, 4_000_000),
        name="sum_shard",
    )(*parts)


def adamw(master, first, second, grad):
    new_first = beta_one * first + (1.0 - beta_one) * grad
    new_second = beta_two * second + (1.0 - beta_two) * grad * grad
    first_hat = new_first / (1.0 - beta_one**adam_count)
    second_hat = new_second / (1.0 - beta_two**adam_count)
    new_master = master - learn_rate * (
        first_hat / (jnp.sqrt(second_hat) + adam_eps) + decay_rate * master
    )
    return (new_master, new_first, new_second)


def adam_kernel(s, own, far, master, first, second, earlier, n_master, n_first, n_second, gain, grad):
    total = own[...] + far[...].astype(F32)
    core = s[0]
    gain[...] = total[2 * ROWS_A : 2 * ROWS_A + 8]

    def both(lo, n):
        return [total[h * ROWS_A + lo : h * ROWS_A + lo + n] for h in range(2)]

    for i in range(3):
        block = jnp.concatenate(both(i * HALF, HALF), axis=0)
        grad[pl.ds(pl.multiple_of(64 * core + 128 * i, 64), 128), :] = block.T
    edge = []
    for part in both(3 * HALF, HALF // 2):
        edge += [part, pltpu.roll(part, 64, 1)]
    block = jnp.concatenate(edge, axis=0)
    grad[pl.ds(pl.multiple_of(384 * (1 - core), 64), 64), :] = block.T[:64]
    n_master[...], n_first[...], n_second[...] = adamw(
        master[...], first[...], second[...], grad[...]
    )


def adam_step(s, own, far, master, first, second, earlier):
    shape = jax.ShapeDtypeStruct(master.shape, F32)
    spec = pl.BlockSpec(memory_space=pltpu.VMEM)
    return pl.pallas_call(
        adam_kernel,
        in_specs=[pl.BlockSpec(memory_space=pltpu.SMEM)]
        + [spec] * 5
        + [LATER],
        out_specs=[spec] * 4,
        out_shape=[shape] * 3 + [jax.ShapeDtypeStruct((8, 128), F32)],
        scratch_shapes=[pltpu.VMEM(master.shape, F32)],
        compiler_params=params(32),
        cost_estimate=cost(0, 9_000_000),
        name="adamw",
    )(s, own, far, master, first, second, earlier)


def input_step(grad, pieces, earlier, begun=None):
    places = [(n, i, dz, e) for n, piece in enumerate(pieces) for i, (dz, e) in enumerate(piece[2])]
    count, arrays = len(places), len(pieces)

    def kernel(grad, *rest):
        halves = rest[: 2 * arrays]
        out, flag, held, blocks, in_sems, out_sems = rest[-6:]
        z, y, core = place()
        incoming = []
        for at, (n, i, _, _) in enumerate(places):
            for half in range(2):
                slot = core ^ half
                rows = pl.ds(pl.multiple_of(slot * HALF, HALF), HALF)
                incoming.append(
                    pltpu.make_async_copy(
                        halves[2 * n + half].at[i], held.at[at, rows], in_sems.at[at, half]
                    )
                )
        start_all(incoming)
        flag[...] = jnp.zeros_like(flag)
        turned = grad[:COLS, :].astype(F32).T.astype(BF)
        outgoing = []
        for at, (_, _, dz, e) in enumerate(places):
            wait_all(incoming[2 * at : 2 * at + 2])
            blocks[at] = jnp.dot(turned, held[at], preferred_element_type=F32).astype(BF)
            block = 2 * ((z + dz) & 3) + (y ^ e)
            cols = pl.ds(pl.multiple_of(block * BLOCK, BLOCK), BLOCK)
            outgoing.append(
                pltpu.make_async_copy(blocks.at[at], out.at[:, cols], out_sems.at[at])
            )
            outgoing[-1].start()
        wait_all(outgoing)

    inside = pl.BlockSpec(memory_space=pltpu.VMEM)
    operands = [grad]
    for own, far, _ in pieces:
        operands += [own, far]
    halves = len(operands) - 1
    operands += earlier + ([] if begun is None else [begun])
    return pl.pallas_call(
        kernel,
        in_specs=[inside]
        + [ANYWHERE] * halves
        + [LATER] * len(earlier)
        + ([] if begun is None else [ANYWHERE]),
        out_specs=[ANYWHERE, inside],
        out_shape=[jax.ShapeDtypeStruct((TOK, WIDTH), BF), FLAG],
        scratch_shapes=[
            pltpu.VMEM((count, COLS, BLOCK), BF),
            pltpu.VMEM((count, TOK, BLOCK), BF),
            pltpu.SemaphoreType.DMA((count, 2)),
            pltpu.SemaphoreType.DMA((count,)),
        ],
        input_output_aliases={} if begun is None else {len(operands) - 1: 0},
        compiler_params=params(36),
        cost_estimate=cost(TOK * WIDTH * COLS, 8_000_000),
        name="input_grad",
    )(*operands)


def rope_step(rope_cot):
    half = ROPE // 2
    position = jnp.arange(TOK).astype(F32)
    freqs = 10000.0 ** (-2.0 * jnp.arange(half).astype(F32) / ROPE)
    angle = freqs[:, None] * position[None, :]
    cosine = jnp.cos(angle)
    sine = jnp.sin(angle)
    rope = rope_cot.T.astype(F32)
    first, second = rope[:half], rope[half:]
    return jnp.concatenate(
        [first * cosine + second * sine, second * cosine - first * sine], axis=0
    ).astype(BF)


def on_device(
    hidden_in,
    weight,
    gain,
    latent_cot,
    rope_cot,
    master_weight,
    first_moment,
    second_moment,
    gain_master,
    gain_first,
    gain_second,
):
    shard = lax.axis_index("dp")
    s = (shard & 1).astype(jnp.int32)[None]
    hidden = hidden_in[0]
    turned = weight[0].T
    other = moved(hidden, to_core)
    cuts = [cut_weight(turned, [(0, 0)])]
    cuts.append(cut_weight(turned, [(0, 1)], cuts[0]))
    cuts.append(cut_weight(turned, [(2, 0), (2, 1)], cuts[1]))
    here, beside, across = (moved(value, to_before_near) for value in cuts)
    rope = rope_step(rope_cot[0])
    grad = latent_step(hidden, turned, latent_cot[0], gain, rope, cuts[2])
    grad_other = moved(grad, to_core)
    grad_next = moved(grad, to_before)
    above, below = moved(here, to_z(-1)), moved(here, to_z(1))
    def both(value, *blocks):
        return value, moved(value, to_core), blocks

    pieces = (
        both(here, (0, 0)),
        both(across, (2, 0), (2, 1)),
        both(above, (1, 0)),
        both(below, (3, 0)),
        both(beside, (0, 1)),
    )
    own_a, send_a, own_b, send_b = weight_step(hidden, other, grad, grad_other, pieces[0][1])
    along_z = [[4 * z + k for z in range(4)] for k in range(4)]

    def exchanged(value):
        return lax.all_to_all(value, "dp", 0, 0, axis_index_groups=along_z, tiled=True)

    rb = moved(send_b, to_ylo)
    keep_a, send_a, is_a = sum_a(own_a, exchanged(send_a), *(piece[1] for piece in pieces))
    ra = moved(send_a, to_ylo)
    keep_b, send_b, is_b = sum_b(own_b, rb)
    received, is_begun = input_step(grad_next, pieces, [is_a, is_b])
    total, send, is_summed = sum_all(keep_a, ra, keep_b, exchanged(send_b), is_begun)
    far = moved(send, to_mirror)
    beside = after(beside, is_begun)
    above_2, below_2 = moved(beside, to_z(-1)), moved(beside, to_z(1))
    pieces = both(above_2, (1, 1)), both(below_2, (3, 1))
    received, is_received = input_step(grad_next, pieces, [is_summed], received)
    next_master, next_first, next_second, gain_rows = adam_step(
        s, total, far, master_weight[0], first_moment[0], second_moment[0], is_received
    )
    gain_total = lax.dynamic_slice(gain_rows[:4].reshape(LAT), (shard * 32,), (32,))
    next_gain = adamw(gain_master[0], gain_first[0], gain_second[0], gain_total)
    return (
        received[None],
        next_master[None],
        next_first[None],
        next_second[None],
        *(value[None] for value in next_gain),
    )


def solution(mesh):
    tokens, shared = P("pipe", "dp", None), P("pipe", None)
    split = P("pipe", "dp")
    return jax.shard_map(
        on_device,
        mesh=mesh,
        in_specs=(tokens, P("pipe", None, None), shared) + (tokens,) * 5 + (split,) * 3,
        out_specs=(tokens,) * 4 + (split,) * 3,
        check_vma=False,
    )
```

```python
import jax
import jax.numpy as jnp
from jax import lax
from jax.experimental import pallas as pl
from jax.experimental.pallas import tpu as pltpu
from jax.sharding import PartitionSpec as P

beta_one = 0.9
beta_two = 0.95
adam_count = 10
learn_rate = 0.00022
adam_eps = 1e-08
decay_rate = 0.1

RANKS, SHARDS = 8, 16
TOK, WIDTH, LAT, ROPE = 512, 7168, 512, 64
COLS = LAT + ROPE
BLOCK = WIDTH // 8
TILE = 512
HALF = COLS // 2
ROWS_A = 3 * HALF + HALF // 2
ROWS_B = ROWS_A + 16
EXT = COLS + 16
BF, F32 = jnp.bfloat16, jnp.float32
MIB = 1 << 20


def params(mib):
    return pltpu.CompilerParams(vmem_limit_bytes=mib * MIB)


def cost(flops, moved):
    return pl.CostEstimate(flops=flops, bytes_accessed=moved, transcendentals=0)


def moved(value, target):
    pairs = []
    for r in range(RANKS):
        for d in range(SHARDS):
            to = target(r, d)
            if 0 <= to[0] < RANKS:
                pairs.append((r * SHARDS + d, to[0] * SHARDS + to[1]))
    return lax.ppermute(value, ("pipe", "dp"), pairs)


def to_core(r, d):
    return r, d ^ 1


def to_ylo(r, d):
    return r, d ^ 2


def to_z(steps):
    return lambda r, d: (r, (d + 4 * steps) % SHARDS)


def to_mirror(r, d):
    return RANKS - 1 - r, d


def to_before(r, d):
    return r - 1, d


def to_before_near(r, d):
    return r - 1, d ^ 2


FLAG = jax.ShapeDtypeStruct((8, 128), F32)
ANYWHERE = pl.BlockSpec(memory_space=pltpu.HBM)
LATER = pl.BlockSpec(memory_space=pl.ANY)


def place():
    shard = lax.axis_index("dp")
    return shard >> 2, (shard >> 1) & 1, shard & 1


def columns(block, core):
    return pl.ds(pl.multiple_of(block * BLOCK + 384 * core, 128), TILE)


def start_all(copies):
    for copy in copies:
        copy.start()


def wait_all(copies):
    for copy in copies:
        copy.wait()


def after(value, *earlier):
    def kernel(*refs):
        pass

    return pl.pallas_call(
        kernel,
        in_specs=[ANYWHERE] + [LATER] * len(earlier),
        out_specs=ANYWHERE,
        out_shape=jax.ShapeDtypeStruct(value.shape, value.dtype),
        input_output_aliases={0: 0},
        compiler_params=params(1),
        cost_estimate=cost(0, 0),
        name="after",
    )(value, *earlier)


def cut_weight(weight, blocks, *earlier):
    def kernel(weight, *rest):
        out, sems = rest[-2:]
        z, y, core = place()
        rows = pl.ds(pl.multiple_of(core * HALF, HALF), HALF)
        copies = []
        for i, (dz, e) in enumerate(blocks):
            block = 2 * ((z + dz) & 3) + ((1 - y) ^ e)
            cols = pl.ds(pl.multiple_of(block * BLOCK, BLOCK), BLOCK)
            copies.append(pltpu.make_async_copy(weight.at[rows, cols], out.at[i], sems.at[i]))
        start_all(copies)
        wait_all(copies)

    count = len(blocks)
    return pl.pallas_call(
        kernel,
        in_specs=[ANYWHERE] + [LATER] * len(earlier),
        out_shape=jax.ShapeDtypeStruct((count, HALF, BLOCK), BF),
        scratch_shapes=[pltpu.SemaphoreType.DMA((count,))],
        compiler_params=params(60),
        cost_estimate=cost(0, 1_000),
        name="cut_weight",
    )(weight, *earlier)


PARTS = 7
PART = WIDTH // PARTS


def latent_kernel(hidden, weight, cot, gain, rope, earlier, out, tokens, matrix, sems):
    copies = []
    for i in range(PARTS):
        cols = pl.ds(i * PART, PART)
        copies.append(
            (
                pltpu.make_async_copy(hidden.at[:, cols], tokens.at[:, cols], sems.at[0, i]),
                pltpu.make_async_copy(
                    weight.at[pl.ds(0, LAT), cols], matrix.at[:, cols], sems.at[1, i]
                ),
            )
        )
    for pair in copies:
        start_all(pair)
    latent = jnp.zeros((TOK, LAT), F32)
    for i in range(PARTS):
        wait_all(copies[i])
        cols = slice(i * PART, i * PART + PART)
        latent += lax.dot_general(
            tokens[:, cols],
            matrix[:, cols],
            (((1,), (1,)), ((), ())),
            preferred_element_type=F32,
        )
    inv = lax.rsqrt(jnp.mean(latent * latent, axis=-1, keepdims=True) + 1e-06)
    normed = latent * inv
    c = cot[...].astype(F32)
    scaled = c * gain[...]
    grad = inv * (scaled - normed * jnp.mean(scaled * normed, axis=-1, keepdims=True))
    gain_part = jnp.sum(c * normed, axis=0, keepdims=True)
    out[0:LAT, :] = grad.T.astype(BF)
    out[LAT:COLS, :] = rope[...]
    high = gain_part.astype(BF)
    low = (gain_part - high.astype(F32)).astype(BF)
    row = lax.broadcasted_iota(jnp.int32, (16, LAT), 0)
    high = jnp.broadcast_to(high.astype(F32), (16, LAT))
    low = jnp.broadcast_to(low.astype(F32), (16, LAT))
    both = jnp.where(row == 0, high, jnp.where(row == 1, low, 0.0))
    out[COLS:EXT, :] = both.astype(BF)


def latent_step(hidden, weight, cot, gain, rope, earlier):
    inside = pl.BlockSpec(memory_space=pltpu.VMEM)
    return pl.pallas_call(
        latent_kernel,
        in_specs=[ANYWHERE, ANYWHERE, inside, inside, inside, LATER],
        out_shape=jax.ShapeDtypeStruct((EXT, TOK), BF),
        scratch_shapes=[
            pltpu.VMEM((TOK, WIDTH), BF),
            pltpu.VMEM((LAT, WIDTH), BF),
            pltpu.SemaphoreType.DMA((2, PARTS)),
        ],
        compiler_params=params(60),
        cost_estimate=cost(0, 1_000),
        name="latent_grad",
    )(hidden, weight, cot, gain, rope, earlier)


def weight_kernel(
    hidden,
    other,
    grad,
    grad_other,
    earlier,
    own_a,
    send_a,
    own_b,
    send_b,
    tiles,
    turned,
    first_a,
    rest_a,
    keep_b,
    give_b,
    gain,
    in_sems,
    out_sems,
    grad_sems,
):
    z, y, core = place()
    steps = [(k, e) for k in (1, 2, 3, 0) for e in (1, 0)]
    incoming = []
    for i, (k, e) in enumerate(steps):
        cols = columns(2 * ((z + k) & 3) + (y ^ e), core)
        incoming.append(
            (
                pltpu.make_async_copy(
                    hidden.at[:, cols], tiles.at[i, pl.ds(0, TOK)], in_sems.at[0, i]
                ),
                pltpu.make_async_copy(
                    other.at[:, cols], tiles.at[i, pl.ds(TOK, TOK)], in_sems.at[1, i]
                ),
            )
        )
    grads = [
        pltpu.make_async_copy(grad, turned.at[:, pl.ds(0, TOK)], grad_sems.at[0]),
        pltpu.make_async_copy(grad_other, turned.at[:, pl.ds(TOK, TOK)], grad_sems.at[1]),
    ]
    start_all(grads)
    for pair in incoming:
        start_all(pair)
    wait_all(grads)

    sums = jnp.zeros((1, LAT), F32)
    for at in (0, TOK):
        pair = turned[COLS:EXT, at : at + TOK].astype(F32)
        sums = sums + pair[0:1] + pair[1:2]
    gain[...] = jnp.zeros_like(gain)
    for i in range(4):
        gain[i : i + 1, :] = sums[:, 128 * i : 128 * i + 128]

    lane = lax.broadcasted_iota(jnp.int32, (HALF // 2, 128), 1)
    first = core == 0

    def packed(full):
        col = [full[:, 128 * j : 128 * j + 128] for j in range(4)]
        edge = jnp.where(first, col[3], col[0])
        top, low = edge[: HALF // 2], edge[HALF // 2 :]
        left = jnp.where(first, top, pltpu.roll(top, 64, 1))
        right = jnp.where(first, pltpu.roll(low, 64, 1), low)
        return [jnp.where(first, col[i], col[i + 1]) for i in range(3)] + [
            jnp.where(lane < 64, left, right)
        ]

    def put(ref, parts):
        at = 0
        for part in parts:
            n = part.shape[0]
            ref[at : at + n, :] = part.astype(ref.dtype)
            at += n

    outgoing = []
    for i, (k, e) in enumerate(steps):
        wait_all(incoming[i])
        whole = jnp.dot(turned[:COLS, :], tiles[i], preferred_element_type=F32)
        buffer_a = first_a.at[e] if k == 0 else rest_a.at[2 * (k - 1) + e]
        buffer_b = keep_b.at[k] if e == 0 else give_b.at[k]
        put(buffer_a, packed(whole[:HALF]))
        put(buffer_b, packed(whole[HALF:]) + [gain[...]])
        to_a = own_a.at[e] if k == 0 else send_a.at[(z + k) & 3, e]
        to_b = (own_b, send_b)[e].at[(z + k) & 3]
        outgoing.append(pltpu.make_async_copy(buffer_a, to_a, out_sems.at[0, i]))
        outgoing.append(pltpu.make_async_copy(buffer_b, to_b, out_sems.at[1, i]))
        start_all(outgoing[-2:])
    wait_all(outgoing)


def weight_step(hidden, other, grad, grad_other, earlier):
    return pl.pallas_call(
        weight_kernel,
        in_specs=[ANYWHERE] * 4 + [LATER],
        out_specs=[ANYWHERE] * 4,
        out_shape=[
            jax.ShapeDtypeStruct((2, ROWS_A, 128), F32),
            jax.ShapeDtypeStruct((4, 2, ROWS_A, 128), BF),
            jax.ShapeDtypeStruct((4, ROWS_B, 128), F32),
            jax.ShapeDtypeStruct((4, ROWS_B, 128), BF),
        ],
        scratch_shapes=[
            pltpu.VMEM((8, 2 * TOK, TILE), BF),
            pltpu.VMEM((EXT, 2 * TOK), BF),
            pltpu.VMEM((2, ROWS_A, 128), F32),
            pltpu.VMEM((6, ROWS_A, 128), BF),
            pltpu.VMEM((4, ROWS_B, 128), F32),
            pltpu.VMEM((4, ROWS_B, 128), BF),
            pltpu.VMEM((16, 128), F32),
            pltpu.SemaphoreType.DMA((2, 8)),
            pltpu.SemaphoreType.DMA((2, 8)),
            pltpu.SemaphoreType.DMA((2,)),
        ],
        compiler_params=params(60),
        cost_estimate=cost(0, 1_000),
        name="weight_grad",
    )(hidden, other, grad, grad_other, earlier)


def received_sum(own, parts, z):
    for other in range(4):
        own = own + jnp.where(z == other, 0.0, parts[other].astype(F32))
    return own


def adamw(master, first, second, grad):
    new_first = beta_one * first + (1.0 - beta_one) * grad
    new_second = beta_two * second + (1.0 - beta_two) * grad * grad
    first_hat = new_first / (1.0 - beta_one**adam_count)
    second_hat = new_second / (1.0 - beta_two**adam_count)
    new_master = master - learn_rate * (
        first_hat / (jnp.sqrt(second_hat) + adam_eps) + decay_rate * master
    )
    return (new_master, new_first, new_second)


def adam_kernel(s, own_a, own_b, far, master, first, second, n_master, n_first, n_second, gain, grad):
    total_a = own_a[...] + far[:ROWS_A, :].astype(F32)
    total_b = own_b[...] + far[ROWS_A:, :].astype(F32)
    core = s[0]
    gain[...] = total_b[ROWS_A : ROWS_A + 8]

    def both(lo, n):
        return [total[lo : lo + n] for total in (total_a, total_b)]

    for i in range(3):
        block = jnp.concatenate(both(i * HALF, HALF), axis=0)
        grad[pl.ds(pl.multiple_of(64 * core + 128 * i, 64), 128), :] = block.T
    edge = []
    for part in both(3 * HALF, HALF // 2):
        edge += [part, pltpu.roll(part, 64, 1)]
    block = jnp.concatenate(edge, axis=0)
    grad[pl.ds(pl.multiple_of(384 * (1 - core), 64), 64), :] = block.T[:64]
    n_master[...], n_first[...], n_second[...] = adamw(
        master[...], first[...], second[...], grad[...]
    )


def adam_step(s, own_a, own_b, far, master, first, second):
    shape = jax.ShapeDtypeStruct(master.shape, F32)
    spec = pl.BlockSpec(memory_space=pltpu.VMEM)
    return pl.pallas_call(
        adam_kernel,
        in_specs=[pl.BlockSpec(memory_space=pltpu.SMEM)] + [spec] * 6,
        out_specs=[spec] * 4,
        out_shape=[shape] * 3 + [jax.ShapeDtypeStruct((8, 128), F32)],
        scratch_shapes=[pltpu.VMEM(master.shape, F32)],
        compiler_params=params(32),
        cost_estimate=cost(0, 9_000_000),
        name="adamw",
    )(s, own_a, own_b, far, master, first, second)


def input_step(grad, pieces, earlier, begun=None):
    places = [(n, i, dz, e) for n, piece in enumerate(pieces) for i, (dz, e) in enumerate(piece[2])]
    count, arrays = len(places), len(pieces)

    def kernel(grad, *rest):
        halves = rest[: 2 * arrays]
        out, flag, held, blocks, in_sems, out_sems = rest[-6:]
        z, y, core = place()
        incoming = []
        for at, (n, i, _, _) in enumerate(places):
            for half in range(2):
                slot = core ^ half
                rows = pl.ds(pl.multiple_of(slot * HALF, HALF), HALF)
                incoming.append(
                    pltpu.make_async_copy(
                        halves[2 * n + half].at[i], held.at[at, rows], in_sems.at[at, half]
                    )
                )
        start_all(incoming)
        flag[...] = jnp.zeros_like(flag)
        turned = grad[:COLS, :].astype(F32).T.astype(BF)
        outgoing = []
        for at, (_, _, dz, e) in enumerate(places):
            wait_all(incoming[2 * at : 2 * at + 2])
            blocks[at] = jnp.dot(turned, held[at], preferred_element_type=F32).astype(BF)
            block = 2 * ((z + dz) & 3) + (y ^ e)
            cols = pl.ds(pl.multiple_of(block * BLOCK, BLOCK), BLOCK)
            outgoing.append(
                pltpu.make_async_copy(blocks.at[at], out.at[:, cols], out_sems.at[at])
            )
            outgoing[-1].start()
        wait_all(outgoing)

    inside = pl.BlockSpec(memory_space=pltpu.VMEM)
    operands = [grad]
    for own, far, _ in pieces:
        operands += [own, far]
    halves = len(operands) - 1
    operands += earlier + ([] if begun is None else [begun])
    return pl.pallas_call(
        kernel,
        in_specs=[inside]
        + [ANYWHERE] * halves
        + [LATER] * len(earlier)
        + ([] if begun is None else [ANYWHERE]),
        out_specs=[ANYWHERE, inside],
        out_shape=[jax.ShapeDtypeStruct((TOK, WIDTH), BF), FLAG],
        scratch_shapes=[
            pltpu.VMEM((count, COLS, BLOCK), BF),
            pltpu.VMEM((count, TOK, BLOCK), BF),
            pltpu.SemaphoreType.DMA((count, 2)),
            pltpu.SemaphoreType.DMA((count,)),
        ],
        input_output_aliases={} if begun is None else {len(operands) - 1: 0},
        compiler_params=params(36),
        cost_estimate=cost(TOK * WIDTH * COLS, 8_000_000),
        name="input_grad",
    )(*operands)


def rope_step(rope_cot):
    half = ROPE // 2
    position = jnp.arange(TOK).astype(F32)
    freqs = 10000.0 ** (-2.0 * jnp.arange(half).astype(F32) / ROPE)
    angle = freqs[:, None] * position[None, :]
    cosine = jnp.cos(angle)
    sine = jnp.sin(angle)
    rope = rope_cot.T.astype(F32)
    first, second = rope[:half], rope[half:]
    return jnp.concatenate(
        [first * cosine + second * sine, second * cosine - first * sine], axis=0
    ).astype(BF)


def on_device(
    hidden_in,
    weight,
    gain,
    latent_cot,
    rope_cot,
    master_weight,
    first_moment,
    second_moment,
    gain_master,
    gain_first,
    gain_second,
):
    shard = lax.axis_index("dp")
    s = (shard & 1).astype(jnp.int32)[None]
    hidden = hidden_in[0]
    turned = weight[0].T
    other = moved(hidden, to_core)
    cut_here = cut_weight(turned, [(0, 0)])
    here = moved(cut_here, to_before_near)
    rope = rope_step(rope_cot[0])
    grad = latent_step(hidden, turned, latent_cot[0], gain, rope, cut_here)
    cut_1 = cut_weight(turned, [(0, 1), (2, 0)], grad)
    cut_2 = cut_weight(turned, [(2, 1), (1, 1)], cut_1)
    grad_other = moved(grad, to_core)
    grad_next = moved(grad, to_before)
    rest_1 = moved(cut_1, to_before_near)
    rest_2 = moved(cut_2, to_before_near)
    above, below = moved(here, to_z(-1)), moved(here, to_z(1))
    side = moved(below, to_ylo)
    pieces = [
        (value, moved(value, to_core), blocks)
        for value, blocks in (
            (here, [(0, 0)]),
            (above, [(1, 0)]),
            (below, [(3, 0)]),
            (rest_1, [(0, 1), (2, 0)]),
            (side, [(3, 1)]),
            (rest_2, [(2, 1), (1, 1)]),
        )
    ]
    far_here, far_above, far_below, far_1, far_side, far_2 = (piece[1] for piece in pieces)

    own_a, send_a, own_b, send_b = weight_step(hidden, other, grad, grad_other, cut_2)
    z = shard >> 2
    along_z = [[4 * z + k for z in range(4)] for k in range(4)]

    def exchanged(value):
        return lax.all_to_all(value, "dp", 0, 0, axis_index_groups=along_z, tiled=True)

    ra = exchanged(send_a)
    rb = moved(after(send_b, above, below), to_ylo)
    rb = after(rb, grad_next, far_here, far_above, far_below)
    send_b = (own_b + rb.astype(F32)).astype(BF)
    rz = exchanged(send_b)
    ra = after(ra, far_1)
    send_a = received_sum(own_a[1], ra[:, 1], z).astype(BF)
    ry = moved(send_a, to_ylo)
    total_a = received_sum(own_a[0], ra[:, 0], z) + ry.astype(F32)
    keep_b = lax.dynamic_index_in_dim(own_b, z, 0, False)
    keep_b += lax.dynamic_index_in_dim(rb, z, 0, False).astype(F32)
    total_b = received_sum(keep_b, after(rz, far_side), z)
    send = jnp.concatenate([total_a, total_b], axis=0).astype(BF)
    far = moved(send, to_mirror)
    received, _ = input_step(grad_next, pieces, [send])
    next_master, next_first, next_second, gain_rows = adam_step(
        s, total_a, total_b, far, master_weight[0], first_moment[0], second_moment[0]
    )
    gain_total = lax.dynamic_slice(gain_rows[:4].reshape(LAT), (shard * 32,), (32,))
    next_gain = adamw(gain_master[0], gain_first[0], gain_second[0], gain_total)
    return (
        received[None],
        next_master[None],
        next_first[None],
        next_second[None],
        *(value[None] for value in next_gain),
    )


def solution(mesh):
    tokens, shared = P("pipe", "dp", None), P("pipe", None)
    split = P("pipe", "dp")
    return jax.shard_map(
        on_device,
        mesh=mesh,
        in_specs=(tokens, P("pipe", None, None), shared) + (tokens,) * 5 + (split,) * 3,
        out_specs=(tokens,) * 4 + (split,) * 3,
        check_vma=False,
    )
```

```python
import jax
import jax.numpy as jnp
from jax import lax
from jax.experimental import pallas as pl
from jax.experimental.pallas import tpu as pltpu
from jax.sharding import PartitionSpec as P

beta_one = 0.9
beta_two = 0.95
adam_count = 10
learn_rate = 0.00022
adam_eps = 1e-08
decay_rate = 0.1

RANKS, SHARDS = 8, 16
TOK, WIDTH, LAT, ROPE = 512, 7168, 512, 64
COLS = LAT + ROPE
BLOCK = WIDTH // 8
TILE = 512
HALF = COLS // 2
ROWS_A = 3 * HALF + HALF // 2
ROWS_B = ROWS_A + 16
EXT = COLS + 16
BF, F32 = jnp.bfloat16, jnp.float32
MIB = 1 << 20


def params(mib):
    return pltpu.CompilerParams(vmem_limit_bytes=mib * MIB)


def cost(flops, moved):
    return pl.CostEstimate(flops=flops, bytes_accessed=moved, transcendentals=0)


def moved(value, target):
    pairs = []
    for r in range(RANKS):
        for d in range(SHARDS):
            to = target(r, d)
            if 0 <= to[0] < RANKS:
                pairs.append((r * SHARDS + d, to[0] * SHARDS + to[1]))
    return lax.ppermute(value, ("pipe", "dp"), pairs)


def to_core(r, d):
    return r, d ^ 1


def to_ylo(r, d):
    return r, d ^ 2


def to_z(steps):
    return lambda r, d: (r, (d + 4 * steps) % SHARDS)


def to_mirror(r, d):
    return RANKS - 1 - r, d


def to_before(r, d):
    return r - 1, d


def to_before_near(r, d):
    return r - 1, d ^ 2


FLAG = jax.ShapeDtypeStruct((8, 128), F32)
ANYWHERE = pl.BlockSpec(memory_space=pltpu.HBM)
LATER = pl.BlockSpec(memory_space=pl.ANY)


def place():
    shard = lax.axis_index("dp")
    return shard >> 2, (shard >> 1) & 1, shard & 1


def columns(block, core):
    return pl.ds(pl.multiple_of(block * BLOCK + 384 * core, 128), TILE)


def start_all(copies):
    for copy in copies:
        copy.start()


def wait_all(copies):
    for copy in copies:
        copy.wait()


def after(value, *earlier, mib=1):
    def kernel(*refs):
        pass

    return pl.pallas_call(
        kernel,
        in_specs=[ANYWHERE] + [LATER] * len(earlier),
        out_specs=ANYWHERE,
        out_shape=jax.ShapeDtypeStruct(value.shape, value.dtype),
        input_output_aliases={0: 0},
        compiler_params=params(mib),
        cost_estimate=cost(0, 0),
        name="after",
    )(value, *earlier)


def cut_weight(weight, groups):
    def kernel(weight, *rest):
        outs, sems = rest[:-1], rest[-1]
        z, y, core = place()
        rows = pl.ds(pl.multiple_of(core * HALF, HALF), HALF)
        copies = []
        for out, group in zip(outs, groups):
            for i, (dz, e) in enumerate(group):
                block = 2 * ((z + dz) & 3) + ((1 - y) ^ e)
                cols = pl.ds(pl.multiple_of(block * BLOCK, BLOCK), BLOCK)
                sem = sems.at[len(copies)]
                copies.append(pltpu.make_async_copy(weight.at[rows, cols], out.at[i], sem))
        start_all(copies)
        wait_all(copies)

    return pl.pallas_call(
        kernel,
        in_specs=[ANYWHERE],
        out_shape=[jax.ShapeDtypeStruct((len(group), HALF, BLOCK), BF) for group in groups],
        scratch_shapes=[pltpu.SemaphoreType.DMA((sum(len(group) for group in groups),))],
        compiler_params=params(60),
        cost_estimate=cost(0, 1_000),
        name="cut_weight",
    )(weight)


PARTS = 7
PART = WIDTH // PARTS


def latent_kernel(hidden, weight, cot, gain, rope, earlier, out, tokens, matrix, sems):
    copies = []
    for i in range(PARTS):
        cols = pl.ds(i * PART, PART)
        copies.append(
            (
                pltpu.make_async_copy(hidden.at[:, cols], tokens.at[:, cols], sems.at[0, i]),
                pltpu.make_async_copy(
                    weight.at[pl.ds(0, LAT), cols], matrix.at[:, cols], sems.at[1, i]
                ),
            )
        )
    for pair in copies:
        start_all(pair)
    latent = jnp.zeros((TOK, LAT), F32)
    for i in range(PARTS):
        wait_all(copies[i])
        cols = slice(i * PART, i * PART + PART)
        latent += lax.dot_general(
            tokens[:, cols],
            matrix[:, cols],
            (((1,), (1,)), ((), ())),
            preferred_element_type=F32,
        )
    inv = lax.rsqrt(jnp.mean(latent * latent, axis=-1, keepdims=True) + 1e-06)
    normed = latent * inv
    c = cot[...].astype(F32)
    scaled = c * gain[...]
    grad = inv * (scaled - normed * jnp.mean(scaled * normed, axis=-1, keepdims=True))
    gain_part = jnp.sum(c * normed, axis=0, keepdims=True)
    out[0:LAT, :] = grad.T.astype(BF)
    out[LAT:COLS, :] = rope[...]
    high = gain_part.astype(BF)
    low = (gain_part - high.astype(F32)).astype(BF)
    row = lax.broadcasted_iota(jnp.int32, (16, LAT), 0)
    high = jnp.broadcast_to(high.astype(F32), (16, LAT))
    low = jnp.broadcast_to(low.astype(F32), (16, LAT))
    both = jnp.where(row == 0, high, jnp.where(row == 1, low, 0.0))
    out[COLS:EXT, :] = both.astype(BF)


def latent_step(hidden, weight, cot, gain, rope, earlier):
    inside = pl.BlockSpec(memory_space=pltpu.VMEM)
    return pl.pallas_call(
        latent_kernel,
        in_specs=[ANYWHERE, ANYWHERE, inside, inside, inside, LATER],
        out_shape=jax.ShapeDtypeStruct((EXT, TOK), BF),
        scratch_shapes=[
            pltpu.VMEM((TOK, WIDTH), BF),
            pltpu.VMEM((LAT, WIDTH), BF),
            pltpu.SemaphoreType.DMA((2, PARTS)),
        ],
        compiler_params=params(60),
        cost_estimate=cost(0, 1_000),
        name="latent_grad",
    )(hidden, weight, cot, gain, rope, earlier)


def weight_kernel(
    hidden,
    other,
    grad,
    grad_other,
    own_a,
    send_a,
    own_b,
    send_b,
    tiles,
    turned,
    first_a,
    rest_a,
    keep_b,
    give_b,
    gain,
    in_sems,
    out_sems,
    grad_sems,
):
    z, y, core = place()
    steps = [(k, e) for k in (1, 2, 3, 0) for e in (1, 0)]
    incoming = []
    for i, (k, e) in enumerate(steps):
        cols = columns(2 * ((z + k) & 3) + (y ^ e), core)
        incoming.append(
            (
                pltpu.make_async_copy(
                    hidden.at[:, cols], tiles.at[i, pl.ds(0, TOK)], in_sems.at[0, i]
                ),
                pltpu.make_async_copy(
                    other.at[:, cols], tiles.at[i, pl.ds(TOK, TOK)], in_sems.at[1, i]
                ),
            )
        )
    grads = [
        pltpu.make_async_copy(grad, turned.at[:, pl.ds(0, TOK)], grad_sems.at[0]),
        pltpu.make_async_copy(grad_other, turned.at[:, pl.ds(TOK, TOK)], grad_sems.at[1]),
    ]
    start_all(grads)
    for pair in incoming[:2]:
        start_all(pair)
    wait_all(grads)

    sums = jnp.zeros((1, LAT), F32)
    for at in (0, TOK):
        pair = turned[COLS:EXT, at : at + TOK].astype(F32)
        sums = sums + pair[0:1] + pair[1:2]
    gain[...] = jnp.zeros_like(gain)
    for i in range(4):
        gain[i : i + 1, :] = sums[:, 128 * i : 128 * i + 128]

    lane = lax.broadcasted_iota(jnp.int32, (HALF // 2, 128), 1)
    first = core == 0

    def packed(full):
        col = [full[:, 128 * j : 128 * j + 128] for j in range(4)]
        edge = jnp.where(first, col[3], col[0])
        top, low = edge[: HALF // 2], edge[HALF // 2 :]
        left = jnp.where(first, top, pltpu.roll(top, 64, 1))
        right = jnp.where(first, pltpu.roll(low, 64, 1), low)
        return [jnp.where(first, col[i], col[i + 1]) for i in range(3)] + [
            jnp.where(lane < 64, left, right)
        ]

    def put(ref, parts):
        at = 0
        for part in parts:
            n = part.shape[0]
            ref[at : at + n, :] = part.astype(ref.dtype)
            at += n

    outgoing = []
    for i, (k, e) in enumerate(steps):
        wait_all(incoming[i])
        if i + 2 < len(steps):
            start_all(incoming[i + 2])
        whole = jnp.dot(turned[:COLS, :], tiles[i], preferred_element_type=F32)
        buffer_a = first_a.at[e] if k == 0 else rest_a.at[2 * (k - 1) + e]
        buffer_b = keep_b.at[k] if e == 0 else give_b.at[k]
        put(buffer_a, packed(whole[:HALF]))
        put(buffer_b, packed(whole[HALF:]) + [gain[...]])
        to_a = own_a.at[e] if k == 0 else send_a.at[(z + k) & 3, e]
        to_b = (own_b, send_b)[e].at[(z + k) & 3]
        outgoing.append(pltpu.make_async_copy(buffer_a, to_a, out_sems.at[0, i]))
        outgoing.append(pltpu.make_async_copy(buffer_b, to_b, out_sems.at[1, i]))
        start_all(outgoing[-2:])
    wait_all(outgoing)


def weight_step(hidden, other, grad, grad_other):
    return pl.pallas_call(
        weight_kernel,
        in_specs=[ANYWHERE] * 4,
        out_specs=[ANYWHERE] * 4,
        out_shape=[
            jax.ShapeDtypeStruct((2, ROWS_A, 128), F32),
            jax.ShapeDtypeStruct((4, 2, ROWS_A, 128), BF),
            jax.ShapeDtypeStruct((4, ROWS_B, 128), F32),
            jax.ShapeDtypeStruct((4, ROWS_B, 128), BF),
        ],
        scratch_shapes=[
            pltpu.VMEM((8, 2 * TOK, TILE), BF),
            pltpu.VMEM((EXT, 2 * TOK), BF),
            pltpu.VMEM((2, ROWS_A, 128), F32),
            pltpu.VMEM((6, ROWS_A, 128), BF),
            pltpu.VMEM((4, ROWS_B, 128), F32),
            pltpu.VMEM((4, ROWS_B, 128), BF),
            pltpu.VMEM((16, 128), F32),
            pltpu.SemaphoreType.DMA((2, 8)),
            pltpu.SemaphoreType.DMA((2, 8)),
            pltpu.SemaphoreType.DMA((2,)),
        ],
        compiler_params=params(60),
        cost_estimate=cost(0, 1_000),
        name="weight_grad",
    )(hidden, other, grad, grad_other)


def received_sum(own, parts, z):
    for other in range(4):
        own = own + jnp.where(z == other, 0.0, parts[other].astype(F32))
    return own


def adamw(master, first, second, grad):
    new_first = beta_one * first + (1.0 - beta_one) * grad
    new_second = beta_two * second + (1.0 - beta_two) * grad * grad
    first_hat = new_first / (1.0 - beta_one**adam_count)
    second_hat = new_second / (1.0 - beta_two**adam_count)
    new_master = master - learn_rate * (
        first_hat / (jnp.sqrt(second_hat) + adam_eps) + decay_rate * master
    )
    return (new_master, new_first, new_second)


def adam_kernel(s, own_a, own_b, far, master, first, second, n_master, n_first, n_second, gain, grad):
    total_a = own_a[...] + far[:ROWS_A, :].astype(F32)
    total_b = own_b[...] + far[ROWS_A:, :].astype(F32)
    core = s[0]
    gain[...] = total_b[ROWS_A : ROWS_A + 8]

    def both(lo, n):
        return [total[lo : lo + n] for total in (total_a, total_b)]

    for i in range(3):
        block = jnp.concatenate(both(i * HALF, HALF), axis=0)
        grad[pl.ds(pl.multiple_of(64 * core + 128 * i, 64), 128), :] = block.T
    edge = []
    for part in both(3 * HALF, HALF // 2):
        edge += [part, pltpu.roll(part, 64, 1)]
    block = jnp.concatenate(edge, axis=0)
    grad[pl.ds(pl.multiple_of(384 * (1 - core), 64), 64), :] = block.T[:64]
    n_master[...], n_first[...], n_second[...] = adamw(
        master[...], first[...], second[...], grad[...]
    )


def adam_step(s, own_a, own_b, far, master, first, second):
    shape = jax.ShapeDtypeStruct(master.shape, F32)
    spec = pl.BlockSpec(memory_space=pltpu.VMEM)
    return pl.pallas_call(
        adam_kernel,
        in_specs=[pl.BlockSpec(memory_space=pltpu.SMEM)] + [spec] * 6,
        out_specs=[spec] * 4,
        out_shape=[shape] * 3 + [jax.ShapeDtypeStruct((8, 128), F32)],
        scratch_shapes=[pltpu.VMEM(master.shape, F32)],
        compiler_params=params(32),
        cost_estimate=cost(0, 9_000_000),
        name="adamw",
    )(s, own_a, own_b, far, master, first, second)


def input_step(grad, pieces, earlier, begun=None):
    places = [(n, i, dz, e) for n, piece in enumerate(pieces) for i, (dz, e) in enumerate(piece[2])]
    count, arrays = len(places), len(pieces)

    def kernel(grad, *rest):
        halves = rest[: 2 * arrays]
        out, flag, held, blocks, in_sems, out_sems = rest[-6:]
        z, y, core = place()
        incoming = []
        for at, (n, i, _, _) in enumerate(places):
            for half in range(2):
                slot = core ^ half
                rows = pl.ds(pl.multiple_of(slot * HALF, HALF), HALF)
                incoming.append(
                    pltpu.make_async_copy(
                        halves[2 * n + half].at[i], held.at[at, rows], in_sems.at[at, half]
                    )
                )
        start_all(incoming)
        flag[...] = jnp.zeros_like(flag)
        turned = grad[:COLS, :].astype(F32).T.astype(BF)
        outgoing = []
        for at, (_, _, dz, e) in enumerate(places):
            wait_all(incoming[2 * at : 2 * at + 2])
            blocks[at] = jnp.dot(turned, held[at], preferred_element_type=F32).astype(BF)
            block = 2 * ((z + dz) & 3) + (y ^ e)
            cols = pl.ds(pl.multiple_of(block * BLOCK, BLOCK), BLOCK)
            outgoing.append(
                pltpu.make_async_copy(blocks.at[at], out.at[:, cols], out_sems.at[at])
            )
            outgoing[-1].start()
        wait_all(outgoing)

    inside = pl.BlockSpec(memory_space=pltpu.VMEM)
    operands = [grad]
    for own, far, _ in pieces:
        operands += [own, far]
    halves = len(operands) - 1
    operands += earlier + ([] if begun is None else [begun])
    return pl.pallas_call(
        kernel,
        in_specs=[inside]
        + [ANYWHERE] * halves
        + [LATER] * len(earlier)
        + ([] if begun is None else [ANYWHERE]),
        out_specs=[ANYWHERE, inside],
        out_shape=[jax.ShapeDtypeStruct((TOK, WIDTH), BF), FLAG],
        scratch_shapes=[
            pltpu.VMEM((count, COLS, BLOCK), BF),
            pltpu.VMEM((count, TOK, BLOCK), BF),
            pltpu.SemaphoreType.DMA((count, 2)),
            pltpu.SemaphoreType.DMA((count,)),
        ],
        input_output_aliases={} if begun is None else {len(operands) - 1: 0},
        compiler_params=params(60),
        cost_estimate=cost(TOK * WIDTH * COLS, 8_000_000),
        name="input_grad",
    )(*operands)


def rope_step(rope_cot):
    half = ROPE // 2
    position = jnp.arange(TOK).astype(F32)
    freqs = 10000.0 ** (-2.0 * jnp.arange(half).astype(F32) / ROPE)
    angle = freqs[:, None] * position[None, :]
    cosine = jnp.cos(angle)
    sine = jnp.sin(angle)
    rope = rope_cot.T.astype(F32)
    first, second = rope[:half], rope[half:]
    return jnp.concatenate(
        [first * cosine + second * sine, second * cosine - first * sine], axis=0
    ).astype(BF)


def on_device(
    hidden_in,
    weight,
    gain,
    latent_cot,
    rope_cot,
    master_weight,
    first_moment,
    second_moment,
    gain_master,
    gain_first,
    gain_second,
):
    shard = lax.axis_index("dp")
    s = (shard & 1).astype(jnp.int32)[None]
    hidden = hidden_in[0]
    turned = weight[0].T
    other = moved(hidden, to_core)
    groups = [[(0, 0)], [(0, 1), (2, 0)], [(2, 1), (1, 1)]]
    cut_0, cut_1, cut_2 = cut_weight(turned, groups)
    here = moved(cut_0, to_before_near)
    rope = rope_step(rope_cot[0])
    grad = latent_step(hidden, turned, latent_cot[0], gain, rope, cut_0)
    grad = after(grad, here, mib=62)
    grad_other = moved(grad, to_core)
    grad_next = moved(grad, to_before)
    rest_1 = moved(cut_1, to_before_near)
    rest_2 = moved(cut_2, to_before_near)
    above, below = moved(here, to_z(-1)), moved(here, to_z(1))

    def both(value, *blocks):
        return value, moved(value, to_core), blocks

    own_a, send_a, own_b, send_b = weight_step(hidden, other, grad, grad_other)
    z = shard >> 2
    along_z = [[4 * z + k for z in range(4)] for k in range(4)]

    def exchanged(value):
        return lax.all_to_all(value, "dp", 0, 0, axis_index_groups=along_z, tiled=True)

    ra = exchanged(send_a)
    rb = moved(after(send_b, above, below, grad_next, mib=62), to_ylo)
    pieces = both(here, (0, 0)), both(above, (1, 0)), both(rest_1, (0, 1), (2, 0))
    received, is_begun = input_step(grad_next, pieces, [])
    send_b = (own_b + rb.astype(F32)).astype(BF)
    rz = exchanged(send_b)
    ra = after(ra, is_begun)
    send_a = received_sum(own_a[1], ra[:, 1], z).astype(BF)
    ry = moved(send_a, to_ylo)
    below = after(below, send_b)
    side = moved(below, to_ylo)
    total_a = received_sum(own_a[0], ra[:, 0], z) + ry.astype(F32)
    keep_b = lax.dynamic_index_in_dim(own_b, z, 0, False)
    keep_b += lax.dynamic_index_in_dim(rb, z, 0, False).astype(F32)
    total_b = received_sum(keep_b, after(rz, rest_2), z)
    send = jnp.concatenate([total_a, total_b], axis=0).astype(BF)
    far = moved(send, to_mirror)
    pieces = both(below, (3, 0)), both(side, (3, 1)), both(rest_2, (2, 1), (1, 1))
    received, _ = input_step(grad_next, pieces, [send], received)
    next_master, next_first, next_second, gain_rows = adam_step(
        s, total_a, total_b, far, master_weight[0], first_moment[0], second_moment[0]
    )
    gain_total = lax.dynamic_slice(gain_rows[:4].reshape(LAT), (shard * 32,), (32,))
    next_gain = adamw(gain_master[0], gain_first[0], gain_second[0], gain_total)
    return (
        received[None],
        next_master[None],
        next_first[None],
        next_second[None],
        *(value[None] for value in next_gain),
    )


def solution(mesh):
    tokens, shared = P("pipe", "dp", None), P("pipe", None)
    split = P("pipe", "dp")
    return jax.shard_map(
        on_device,
        mesh=mesh,
        in_specs=(tokens, P("pipe", None, None), shared) + (tokens,) * 5 + (split,) * 3,
        out_specs=(tokens,) * 4 + (split,) * 3,
        check_vma=False,
    )
```

```python
import jax
import jax.numpy as jnp
from jax import lax
from jax.experimental import pallas as pl
from jax.experimental.pallas import tpu as pltpu
from jax.sharding import PartitionSpec as P

beta_one = 0.9
beta_two = 0.95
adam_count = 10
learn_rate = 0.00022
adam_eps = 1e-08
decay_rate = 0.1

RANKS, SHARDS = 8, 16
TOK, WIDTH, LAT, ROPE = 512, 7168, 512, 64
COLS = LAT + ROPE
BLOCK = WIDTH // 8
TILE = 512
HALF = COLS // 2
ROWS_A = 3 * HALF + HALF // 2
ROWS_B = ROWS_A + 16
EXT = COLS + 16
BF, F32 = jnp.bfloat16, jnp.float32
MIB = 1 << 20


def params(mib):
    return pltpu.CompilerParams(vmem_limit_bytes=mib * MIB)


def cost(flops, moved):
    return pl.CostEstimate(flops=flops, bytes_accessed=moved, transcendentals=0)


def moved(value, target):
    pairs = []
    for r in range(RANKS):
        for d in range(SHARDS):
            to = target(r, d)
            if 0 <= to[0] < RANKS:
                pairs.append((r * SHARDS + d, to[0] * SHARDS + to[1]))
    return lax.ppermute(value, ("pipe", "dp"), pairs)


def to_core(r, d):
    return r, d ^ 1


def to_ylo(r, d):
    return r, d ^ 2


def to_z(steps):
    return lambda r, d: (r, (d + 4 * steps) % SHARDS)


def to_mirror(r, d):
    return RANKS - 1 - r, d


def to_before(r, d):
    return r - 1, d


def to_before_near(r, d):
    return r - 1, d ^ 2


FLAG = jax.ShapeDtypeStruct((8, 128), F32)
ANYWHERE = pl.BlockSpec(memory_space=pltpu.HBM)
LATER = pl.BlockSpec(memory_space=pl.ANY)


def place():
    shard = lax.axis_index("dp")
    return shard >> 2, (shard >> 1) & 1, shard & 1


def columns(block, core):
    return pl.ds(pl.multiple_of(block * BLOCK + 384 * core, 128), TILE)


def start_all(copies):
    for copy in copies:
        copy.start()


def wait_all(copies):
    for copy in copies:
        copy.wait()


def after(value, *earlier, mib=1):
    def kernel(*refs):
        pass

    return pl.pallas_call(
        kernel,
        in_specs=[ANYWHERE] + [LATER] * len(earlier),
        out_specs=ANYWHERE,
        out_shape=jax.ShapeDtypeStruct(value.shape, value.dtype),
        input_output_aliases={0: 0},
        compiler_params=params(mib),
        cost_estimate=cost(0, 0),
        name="after",
    )(value, *earlier)


def cut_weight(weight, groups):
    def kernel(weight, *rest):
        outs, sems = rest[:-1], rest[-1]
        z, y, core = place()
        rows = pl.ds(pl.multiple_of(core * HALF, HALF), HALF)
        copies = []
        for out, group in zip(outs, groups):
            for i, (dz, e) in enumerate(group):
                block = 2 * ((z + dz) & 3) + ((1 - y) ^ e)
                cols = pl.ds(pl.multiple_of(block * BLOCK, BLOCK), BLOCK)
                sem = sems.at[len(copies)]
                copies.append(pltpu.make_async_copy(weight.at[rows, cols], out.at[i], sem))
        start_all(copies)
        wait_all(copies)

    return pl.pallas_call(
        kernel,
        in_specs=[ANYWHERE],
        out_shape=[jax.ShapeDtypeStruct((len(group), HALF, BLOCK), BF) for group in groups],
        scratch_shapes=[pltpu.SemaphoreType.DMA((sum(len(group) for group in groups),))],
        compiler_params=params(60),
        cost_estimate=cost(0, 1_000),
        name="cut_weight",
    )(weight)


PARTS = 7
PART = WIDTH // PARTS


def latent_kernel(hidden, weight, cot, gain, rope, earlier, out, tokens, matrix, sems):
    copies = []
    for i in range(PARTS):
        cols = pl.ds(i * PART, PART)
        copies.append(
            (
                pltpu.make_async_copy(hidden.at[:, cols], tokens.at[:, cols], sems.at[0, i]),
                pltpu.make_async_copy(
                    weight.at[pl.ds(0, LAT), cols], matrix.at[:, cols], sems.at[1, i]
                ),
            )
        )
    for pair in copies:
        start_all(pair)
    latent = jnp.zeros((TOK, LAT), F32)
    for i in range(PARTS):
        wait_all(copies[i])
        cols = slice(i * PART, i * PART + PART)
        latent += lax.dot_general(
            tokens[:, cols],
            matrix[:, cols],
            (((1,), (1,)), ((), ())),
            preferred_element_type=F32,
        )
    inv = lax.rsqrt(jnp.mean(latent * latent, axis=-1, keepdims=True) + 1e-06)
    normed = latent * inv
    c = cot[...].astype(F32)
    scaled = c * gain[...]
    grad = inv * (scaled - normed * jnp.mean(scaled * normed, axis=-1, keepdims=True))
    gain_part = jnp.sum(c * normed, axis=0, keepdims=True)
    out[0:LAT, :] = grad.T.astype(BF)
    out[LAT:COLS, :] = rope[...]
    high = gain_part.astype(BF)
    low = (gain_part - high.astype(F32)).astype(BF)
    row = lax.broadcasted_iota(jnp.int32, (16, LAT), 0)
    high = jnp.broadcast_to(high.astype(F32), (16, LAT))
    low = jnp.broadcast_to(low.astype(F32), (16, LAT))
    both = jnp.where(row == 0, high, jnp.where(row == 1, low, 0.0))
    out[COLS:EXT, :] = both.astype(BF)


def latent_step(hidden, weight, cot, gain, rope, earlier):
    inside = pl.BlockSpec(memory_space=pltpu.VMEM)
    return pl.pallas_call(
        latent_kernel,
        in_specs=[ANYWHERE, ANYWHERE, inside, inside, inside, LATER],
        out_shape=jax.ShapeDtypeStruct((EXT, TOK), BF),
        scratch_shapes=[
            pltpu.VMEM((TOK, WIDTH), BF),
            pltpu.VMEM((LAT, WIDTH), BF),
            pltpu.SemaphoreType.DMA((2, PARTS)),
        ],
        compiler_params=params(60),
        cost_estimate=cost(0, 1_000),
        name="latent_grad",
    )(hidden, weight, cot, gain, rope, earlier)


def weight_kernel(
    hidden,
    other,
    grad,
    grad_other,
    own_a,
    send_a,
    own_b,
    send_b,
    tiles,
    turned,
    first_a,
    rest_a,
    keep_b,
    give_b,
    gain,
    in_sems,
    out_sems,
    grad_sems,
):
    z, y, core = place()
    steps = [(k, e) for k in (1, 2, 3, 0) for e in (1, 0)]
    incoming = []
    for i, (k, e) in enumerate(steps):
        cols = columns(2 * ((z + k) & 3) + (y ^ e), core)
        incoming.append(
            (
                pltpu.make_async_copy(
                    hidden.at[:, cols], tiles.at[i, pl.ds(0, TOK)], in_sems.at[0, i]
                ),
                pltpu.make_async_copy(
                    other.at[:, cols], tiles.at[i, pl.ds(TOK, TOK)], in_sems.at[1, i]
                ),
            )
        )
    grads = [
        pltpu.make_async_copy(grad, turned.at[:, pl.ds(0, TOK)], grad_sems.at[0]),
        pltpu.make_async_copy(grad_other, turned.at[:, pl.ds(TOK, TOK)], grad_sems.at[1]),
    ]
    start_all(grads)
    for pair in incoming[:2]:
        start_all(pair)
    wait_all(grads)

    sums = jnp.zeros((1, LAT), F32)
    for at in (0, TOK):
        pair = turned[COLS:EXT, at : at + TOK].astype(F32)
        sums = sums + pair[0:1] + pair[1:2]
    gain[...] = jnp.zeros_like(gain)
    for i in range(4):
        gain[i : i + 1, :] = sums[:, 128 * i : 128 * i + 128]

    lane = lax.broadcasted_iota(jnp.int32, (HALF // 2, 128), 1)
    first = core == 0

    def packed(full):
        col = [full[:, 128 * j : 128 * j + 128] for j in range(4)]
        edge = jnp.where(first, col[3], col[0])
        top, low = edge[: HALF // 2], edge[HALF // 2 :]
        left = jnp.where(first, top, pltpu.roll(top, 64, 1))
        right = jnp.where(first, pltpu.roll(low, 64, 1), low)
        return [jnp.where(first, col[i], col[i + 1]) for i in range(3)] + [
            jnp.where(lane < 64, left, right)
        ]

    def put(ref, parts):
        at = 0
        for part in parts:
            n = part.shape[0]
            ref[at : at + n, :] = part.astype(ref.dtype)
            at += n

    outgoing = []
    for i, (k, e) in enumerate(steps):
        wait_all(incoming[i])
        if i + 2 < len(steps):
            start_all(incoming[i + 2])
        whole = jnp.dot(turned[:COLS, :], tiles[i], preferred_element_type=F32)
        buffer_a = first_a.at[e] if k == 0 else rest_a.at[2 * (k - 1) + e]
        buffer_b = keep_b.at[k] if e == 0 else give_b.at[k]
        put(buffer_a, packed(whole[:HALF]))
        put(buffer_b, packed(whole[HALF:]) + [gain[...]])
        to_a = own_a.at[e] if k == 0 else send_a.at[(z + k) & 3, e]
        to_b = (own_b, send_b)[e].at[(z + k) & 3]
        outgoing.append(pltpu.make_async_copy(buffer_a, to_a, out_sems.at[0, i]))
        outgoing.append(pltpu.make_async_copy(buffer_b, to_b, out_sems.at[1, i]))
        start_all(outgoing[-2:])
    wait_all(outgoing)


def weight_step(hidden, other, grad, grad_other):
    return pl.pallas_call(
        weight_kernel,
        in_specs=[ANYWHERE] * 4,
        out_specs=[ANYWHERE] * 4,
        out_shape=[
            jax.ShapeDtypeStruct((2, ROWS_A, 128), F32),
            jax.ShapeDtypeStruct((4, 2, ROWS_A, 128), BF),
            jax.ShapeDtypeStruct((4, ROWS_B, 128), F32),
            jax.ShapeDtypeStruct((4, ROWS_B, 128), BF),
        ],
        scratch_shapes=[
            pltpu.VMEM((8, 2 * TOK, TILE), BF),
            pltpu.VMEM((EXT, 2 * TOK), BF),
            pltpu.VMEM((2, ROWS_A, 128), F32),
            pltpu.VMEM((6, ROWS_A, 128), BF),
            pltpu.VMEM((4, ROWS_B, 128), F32),
            pltpu.VMEM((4, ROWS_B, 128), BF),
            pltpu.VMEM((16, 128), F32),
            pltpu.SemaphoreType.DMA((2, 8)),
            pltpu.SemaphoreType.DMA((2, 8)),
            pltpu.SemaphoreType.DMA((2,)),
        ],
        compiler_params=params(60),
        cost_estimate=cost(0, 1_000),
        name="weight_grad",
    )(hidden, other, grad, grad_other)


def received_sum(own, parts, z):
    for other in range(4):
        own = own + jnp.where(z == other, 0.0, parts[other].astype(F32))
    return own


def adamw(master, first, second, grad):
    new_first = beta_one * first + (1.0 - beta_one) * grad
    new_second = beta_two * second + (1.0 - beta_two) * grad * grad
    first_hat = new_first / (1.0 - beta_one**adam_count)
    second_hat = new_second / (1.0 - beta_two**adam_count)
    new_master = master - learn_rate * (
        first_hat / (jnp.sqrt(second_hat) + adam_eps) + decay_rate * master
    )
    return (new_master, new_first, new_second)


def adam_kernel(s, own_a, own_b, far, master, first, second, n_master, n_first, n_second, gain, grad):
    total_a = own_a[...] + far[:ROWS_A, :].astype(F32)
    total_b = own_b[...] + far[ROWS_A:, :].astype(F32)
    core = s[0]
    gain[...] = total_b[ROWS_A : ROWS_A + 8]

    def both(lo, n):
        return [total[lo : lo + n] for total in (total_a, total_b)]

    for i in range(3):
        block = jnp.concatenate(both(i * HALF, HALF), axis=0)
        grad[pl.ds(pl.multiple_of(64 * core + 128 * i, 64), 128), :] = block.T
    edge = []
    for part in both(3 * HALF, HALF // 2):
        edge += [part, pltpu.roll(part, 64, 1)]
    block = jnp.concatenate(edge, axis=0)
    grad[pl.ds(pl.multiple_of(384 * (1 - core), 64), 64), :] = block.T[:64]
    n_master[...], n_first[...], n_second[...] = adamw(
        master[...], first[...], second[...], grad[...]
    )


def adam_step(s, own_a, own_b, far, master, first, second):
    shape = jax.ShapeDtypeStruct(master.shape, F32)
    spec = pl.BlockSpec(memory_space=pltpu.VMEM)
    return pl.pallas_call(
        adam_kernel,
        in_specs=[pl.BlockSpec(memory_space=pltpu.SMEM)] + [spec] * 6,
        out_specs=[spec] * 4,
        out_shape=[shape] * 3 + [jax.ShapeDtypeStruct((8, 128), F32)],
        scratch_shapes=[pltpu.VMEM(master.shape, F32)],
        compiler_params=params(32),
        cost_estimate=cost(0, 9_000_000),
        name="adamw",
    )(s, own_a, own_b, far, master, first, second)


def input_step(grad, pieces, earlier, begun=None):
    places = [(n, i, dz, e) for n, piece in enumerate(pieces) for i, (dz, e) in enumerate(piece[2])]
    count, arrays = len(places), len(pieces)

    def kernel(grad, *rest):
        halves = rest[: 2 * arrays]
        out, flag, held, blocks, in_sems, out_sems = rest[-6:]
        z, y, core = place()
        incoming = []
        for at, (n, i, _, _) in enumerate(places):
            for half in range(2):
                slot = core ^ half
                rows = pl.ds(pl.multiple_of(slot * HALF, HALF), HALF)
                incoming.append(
                    pltpu.make_async_copy(
                        halves[2 * n + half].at[i], held.at[at, rows], in_sems.at[at, half]
                    )
                )
        start_all(incoming)
        flag[...] = jnp.zeros_like(flag)
        turned = grad[:COLS, :].astype(F32).T.astype(BF)
        outgoing = []
        for at, (_, _, dz, e) in enumerate(places):
            wait_all(incoming[2 * at : 2 * at + 2])
            blocks[at] = jnp.dot(turned, held[at], preferred_element_type=F32).astype(BF)
            block = 2 * ((z + dz) & 3) + (y ^ e)
            cols = pl.ds(pl.multiple_of(block * BLOCK, BLOCK), BLOCK)
            outgoing.append(
                pltpu.make_async_copy(blocks.at[at], out.at[:, cols], out_sems.at[at])
            )
            outgoing[-1].start()
        wait_all(outgoing)

    inside = pl.BlockSpec(memory_space=pltpu.VMEM)
    operands = [grad]
    for own, far, _ in pieces:
        operands += [own, far]
    halves = len(operands) - 1
    operands += earlier + ([] if begun is None else [begun])
    return pl.pallas_call(
        kernel,
        in_specs=[inside]
        + [ANYWHERE] * halves
        + [LATER] * len(earlier)
        + ([] if begun is None else [ANYWHERE]),
        out_specs=[ANYWHERE, inside],
        out_shape=[jax.ShapeDtypeStruct((TOK, WIDTH), BF), FLAG],
        scratch_shapes=[
            pltpu.VMEM((count, COLS, BLOCK), BF),
            pltpu.VMEM((count, TOK, BLOCK), BF),
            pltpu.SemaphoreType.DMA((count, 2)),
            pltpu.SemaphoreType.DMA((count,)),
        ],
        input_output_aliases={} if begun is None else {len(operands) - 1: 0},
        compiler_params=params(60),
        cost_estimate=cost(TOK * WIDTH * COLS, 8_000_000),
        name="input_grad",
    )(*operands)


def rope_step(rope_cot):
    half = ROPE // 2
    position = jnp.arange(TOK).astype(F32)
    freqs = 10000.0 ** (-2.0 * jnp.arange(half).astype(F32) / ROPE)
    angle = freqs[:, None] * position[None, :]
    cosine = jnp.cos(angle)
    sine = jnp.sin(angle)
    rope = rope_cot.T.astype(F32)
    first, second = rope[:half], rope[half:]
    return jnp.concatenate(
        [first * cosine + second * sine, second * cosine - first * sine], axis=0
    ).astype(BF)


def on_device(
    hidden_in,
    weight,
    gain,
    latent_cot,
    rope_cot,
    master_weight,
    first_moment,
    second_moment,
    gain_master,
    gain_first,
    gain_second,
):
    shard = lax.axis_index("dp")
    s = (shard & 1).astype(jnp.int32)[None]
    hidden = hidden_in[0]
    turned = weight[0].T
    other = moved(hidden, to_core)
    groups = [[(0, 0)], [(2, 0), (2, 1)], [(1, 1), (3, 1)]]
    cut_0, cut_1, cut_2 = cut_weight(turned, groups)
    here = moved(cut_0, to_before_near)
    rope = rope_step(rope_cot[0])
    grad = latent_step(hidden, turned, latent_cot[0], gain, rope, cut_0)
    grad_other = moved(grad, to_core)
    rest_1 = moved(after(cut_1, here, mib=62), to_before_near)
    rest_2 = moved(after(cut_2, rest_1, mib=62), to_before_near)
    above, below = moved(here, to_z(-1)), moved(here, to_z(1))
    beside = moved(here, to_ylo)

    def both(value, *blocks):
        return value, moved(value, to_core), blocks

    own_a, send_a, own_b, send_b = weight_step(hidden, other, grad, grad_other)
    z = shard >> 2
    along_z = [[4 * z + k for z in range(4)] for k in range(4)]

    def exchanged(value):
        return lax.all_to_all(value, "dp", 0, 0, axis_index_groups=along_z, tiled=True)

    ra = exchanged(send_a)
    rb = moved(after(send_b, above, below, beside, rest_1, mib=62), to_ylo)
    pieces = [
        both(here, (0, 0)),
        both(above, (1, 0)),
        both(below, (3, 0)),
        both(beside, (0, 1)),
        both(rest_1, *groups[1]),
        both(rest_2, *groups[2]),
    ]
    rb = after(rb, *(piece[1] for piece in pieces[:4]))
    send_b = (own_b + rb.astype(F32)).astype(BF)
    grad_next = moved(after(grad, send_b, mib=62), to_before)
    rz = exchanged(send_b)
    send_a = received_sum(own_a[1], ra[:, 1], z).astype(BF)
    ry = moved(send_a, to_ylo)
    total_a = received_sum(own_a[0], ra[:, 0], z) + ry.astype(F32)
    keep_b = lax.dynamic_index_in_dim(own_b, z, 0, False)
    keep_b += lax.dynamic_index_in_dim(rb, z, 0, False).astype(F32)
    total_b = received_sum(keep_b, after(rz, rest_2), z)
    send = jnp.concatenate([total_a, total_b], axis=0).astype(BF)
    far = moved(send, to_mirror)
    received, _ = input_step(grad_next, pieces, [send])
    next_master, next_first, next_second, gain_rows = adam_step(
        s, total_a, total_b, far, master_weight[0], first_moment[0], second_moment[0]
    )
    gain_total = lax.dynamic_slice(gain_rows[:4].reshape(LAT), (shard * 32,), (32,))
    next_gain = adamw(gain_master[0], gain_first[0], gain_second[0], gain_total)
    return (
        received[None],
        next_master[None],
        next_first[None],
        next_second[None],
        *(value[None] for value in next_gain),
    )


def solution(mesh):
    tokens, shared = P("pipe", "dp", None), P("pipe", None)
    split = P("pipe", "dp")
    return jax.shard_map(
        on_device,
        mesh=mesh,
        in_specs=(tokens, P("pipe", None, None), shared) + (tokens,) * 5 + (split,) * 3,
        out_specs=(tokens,) * 4 + (split,) * 3,
        check_vma=False,
    )
```

```python
import jax
import jax.numpy as jnp
from jax import lax
from jax.experimental import pallas as pl
from jax.experimental.pallas import tpu as pltpu
from jax.sharding import PartitionSpec as P

beta_one = 0.9
beta_two = 0.95
adam_count = 10
learn_rate = 0.00022
adam_eps = 1e-08
decay_rate = 0.1

RANKS, SHARDS = 8, 16
TOK, WIDTH, LAT, ROPE = 512, 7168, 512, 64
COLS = LAT + ROPE
BLOCK = WIDTH // 8
TILE = 512
HALF = COLS // 2
ROWS_A = 3 * HALF + HALF // 2
ROWS_B = ROWS_A + 16
EXT = COLS + 16
BF, F32 = jnp.bfloat16, jnp.float32
MIB = 1 << 20


def params(mib):
    return pltpu.CompilerParams(vmem_limit_bytes=mib * MIB)


def cost(flops, moved):
    return pl.CostEstimate(flops=flops, bytes_accessed=moved, transcendentals=0)


def moved(value, target):
    pairs = []
    for r in range(RANKS):
        for d in range(SHARDS):
            to = target(r, d)
            if 0 <= to[0] < RANKS:
                pairs.append((r * SHARDS + d, to[0] * SHARDS + to[1]))
    return lax.ppermute(value, ("pipe", "dp"), pairs)


def to_core(r, d):
    return r, d ^ 1


def to_ylo(r, d):
    return r, d ^ 2


def to_z(steps):
    return lambda r, d: (r, (d + 4 * steps) % SHARDS)


def to_mirror(r, d):
    return RANKS - 1 - r, d


def to_before(r, d):
    return r - 1, d


def to_before_near(r, d):
    return r - 1, d ^ 2


FLAG = jax.ShapeDtypeStruct((8, 128), F32)
ANYWHERE = pl.BlockSpec(memory_space=pltpu.HBM)
LATER = pl.BlockSpec(memory_space=pl.ANY)


def place():
    shard = lax.axis_index("dp")
    return shard >> 2, (shard >> 1) & 1, shard & 1


def columns(block, core):
    return pl.ds(pl.multiple_of(block * BLOCK + 384 * core, 128), TILE)


def start_all(copies):
    for copy in copies:
        copy.start()


def wait_all(copies):
    for copy in copies:
        copy.wait()


def after(value, *earlier, mib=1):
    def kernel(*refs):
        pass

    return pl.pallas_call(
        kernel,
        in_specs=[ANYWHERE] + [LATER] * len(earlier),
        out_specs=ANYWHERE,
        out_shape=jax.ShapeDtypeStruct(value.shape, value.dtype),
        input_output_aliases={0: 0},
        compiler_params=params(mib),
        cost_estimate=cost(0, 0),
        name="after",
    )(value, *earlier)


def cut_weight(weight, groups):
    def kernel(weight, *rest):
        outs, sems = rest[:-1], rest[-1]
        z, y, core = place()
        rows = pl.ds(pl.multiple_of(core * HALF, HALF), HALF)
        copies = []
        for out, group in zip(outs, groups):
            for i, (dz, e) in enumerate(group):
                block = 2 * ((z + dz) & 3) + ((1 - y) ^ e)
                cols = pl.ds(pl.multiple_of(block * BLOCK, BLOCK), BLOCK)
                sem = sems.at[len(copies)]
                copies.append(pltpu.make_async_copy(weight.at[rows, cols], out.at[i], sem))
        start_all(copies)
        wait_all(copies)

    return pl.pallas_call(
        kernel,
        in_specs=[ANYWHERE],
        out_shape=[jax.ShapeDtypeStruct((len(group), HALF, BLOCK), BF) for group in groups],
        scratch_shapes=[pltpu.SemaphoreType.DMA((sum(len(group) for group in groups),))],
        compiler_params=params(60),
        cost_estimate=cost(0, 1_000),
        name="cut_weight",
    )(weight)


PARTS = 7
PART = WIDTH // PARTS


def latent_kernel(hidden, weight, cot, gain, rope, earlier, out, tokens, matrix, sems):
    copies = []
    for i in range(PARTS):
        cols = pl.ds(i * PART, PART)
        copies.append(
            (
                pltpu.make_async_copy(hidden.at[:, cols], tokens.at[:, cols], sems.at[0, i]),
                pltpu.make_async_copy(
                    weight.at[pl.ds(0, LAT), cols], matrix.at[:, cols], sems.at[1, i]
                ),
            )
        )
    for pair in copies:
        start_all(pair)
    latent = jnp.zeros((TOK, LAT), F32)
    for i in range(PARTS):
        wait_all(copies[i])
        cols = slice(i * PART, i * PART + PART)
        latent += lax.dot_general(
            tokens[:, cols],
            matrix[:, cols],
            (((1,), (1,)), ((), ())),
            preferred_element_type=F32,
        )
    inv = lax.rsqrt(jnp.mean(latent * latent, axis=-1, keepdims=True) + 1e-06)
    normed = latent * inv
    c = cot[...].astype(F32)
    scaled = c * gain[...]
    grad = inv * (scaled - normed * jnp.mean(scaled * normed, axis=-1, keepdims=True))
    gain_part = jnp.sum(c * normed, axis=0, keepdims=True)
    out[0:LAT, :] = grad.T.astype(BF)
    out[LAT:COLS, :] = rope[...]
    high = gain_part.astype(BF)
    low = (gain_part - high.astype(F32)).astype(BF)
    row = lax.broadcasted_iota(jnp.int32, (16, LAT), 0)
    high = jnp.broadcast_to(high.astype(F32), (16, LAT))
    low = jnp.broadcast_to(low.astype(F32), (16, LAT))
    both = jnp.where(row == 0, high, jnp.where(row == 1, low, 0.0))
    out[COLS:EXT, :] = both.astype(BF)


def latent_step(hidden, weight, cot, gain, rope, earlier):
    inside = pl.BlockSpec(memory_space=pltpu.VMEM)
    return pl.pallas_call(
        latent_kernel,
        in_specs=[ANYWHERE, ANYWHERE, inside, inside, inside, LATER],
        out_shape=jax.ShapeDtypeStruct((EXT, TOK), BF),
        scratch_shapes=[
            pltpu.VMEM((TOK, WIDTH), BF),
            pltpu.VMEM((LAT, WIDTH), BF),
            pltpu.SemaphoreType.DMA((2, PARTS)),
        ],
        compiler_params=params(60),
        cost_estimate=cost(0, 1_000),
        name="latent_grad",
    )(hidden, weight, cot, gain, rope, earlier)


def weight_kernel(
    hidden,
    other,
    grad,
    grad_other,
    own_a,
    send_a,
    own_b,
    send_b,
    tiles,
    turned,
    first_a,
    rest_a,
    keep_b,
    give_b,
    gain,
    in_sems,
    out_sems,
    grad_sems,
):
    z, y, core = place()
    steps = [(k, e) for k in (1, 2, 3, 0) for e in (1, 0)]
    incoming = []
    for i, (k, e) in enumerate(steps):
        cols = columns(2 * ((z + k) & 3) + (y ^ e), core)
        incoming.append(
            (
                pltpu.make_async_copy(
                    hidden.at[:, cols], tiles.at[i, pl.ds(0, TOK)], in_sems.at[0, i]
                ),
                pltpu.make_async_copy(
                    other.at[:, cols], tiles.at[i, pl.ds(TOK, TOK)], in_sems.at[1, i]
                ),
            )
        )
    grads = [
        pltpu.make_async_copy(grad, turned.at[:, pl.ds(0, TOK)], grad_sems.at[0]),
        pltpu.make_async_copy(grad_other, turned.at[:, pl.ds(TOK, TOK)], grad_sems.at[1]),
    ]
    start_all(grads)
    for pair in incoming[:2]:
        start_all(pair)
    wait_all(grads)

    sums = jnp.zeros((1, LAT), F32)
    for at in (0, TOK):
        pair = turned[COLS:EXT, at : at + TOK].astype(F32)
        sums = sums + pair[0:1] + pair[1:2]
    gain[...] = jnp.zeros_like(gain)
    for i in range(4):
        gain[i : i + 1, :] = sums[:, 128 * i : 128 * i + 128]

    lane = lax.broadcasted_iota(jnp.int32, (HALF // 2, 128), 1)
    first = core == 0

    def packed(full):
        col = [full[:, 128 * j : 128 * j + 128] for j in range(4)]
        edge = jnp.where(first, col[3], col[0])
        top, low = edge[: HALF // 2], edge[HALF // 2 :]
        left = jnp.where(first, top, pltpu.roll(top, 64, 1))
        right = jnp.where(first, pltpu.roll(low, 64, 1), low)
        return [jnp.where(first, col[i], col[i + 1]) for i in range(3)] + [
            jnp.where(lane < 64, left, right)
        ]

    def put(ref, parts):
        at = 0
        for part in parts:
            n = part.shape[0]
            ref[at : at + n, :] = part.astype(ref.dtype)
            at += n

    outgoing = []
    for i, (k, e) in enumerate(steps):
        wait_all(incoming[i])
        if i + 2 < len(steps):
            start_all(incoming[i + 2])
        whole = jnp.dot(turned[:COLS, :], tiles[i], preferred_element_type=F32)
        buffer_a = first_a.at[e] if k == 0 else rest_a.at[2 * (k - 1) + e]
        buffer_b = keep_b.at[k] if e == 0 else give_b.at[k]
        put(buffer_a, packed(whole[:HALF]))
        put(buffer_b, packed(whole[HALF:]) + [gain[...]])
        to_a = own_a.at[e] if k == 0 else send_a.at[(z + k) & 3, e]
        to_b = (own_b, send_b)[e].at[(z + k) & 3]
        outgoing.append(pltpu.make_async_copy(buffer_a, to_a, out_sems.at[0, i]))
        outgoing.append(pltpu.make_async_copy(buffer_b, to_b, out_sems.at[1, i]))
        start_all(outgoing[-2:])
    wait_all(outgoing)


def weight_step(hidden, other, grad, grad_other):
    return pl.pallas_call(
        weight_kernel,
        in_specs=[ANYWHERE] * 4,
        out_specs=[ANYWHERE] * 4,
        out_shape=[
            jax.ShapeDtypeStruct((2, ROWS_A, 128), F32),
            jax.ShapeDtypeStruct((4, 2, ROWS_A, 128), BF),
            jax.ShapeDtypeStruct((4, ROWS_B, 128), F32),
            jax.ShapeDtypeStruct((4, ROWS_B, 128), BF),
        ],
        scratch_shapes=[
            pltpu.VMEM((8, 2 * TOK, TILE), BF),
            pltpu.VMEM((EXT, 2 * TOK), BF),
            pltpu.VMEM((2, ROWS_A, 128), F32),
            pltpu.VMEM((6, ROWS_A, 128), BF),
            pltpu.VMEM((4, ROWS_B, 128), F32),
            pltpu.VMEM((4, ROWS_B, 128), BF),
            pltpu.VMEM((16, 128), F32),
            pltpu.SemaphoreType.DMA((2, 8)),
            pltpu.SemaphoreType.DMA((2, 8)),
            pltpu.SemaphoreType.DMA((2,)),
        ],
        compiler_params=params(60),
        cost_estimate=cost(0, 1_000),
        name="weight_grad",
    )(hidden, other, grad, grad_other)


def received_sum(own, parts, z):
    for other in range(4):
        own = own + jnp.where(z == other, 0.0, parts[other].astype(F32))
    return own


def adamw(master, first, second, grad):
    new_first = beta_one * first + (1.0 - beta_one) * grad
    new_second = beta_two * second + (1.0 - beta_two) * grad * grad
    first_hat = new_first / (1.0 - beta_one**adam_count)
    second_hat = new_second / (1.0 - beta_two**adam_count)
    new_master = master - learn_rate * (
        first_hat / (jnp.sqrt(second_hat) + adam_eps) + decay_rate * master
    )
    return (new_master, new_first, new_second)


def adam_kernel(own_a, own_b, far, *rest):
    state, outs, gain_out = rest[:3], rest[3:6], rest[6]
    sum_a, sum_b, sum_far, held, new, grad, gain, sems, out_sems, gain_sem = rest[7:]
    sums = [
        pltpu.make_async_copy(source, target, sems.at[i])
        for i, (source, target) in enumerate(((own_a, sum_a), (own_b, sum_b), (far, sum_far)))
    ]
    loads = [
        pltpu.make_async_copy(ref, held.at[i], sems.at[3 + i]) for i, ref in enumerate(state)
    ]
    start_all(sums + loads)
    wait_all(sums)
    total_a = sum_a[...] + sum_far[:ROWS_A, :].astype(F32)
    total_b = sum_b[...] + sum_far[ROWS_A:, :].astype(F32)
    _, _, core = place()
    gain[...] = total_b[ROWS_A : ROWS_A + 8]
    gain_copy = pltpu.make_async_copy(gain, gain_out, gain_sem)
    gain_copy.start()

    def both(lo, n):
        return [total[lo : lo + n] for total in (total_a, total_b)]

    for i in range(3):
        block = jnp.concatenate(both(i * HALF, HALF), axis=0)
        grad[pl.ds(pl.multiple_of(64 * core + 128 * i, 64), 128), :] = block.T
    edge = []
    for part in both(3 * HALF, HALF // 2):
        edge += [part, pltpu.roll(part, 64, 1)]
    block = jnp.concatenate(edge, axis=0)
    grad[pl.ds(pl.multiple_of(384 * (1 - core), 64), 64), :] = block.T[:64]
    wait_all(loads)
    rows, stores = held.shape[1] // 4, []
    for n in range(4):
        at = slice(n * rows, n * rows + rows)
        values = adamw(held[0, at], held[1, at], held[2, at], grad[at])
        for i, value in enumerate(values):
            new[i, at] = value
            part = pl.ds(n * rows, rows)
            stores.append(
                pltpu.make_async_copy(new.at[i, part], outs[i].at[part], out_sems.at[n, i])
            )
            stores[-1].start()
    wait_all(stores)
    gain_copy.wait()


def adam_step(own_a, own_b, far, master, first, second):
    shape = jax.ShapeDtypeStruct(master.shape, F32)
    return pl.pallas_call(
        adam_kernel,
        in_specs=[LATER] * 6,
        out_specs=[LATER] * 4,
        out_shape=[shape] * 3 + [jax.ShapeDtypeStruct((8, 128), F32)],
        scratch_shapes=[
            pltpu.VMEM(own_a.shape, F32),
            pltpu.VMEM(own_b.shape, F32),
            pltpu.VMEM(far.shape, BF),
            pltpu.VMEM((3, *master.shape), F32),
            pltpu.VMEM((3, *master.shape), F32),
            pltpu.VMEM(master.shape, F32),
            pltpu.VMEM((8, 128), F32),
            pltpu.SemaphoreType.DMA((6,)),
            pltpu.SemaphoreType.DMA((4, 3)),
            pltpu.SemaphoreType.DMA,
        ],
        compiler_params=params(60),
        cost_estimate=cost(0, 9_000_000),
        name="adamw",
    )(own_a, own_b, far, master, first, second)


def input_step(grad, pieces, earlier, begun=None):
    places = [(n, i, dz, e) for n, piece in enumerate(pieces) for i, (dz, e) in enumerate(piece[2])]
    count, arrays = len(places), len(pieces)

    def kernel(grad, *rest):
        halves = rest[: 2 * arrays]
        out, flag, held, blocks, in_sems, out_sems = rest[-6:]
        z, y, core = place()
        incoming = []
        for at, (n, i, _, _) in enumerate(places):
            for half in range(2):
                slot = core ^ half
                rows = pl.ds(pl.multiple_of(slot * HALF, HALF), HALF)
                incoming.append(
                    pltpu.make_async_copy(
                        halves[2 * n + half].at[i], held.at[at, rows], in_sems.at[at, half]
                    )
                )
        start_all(incoming)
        flag[...] = jnp.zeros_like(flag)
        turned = grad[:COLS, :].astype(F32).T.astype(BF)
        outgoing = []
        for at, (_, _, dz, e) in enumerate(places):
            wait_all(incoming[2 * at : 2 * at + 2])
            blocks[at] = jnp.dot(turned, held[at], preferred_element_type=F32).astype(BF)
            block = 2 * ((z + dz) & 3) + (y ^ e)
            cols = pl.ds(pl.multiple_of(block * BLOCK, BLOCK), BLOCK)
            outgoing.append(
                pltpu.make_async_copy(blocks.at[at], out.at[:, cols], out_sems.at[at])
            )
            outgoing[-1].start()
        wait_all(outgoing)

    inside = pl.BlockSpec(memory_space=pltpu.VMEM)
    operands = [grad]
    for own, far, _ in pieces:
        operands += [own, far]
    halves = len(operands) - 1
    operands += earlier + ([] if begun is None else [begun])
    return pl.pallas_call(
        kernel,
        in_specs=[inside]
        + [ANYWHERE] * halves
        + [LATER] * len(earlier)
        + ([] if begun is None else [ANYWHERE]),
        out_specs=[ANYWHERE, inside],
        out_shape=[jax.ShapeDtypeStruct((TOK, WIDTH), BF), FLAG],
        scratch_shapes=[
            pltpu.VMEM((count, COLS, BLOCK), BF),
            pltpu.VMEM((count, TOK, BLOCK), BF),
            pltpu.SemaphoreType.DMA((count, 2)),
            pltpu.SemaphoreType.DMA((count,)),
        ],
        input_output_aliases={} if begun is None else {len(operands) - 1: 0},
        compiler_params=params(60),
        cost_estimate=cost(TOK * WIDTH * COLS, 8_000_000),
        name="input_grad",
    )(*operands)


def rope_step(rope_cot):
    half = ROPE // 2
    position = jnp.arange(TOK).astype(F32)
    freqs = 10000.0 ** (-2.0 * jnp.arange(half).astype(F32) / ROPE)
    angle = freqs[:, None] * position[None, :]
    cosine = jnp.cos(angle)
    sine = jnp.sin(angle)
    rope = rope_cot.T.astype(F32)
    first, second = rope[:half], rope[half:]
    return jnp.concatenate(
        [first * cosine + second * sine, second * cosine - first * sine], axis=0
    ).astype(BF)


def on_device(
    hidden_in,
    weight,
    gain,
    latent_cot,
    rope_cot,
    master_weight,
    first_moment,
    second_moment,
    gain_master,
    gain_first,
    gain_second,
):
    shard = lax.axis_index("dp")
    hidden = hidden_in[0]
    turned = weight[0].T
    other = moved(hidden, to_core)
    groups = [[(0, 0), (0, 1)], [(2, 0), (2, 1)]]
    cut_1, cut_2 = cut_weight(turned, groups)
    rest_1 = moved(cut_1, to_before_near)
    rope = rope_step(rope_cot[0])
    grad = latent_step(hidden, turned, latent_cot[0], gain, rope, cut_1)
    grad_other = moved(grad, to_core)

    def both(value, *blocks):
        return value, moved(value, to_core), blocks

    own_a, send_a, own_b, send_b = weight_step(hidden, other, grad, grad_other)
    z = shard >> 2
    along_z = [[4 * z + k for z in range(4)] for k in range(4)]

    def exchanged(value):
        return lax.all_to_all(value, "dp", 0, 0, axis_index_groups=along_z, tiled=True)

    ra = exchanged(send_a)
    rb = moved(after(send_b, rest_1, mib=62), to_ylo)
    rest_2 = moved(after(cut_2, own_a, mib=62), to_before_near)
    piece_2 = both(rest_2, *groups[1])
    send_b = (own_b + rb.astype(F32)).astype(BF)
    grad_next = moved(after(grad, send_b, mib=62), to_before)
    rz = exchanged(send_b)
    send_a = received_sum(own_a[1], ra[:, 1], z).astype(BF)
    ry = after(moved(send_a, to_ylo), grad_next, piece_2[1])
    total_a = received_sum(own_a[0], ra[:, 0], z) + ry.astype(F32)
    keep_b = lax.dynamic_index_in_dim(own_b, z, 0, False)
    keep_b += lax.dynamic_index_in_dim(rb, z, 0, False).astype(F32)
    total_b = received_sum(keep_b, rz, z)
    send = jnp.concatenate([total_a, total_b], axis=0).astype(BF)
    far = moved(send, to_mirror)
    here = after(rest_1, send_a, mib=62)
    above, below = moved(here, to_z(-1)), moved(here, to_z(1))
    pieces = [both(here, *groups[0]), piece_2]
    received, is_begun = input_step(grad_next, pieces, [send])
    above = after(above, is_begun, far, mib=62)
    below = after(below, is_begun, far, mib=62)
    pieces = [both(above, (1, 0), (1, 1)), both(below, (3, 0), (3, 1))]
    received, _ = input_step(grad_next, pieces, [], received)
    next_master, next_first, next_second, gain_rows = adam_step(
        total_a, total_b, far, master_weight[0], first_moment[0], second_moment[0]
    )
    gain_total = lax.dynamic_slice(gain_rows[:4].reshape(LAT), (shard * 32,), (32,))
    next_gain = adamw(gain_master[0], gain_first[0], gain_second[0], gain_total)
    return (
        received[None],
        next_master[None],
        next_first[None],
        next_second[None],
        *(value[None] for value in next_gain),
    )


def solution(mesh):
    tokens, shared = P("pipe", "dp", None), P("pipe", None)
    split = P("pipe", "dp")
    return jax.shard_map(
        on_device,
        mesh=mesh,
        in_specs=(tokens, P("pipe", None, None), shared) + (tokens,) * 5 + (split,) * 3,
        out_specs=(tokens,) * 4 + (split,) * 3,
        check_vma=False,
    )
```

```python
import jax
import jax.numpy as jnp
from jax import lax
from jax.experimental import pallas as pl
from jax.experimental.pallas import tpu as pltpu
from jax.sharding import PartitionSpec as P

beta_one = 0.9
beta_two = 0.95
adam_count = 10
learn_rate = 0.00022
adam_eps = 1e-08
decay_rate = 0.1

RANKS, SHARDS = 8, 16
TOK, WIDTH, LAT, ROPE = 512, 7168, 512, 64
COLS = LAT + ROPE
BLOCK = WIDTH // 8
TILE = 512
HALF = COLS // 2
ROWS_A = 3 * HALF + HALF // 2
ROWS_B = ROWS_A + 16
EXT = COLS + 16
BF, F32 = jnp.bfloat16, jnp.float32
MIB = 1 << 20


def params(mib):
    return pltpu.CompilerParams(vmem_limit_bytes=mib * MIB)


def cost(flops, moved):
    return pl.CostEstimate(flops=flops, bytes_accessed=moved, transcendentals=0)


def moved(value, target):
    pairs = []
    for r in range(RANKS):
        for d in range(SHARDS):
            to = target(r, d)
            if 0 <= to[0] < RANKS:
                pairs.append((r * SHARDS + d, to[0] * SHARDS + to[1]))
    return lax.ppermute(value, ("pipe", "dp"), pairs)


def to_core(r, d):
    return r, d ^ 1


def to_ylo(r, d):
    return r, d ^ 2


def to_z(steps):
    return lambda r, d: (r, (d + 4 * steps) % SHARDS)


def to_mirror(r, d):
    return RANKS - 1 - r, d


def to_before(r, d):
    return r - 1, d


def to_before_near(r, d):
    return r - 1, d ^ 2


FLAG = jax.ShapeDtypeStruct((8, 128), F32)
ANYWHERE = pl.BlockSpec(memory_space=pltpu.HBM)
LATER = pl.BlockSpec(memory_space=pl.ANY)


def place():
    shard = lax.axis_index("dp")
    return shard >> 2, (shard >> 1) & 1, shard & 1


def columns(block, core):
    return pl.ds(pl.multiple_of(block * BLOCK + 384 * core, 128), TILE)


def start_all(copies):
    for copy in copies:
        copy.start()


def wait_all(copies):
    for copy in copies:
        copy.wait()


def after(value, *earlier, mib=1):
    def kernel(*refs):
        pass

    return pl.pallas_call(
        kernel,
        in_specs=[ANYWHERE] + [LATER] * len(earlier),
        out_specs=ANYWHERE,
        out_shape=jax.ShapeDtypeStruct(value.shape, value.dtype),
        input_output_aliases={0: 0},
        compiler_params=params(mib),
        cost_estimate=cost(0, 0),
        name="after",
    )(value, *earlier)


def cut_weight(weight, groups):
    def kernel(weight, *rest):
        outs, sems = rest[:-1], rest[-1]
        z, y, core = place()
        rows = pl.ds(pl.multiple_of(core * HALF, HALF), HALF)
        copies = []
        for out, group in zip(outs, groups):
            for i, (dz, e) in enumerate(group):
                block = 2 * ((z + dz) & 3) + ((1 - y) ^ e)
                cols = pl.ds(pl.multiple_of(block * BLOCK, BLOCK), BLOCK)
                sem = sems.at[len(copies)]
                copies.append(pltpu.make_async_copy(weight.at[rows, cols], out.at[i], sem))
        start_all(copies)
        wait_all(copies)

    return pl.pallas_call(
        kernel,
        in_specs=[ANYWHERE],
        out_shape=[jax.ShapeDtypeStruct((len(group), HALF, BLOCK), BF) for group in groups],
        scratch_shapes=[pltpu.SemaphoreType.DMA((sum(len(group) for group in groups),))],
        compiler_params=params(60),
        cost_estimate=cost(0, 1_000),
        name="cut_weight",
    )(weight)


PARTS = 7
PART = WIDTH // PARTS


def latent_kernel(hidden, weight, cot, gain, rope, earlier, out, tokens, matrix, sems):
    copies = []
    for i in range(PARTS):
        cols = pl.ds(i * PART, PART)
        copies.append(
            (
                pltpu.make_async_copy(hidden.at[:, cols], tokens.at[:, cols], sems.at[0, i]),
                pltpu.make_async_copy(
                    weight.at[pl.ds(0, LAT), cols], matrix.at[:, cols], sems.at[1, i]
                ),
            )
        )
    for pair in copies:
        start_all(pair)
    latent = jnp.zeros((TOK, LAT), F32)
    for i in range(PARTS):
        wait_all(copies[i])
        cols = slice(i * PART, i * PART + PART)
        latent += lax.dot_general(
            tokens[:, cols],
            matrix[:, cols],
            (((1,), (1,)), ((), ())),
            preferred_element_type=F32,
        )
    inv = lax.rsqrt(jnp.mean(latent * latent, axis=-1, keepdims=True) + 1e-06)
    normed = latent * inv
    c = cot[...].astype(F32)
    scaled = c * gain[...]
    grad = inv * (scaled - normed * jnp.mean(scaled * normed, axis=-1, keepdims=True))
    gain_part = jnp.sum(c * normed, axis=0, keepdims=True)
    out[0:LAT, :] = grad.T.astype(BF)
    out[LAT:COLS, :] = rope[...]
    high = gain_part.astype(BF)
    low = (gain_part - high.astype(F32)).astype(BF)
    row = lax.broadcasted_iota(jnp.int32, (16, LAT), 0)
    high = jnp.broadcast_to(high.astype(F32), (16, LAT))
    low = jnp.broadcast_to(low.astype(F32), (16, LAT))
    both = jnp.where(row == 0, high, jnp.where(row == 1, low, 0.0))
    out[COLS:EXT, :] = both.astype(BF)


def latent_step(hidden, weight, cot, gain, rope, earlier):
    inside = pl.BlockSpec(memory_space=pltpu.VMEM)
    return pl.pallas_call(
        latent_kernel,
        in_specs=[ANYWHERE, ANYWHERE, inside, inside, inside, LATER],
        out_shape=jax.ShapeDtypeStruct((EXT, TOK), BF),
        scratch_shapes=[
            pltpu.VMEM((TOK, WIDTH), BF),
            pltpu.VMEM((LAT, WIDTH), BF),
            pltpu.SemaphoreType.DMA((2, PARTS)),
        ],
        compiler_params=params(60),
        cost_estimate=cost(0, 1_000),
        name="latent_grad",
    )(hidden, weight, cot, gain, rope, earlier)


def weight_kernel(
    hidden,
    other,
    grad,
    grad_other,
    own_a,
    send_a,
    own_b,
    send_b,
    tiles,
    turned,
    first_a,
    rest_a,
    keep_b,
    give_b,
    gain,
    in_sems,
    out_sems,
    grad_sems,
):
    z, y, core = place()
    steps = [(k, e) for k in (1, 2, 3, 0) for e in (1, 0)]
    incoming = []
    for i, (k, e) in enumerate(steps):
        cols = columns(2 * ((z + k) & 3) + (y ^ e), core)
        incoming.append(
            (
                pltpu.make_async_copy(
                    hidden.at[:, cols], tiles.at[i, pl.ds(0, TOK)], in_sems.at[0, i]
                ),
                pltpu.make_async_copy(
                    other.at[:, cols], tiles.at[i, pl.ds(TOK, TOK)], in_sems.at[1, i]
                ),
            )
        )
    grads = [
        pltpu.make_async_copy(grad, turned.at[:, pl.ds(0, TOK)], grad_sems.at[0]),
        pltpu.make_async_copy(grad_other, turned.at[:, pl.ds(TOK, TOK)], grad_sems.at[1]),
    ]
    start_all(grads)
    for pair in incoming[:2]:
        start_all(pair)
    wait_all(grads)

    sums = jnp.zeros((1, LAT), F32)
    for at in (0, TOK):
        pair = turned[COLS:EXT, at : at + TOK].astype(F32)
        sums = sums + pair[0:1] + pair[1:2]
    gain[...] = jnp.zeros_like(gain)
    for i in range(4):
        gain[i : i + 1, :] = sums[:, 128 * i : 128 * i + 128]

    lane = lax.broadcasted_iota(jnp.int32, (HALF // 2, 128), 1)
    first = core == 0

    def packed(full):
        col = [full[:, 128 * j : 128 * j + 128] for j in range(4)]
        edge = jnp.where(first, col[3], col[0])
        top, low = edge[: HALF // 2], edge[HALF // 2 :]
        left = jnp.where(first, top, pltpu.roll(top, 64, 1))
        right = jnp.where(first, pltpu.roll(low, 64, 1), low)
        return [jnp.where(first, col[i], col[i + 1]) for i in range(3)] + [
            jnp.where(lane < 64, left, right)
        ]

    def put(ref, parts):
        at = 0
        for part in parts:
            n = part.shape[0]
            ref[at : at + n, :] = part.astype(ref.dtype)
            at += n

    outgoing = []
    for i, (k, e) in enumerate(steps):
        wait_all(incoming[i])
        if i + 2 < len(steps):
            start_all(incoming[i + 2])
        whole = jnp.dot(turned[:COLS, :], tiles[i], preferred_element_type=F32)
        buffer_a = first_a.at[e] if k == 0 else rest_a.at[2 * (k - 1) + e]
        buffer_b = keep_b.at[k] if e == 0 else give_b.at[k]
        put(buffer_a, packed(whole[:HALF]))
        put(buffer_b, packed(whole[HALF:]) + [gain[...]])
        to_a = own_a.at[e] if k == 0 else send_a.at[(z + k) & 3, e]
        to_b = (own_b, send_b)[e].at[(z + k) & 3]
        outgoing.append(pltpu.make_async_copy(buffer_a, to_a, out_sems.at[0, i]))
        outgoing.append(pltpu.make_async_copy(buffer_b, to_b, out_sems.at[1, i]))
        start_all(outgoing[-2:])
    wait_all(outgoing)


def weight_step(hidden, other, grad, grad_other):
    return pl.pallas_call(
        weight_kernel,
        in_specs=[ANYWHERE] * 4,
        out_specs=[ANYWHERE] * 4,
        out_shape=[
            jax.ShapeDtypeStruct((2, ROWS_A, 128), F32),
            jax.ShapeDtypeStruct((4, 2, ROWS_A, 128), BF),
            jax.ShapeDtypeStruct((4, ROWS_B, 128), F32),
            jax.ShapeDtypeStruct((4, ROWS_B, 128), BF),
        ],
        scratch_shapes=[
            pltpu.VMEM((8, 2 * TOK, TILE), BF),
            pltpu.VMEM((EXT, 2 * TOK), BF),
            pltpu.VMEM((2, ROWS_A, 128), F32),
            pltpu.VMEM((6, ROWS_A, 128), BF),
            pltpu.VMEM((4, ROWS_B, 128), F32),
            pltpu.VMEM((4, ROWS_B, 128), BF),
            pltpu.VMEM((16, 128), F32),
            pltpu.SemaphoreType.DMA((2, 8)),
            pltpu.SemaphoreType.DMA((2, 8)),
            pltpu.SemaphoreType.DMA((2,)),
        ],
        compiler_params=params(60),
        cost_estimate=cost(0, 1_000),
        name="weight_grad",
    )(hidden, other, grad, grad_other)


def received_sum(own, parts, z):
    for other in range(4):
        own = own + jnp.where(z == other, 0.0, parts[other].astype(F32))
    return own


def adamw(master, first, second, grad):
    new_first = beta_one * first + (1.0 - beta_one) * grad
    new_second = beta_two * second + (1.0 - beta_two) * grad * grad
    first_hat = new_first / (1.0 - beta_one**adam_count)
    second_hat = new_second / (1.0 - beta_two**adam_count)
    new_master = master - learn_rate * (
        first_hat / (jnp.sqrt(second_hat) + adam_eps) + decay_rate * master
    )
    return (new_master, new_first, new_second)


def adam_kernel(own_a, own_b, far, *rest):
    state, outs, gain_out = rest[:3], rest[3:6], rest[6]
    sum_a, sum_b, sum_far, held, new, grad, gain, sems, out_sems, gain_sem = rest[7:]
    sums = [
        pltpu.make_async_copy(source, target, sems.at[i])
        for i, (source, target) in enumerate(((own_a, sum_a), (own_b, sum_b), (far, sum_far)))
    ]
    loads = [
        pltpu.make_async_copy(ref, held.at[i], sems.at[3 + i]) for i, ref in enumerate(state)
    ]
    start_all(sums + loads)
    wait_all(sums)
    total_a = sum_a[...] + sum_far[:ROWS_A, :].astype(F32)
    total_b = sum_b[...] + sum_far[ROWS_A:, :].astype(F32)
    _, _, core = place()
    gain[...] = total_b[ROWS_A : ROWS_A + 8]
    gain_copy = pltpu.make_async_copy(gain, gain_out, gain_sem)
    gain_copy.start()

    def both(lo, n):
        return [total[lo : lo + n] for total in (total_a, total_b)]

    for i in range(3):
        block = jnp.concatenate(both(i * HALF, HALF), axis=0)
        grad[pl.ds(pl.multiple_of(64 * core + 128 * i, 64), 128), :] = block.T
    edge = []
    for part in both(3 * HALF, HALF // 2):
        edge += [part, pltpu.roll(part, 64, 1)]
    block = jnp.concatenate(edge, axis=0)
    grad[pl.ds(pl.multiple_of(384 * (1 - core), 64), 64), :] = block.T[:64]
    wait_all(loads)
    rows, stores = held.shape[1] // 4, []
    for n in range(4):
        at = slice(n * rows, n * rows + rows)
        values = adamw(held[0, at], held[1, at], held[2, at], grad[at])
        for i, value in enumerate(values):
            new[i, at] = value
            part = pl.ds(n * rows, rows)
            stores.append(
                pltpu.make_async_copy(new.at[i, part], outs[i].at[part], out_sems.at[n, i])
            )
            stores[-1].start()
    wait_all(stores)
    gain_copy.wait()


def adam_step(own_a, own_b, far, master, first, second):
    shape = jax.ShapeDtypeStruct(master.shape, F32)
    return pl.pallas_call(
        adam_kernel,
        in_specs=[LATER] * 6,
        out_specs=[LATER] * 4,
        out_shape=[shape] * 3 + [jax.ShapeDtypeStruct((8, 128), F32)],
        scratch_shapes=[
            pltpu.VMEM(own_a.shape, F32),
            pltpu.VMEM(own_b.shape, F32),
            pltpu.VMEM(far.shape, BF),
            pltpu.VMEM((3, *master.shape), F32),
            pltpu.VMEM((3, *master.shape), F32),
            pltpu.VMEM(master.shape, F32),
            pltpu.VMEM((8, 128), F32),
            pltpu.SemaphoreType.DMA((6,)),
            pltpu.SemaphoreType.DMA((4, 3)),
            pltpu.SemaphoreType.DMA,
        ],
        compiler_params=params(60),
        cost_estimate=cost(0, 9_000_000),
        name="adamw",
    )(own_a, own_b, far, master, first, second)


def input_step(grad, pieces, earlier, begun=None):
    places = [(n, i, dz, e) for n, piece in enumerate(pieces) for i, (dz, e) in enumerate(piece[2])]
    count, arrays = len(places), len(pieces)

    def kernel(grad, *rest):
        halves = rest[: 2 * arrays]
        out, flag, held, blocks, in_sems, out_sems = rest[-6:]
        z, y, core = place()
        incoming = []
        for at, (n, i, _, _) in enumerate(places):
            for half in range(2):
                slot = core ^ half
                rows = pl.ds(pl.multiple_of(slot * HALF, HALF), HALF)
                incoming.append(
                    pltpu.make_async_copy(
                        halves[2 * n + half].at[i], held.at[at, rows], in_sems.at[at, half]
                    )
                )
        start_all(incoming)
        flag[...] = jnp.zeros_like(flag)
        turned = grad[:COLS, :].astype(F32).T.astype(BF)
        outgoing = []
        for at, (_, _, dz, e) in enumerate(places):
            wait_all(incoming[2 * at : 2 * at + 2])
            blocks[at] = jnp.dot(turned, held[at], preferred_element_type=F32).astype(BF)
            block = 2 * ((z + dz) & 3) + (y ^ e)
            cols = pl.ds(pl.multiple_of(block * BLOCK, BLOCK), BLOCK)
            outgoing.append(
                pltpu.make_async_copy(blocks.at[at], out.at[:, cols], out_sems.at[at])
            )
            outgoing[-1].start()
        wait_all(outgoing)

    inside = pl.BlockSpec(memory_space=pltpu.VMEM)
    operands = [grad]
    for own, far, _ in pieces:
        operands += [own, far]
    halves = len(operands) - 1
    operands += earlier + ([] if begun is None else [begun])
    return pl.pallas_call(
        kernel,
        in_specs=[inside]
        + [ANYWHERE] * halves
        + [LATER] * len(earlier)
        + ([] if begun is None else [ANYWHERE]),
        out_specs=[ANYWHERE, inside],
        out_shape=[jax.ShapeDtypeStruct((TOK, WIDTH), BF), FLAG],
        scratch_shapes=[
            pltpu.VMEM((count, COLS, BLOCK), BF),
            pltpu.VMEM((count, TOK, BLOCK), BF),
            pltpu.SemaphoreType.DMA((count, 2)),
            pltpu.SemaphoreType.DMA((count,)),
        ],
        input_output_aliases={} if begun is None else {len(operands) - 1: 0},
        compiler_params=params(60),
        cost_estimate=cost(TOK * WIDTH * COLS, 8_000_000),
        name="input_grad",
    )(*operands)


def rope_step(rope_cot):
    half = ROPE // 2
    position = jnp.arange(TOK).astype(F32)
    freqs = 10000.0 ** (-2.0 * jnp.arange(half).astype(F32) / ROPE)
    angle = freqs[:, None] * position[None, :]
    cosine = jnp.cos(angle)
    sine = jnp.sin(angle)
    rope = rope_cot.T.astype(F32)
    first, second = rope[:half], rope[half:]
    return jnp.concatenate(
        [first * cosine + second * sine, second * cosine - first * sine], axis=0
    ).astype(BF)


def on_device(
    hidden_in,
    weight,
    gain,
    latent_cot,
    rope_cot,
    master_weight,
    first_moment,
    second_moment,
    gain_master,
    gain_first,
    gain_second,
):
    shard = lax.axis_index("dp")
    hidden = hidden_in[0]
    turned = weight[0].T
    other = moved(hidden, to_core)
    groups = [[(0, 0), (0, 1)], [(2, 0), (2, 1)]]
    cut_1, cut_2 = cut_weight(turned, groups)
    rest_1 = moved(cut_1, to_before_near)
    rope = rope_step(rope_cot[0])
    grad = latent_step(hidden, turned, latent_cot[0], gain, rope, cut_1)
    grad_other = moved(grad, to_core)

    def both(value, *blocks):
        return value, moved(value, to_core), blocks

    own_a, send_a, own_b, send_b = weight_step(hidden, other, grad, grad_other)
    z = shard >> 2
    along_z = [[4 * z + k for z in range(4)] for k in range(4)]

    def exchanged(value):
        return lax.all_to_all(value, "dp", 0, 0, axis_index_groups=along_z, tiled=True)

    ra = exchanged(send_a)
    rb = moved(after(send_b, rest_1, mib=62), to_ylo)
    rest_2 = moved(after(cut_2, own_a, mib=62), to_before_near)
    piece_2 = both(rest_2, *groups[1])
    send_b = (own_b + rb.astype(F32)).astype(BF)
    grad_next = moved(after(grad, rb, mib=1), to_before)
    rz = exchanged(send_b)
    ra = after(ra, grad_next)
    send_a = received_sum(own_a[1], ra[:, 1], z).astype(BF)
    ry = moved(send_a, to_ylo)
    total_a = received_sum(own_a[0], ra[:, 0], z) + ry.astype(F32)
    keep_b = lax.dynamic_index_in_dim(own_b, z, 0, False)
    keep_b += lax.dynamic_index_in_dim(rb, z, 0, False).astype(F32)
    total_b = received_sum(keep_b, rz, z)
    send = jnp.concatenate([total_a, total_b], axis=0).astype(BF)
    far = moved(send, to_mirror)
    here = after(rest_1, send_a, mib=62)
    above, below = moved(here, to_z(-1)), moved(here, to_z(1))
    pieces = [both(here, *groups[0]), piece_2]
    received, is_begun = input_step(grad_next, pieces, [send])
    above = after(above, is_begun, far, mib=62)
    below = after(below, is_begun, far, mib=62)
    pieces = [both(above, (1, 0), (1, 1)), both(below, (3, 0), (3, 1))]
    received, _ = input_step(grad_next, pieces, [], received)
    next_master, next_first, next_second, gain_rows = adam_step(
        total_a, total_b, far, master_weight[0], first_moment[0], second_moment[0]
    )
    gain_total = lax.dynamic_slice(gain_rows[:4].reshape(LAT), (shard * 32,), (32,))
    next_gain = adamw(gain_master[0], gain_first[0], gain_second[0], gain_total)
    return (
        received[None],
        next_master[None],
        next_first[None],
        next_second[None],
        *(value[None] for value in next_gain),
    )


def solution(mesh):
    tokens, shared = P("pipe", "dp", None), P("pipe", None)
    split = P("pipe", "dp")
    return jax.shard_map(
        on_device,
        mesh=mesh,
        in_specs=(tokens, P("pipe", None, None), shared) + (tokens,) * 5 + (split,) * 3,
        out_specs=(tokens,) * 4 + (split,) * 3,
        check_vma=False,
    )
```

```python
import jax
import jax.numpy as jnp
from jax import lax
from jax.experimental import pallas as pl
from jax.experimental.pallas import tpu as pltpu
from jax.sharding import PartitionSpec as P

beta_one = 0.9
beta_two = 0.95
adam_count = 10
learn_rate = 0.00022
adam_eps = 1e-08
decay_rate = 0.1

RANKS, SHARDS = 8, 16
TOK, WIDTH, LAT, ROPE = 512, 7168, 512, 64
COLS = LAT + ROPE
BLOCK = WIDTH // 8
TILE = 512
HALF = COLS // 2
ROWS_A = 3 * HALF + HALF // 2
ROWS_B = ROWS_A + 16
EXT = COLS + 16
BF, F32 = jnp.bfloat16, jnp.float32
MIB = 1 << 20


def params(mib):
    return pltpu.CompilerParams(vmem_limit_bytes=mib * MIB)


def cost(flops, moved):
    return pl.CostEstimate(flops=flops, bytes_accessed=moved, transcendentals=0)


def moved(value, target):
    pairs = []
    for r in range(RANKS):
        for d in range(SHARDS):
            to = target(r, d)
            if 0 <= to[0] < RANKS:
                pairs.append((r * SHARDS + d, to[0] * SHARDS + to[1]))
    return lax.ppermute(value, ("pipe", "dp"), pairs)


def to_core(r, d):
    return r, d ^ 1


def to_ylo(r, d):
    return r, d ^ 2


def to_z(steps):
    return lambda r, d: (r, (d + 4 * steps) % SHARDS)


def to_mirror(r, d):
    return RANKS - 1 - r, d


def to_before(r, d):
    return r - 1, d


def to_before_near(r, d):
    return r - 1, d ^ 2


FLAG = jax.ShapeDtypeStruct((8, 128), F32)
ANYWHERE = pl.BlockSpec(memory_space=pltpu.HBM)
LATER = pl.BlockSpec(memory_space=pl.ANY)


def place():
    shard = lax.axis_index("dp")
    return shard >> 2, (shard >> 1) & 1, shard & 1


def columns(block, core):
    return pl.ds(pl.multiple_of(block * BLOCK + 384 * core, 128), TILE)


def start_all(copies):
    for copy in copies:
        copy.start()


def wait_all(copies):
    for copy in copies:
        copy.wait()


def after(value, *earlier, mib=1):
    def kernel(*refs):
        pass

    return pl.pallas_call(
        kernel,
        in_specs=[ANYWHERE] + [LATER] * len(earlier),
        out_specs=ANYWHERE,
        out_shape=jax.ShapeDtypeStruct(value.shape, value.dtype),
        input_output_aliases={0: 0},
        compiler_params=params(mib),
        cost_estimate=cost(0, 0),
        name="after",
    )(value, *earlier)


def cut_weight(weight, groups):
    def kernel(weight, *rest):
        outs, sems = rest[:-1], rest[-1]
        z, y, core = place()
        rows = pl.ds(pl.multiple_of(core * HALF, HALF), HALF)
        copies = []
        for out, group in zip(outs, groups):
            for i, (dz, e) in enumerate(group):
                block = 2 * ((z + dz) & 3) + ((1 - y) ^ e)
                cols = pl.ds(pl.multiple_of(block * BLOCK, BLOCK), BLOCK)
                sem = sems.at[len(copies)]
                copies.append(pltpu.make_async_copy(weight.at[rows, cols], out.at[i], sem))
        start_all(copies)
        wait_all(copies)

    return pl.pallas_call(
        kernel,
        in_specs=[ANYWHERE],
        out_shape=[jax.ShapeDtypeStruct((len(group), HALF, BLOCK), BF) for group in groups],
        scratch_shapes=[pltpu.SemaphoreType.DMA((sum(len(group) for group in groups),))],
        compiler_params=params(60),
        cost_estimate=cost(0, 1_000),
        name="cut_weight",
    )(weight)


PARTS = 7
PART = WIDTH // PARTS


def latent_kernel(hidden, weight, cot, gain, rope, earlier, out, tokens, matrix, sems):
    copies = []
    for i in range(PARTS):
        cols = pl.ds(i * PART, PART)
        copies.append(
            (
                pltpu.make_async_copy(hidden.at[:, cols], tokens.at[:, cols], sems.at[0, i]),
                pltpu.make_async_copy(
                    weight.at[pl.ds(0, LAT), cols], matrix.at[:, cols], sems.at[1, i]
                ),
            )
        )
    for pair in copies:
        start_all(pair)
    latent = jnp.zeros((TOK, LAT), F32)
    for i in range(PARTS):
        wait_all(copies[i])
        cols = slice(i * PART, i * PART + PART)
        latent += lax.dot_general(
            tokens[:, cols],
            matrix[:, cols],
            (((1,), (1,)), ((), ())),
            preferred_element_type=F32,
        )
    inv = lax.rsqrt(jnp.mean(latent * latent, axis=-1, keepdims=True) + 1e-06)
    normed = latent * inv
    c = cot[...].astype(F32)
    scaled = c * gain[...]
    grad = inv * (scaled - normed * jnp.mean(scaled * normed, axis=-1, keepdims=True))
    gain_part = jnp.sum(c * normed, axis=0, keepdims=True)
    out[0:LAT, :] = grad.T.astype(BF)
    out[LAT:COLS, :] = rope[...]
    high = gain_part.astype(BF)
    low = (gain_part - high.astype(F32)).astype(BF)
    row = lax.broadcasted_iota(jnp.int32, (16, LAT), 0)
    high = jnp.broadcast_to(high.astype(F32), (16, LAT))
    low = jnp.broadcast_to(low.astype(F32), (16, LAT))
    both = jnp.where(row == 0, high, jnp.where(row == 1, low, 0.0))
    out[COLS:EXT, :] = both.astype(BF)


def latent_step(hidden, weight, cot, gain, rope, earlier):
    inside = pl.BlockSpec(memory_space=pltpu.VMEM)
    return pl.pallas_call(
        latent_kernel,
        in_specs=[ANYWHERE, ANYWHERE, inside, inside, inside, LATER],
        out_shape=jax.ShapeDtypeStruct((EXT, TOK), BF),
        scratch_shapes=[
            pltpu.VMEM((TOK, WIDTH), BF),
            pltpu.VMEM((LAT, WIDTH), BF),
            pltpu.SemaphoreType.DMA((2, PARTS)),
        ],
        compiler_params=params(60),
        cost_estimate=cost(0, 1_000),
        name="latent_grad",
    )(hidden, weight, cot, gain, rope, earlier)


def weight_kernel(
    hidden,
    other,
    grad,
    grad_other,
    own_a,
    send_a,
    own_b,
    send_b,
    tiles,
    turned,
    first_a,
    rest_a,
    keep_b,
    give_b,
    gain,
    in_sems,
    out_sems,
    grad_sems,
):
    z, y, core = place()
    steps = [(k, e) for k in (1, 2, 3, 0) for e in (1, 0)]
    incoming = []
    for i, (k, e) in enumerate(steps):
        cols = columns(2 * ((z + k) & 3) + (y ^ e), core)
        incoming.append(
            (
                pltpu.make_async_copy(
                    hidden.at[:, cols], tiles.at[i, pl.ds(0, TOK)], in_sems.at[0, i]
                ),
                pltpu.make_async_copy(
                    other.at[:, cols], tiles.at[i, pl.ds(TOK, TOK)], in_sems.at[1, i]
                ),
            )
        )
    grads = [
        pltpu.make_async_copy(grad, turned.at[:, pl.ds(0, TOK)], grad_sems.at[0]),
        pltpu.make_async_copy(grad_other, turned.at[:, pl.ds(TOK, TOK)], grad_sems.at[1]),
    ]
    start_all(grads)
    for pair in incoming[:2]:
        start_all(pair)
    wait_all(grads)

    sums = jnp.zeros((1, LAT), F32)
    for at in (0, TOK):
        pair = turned[COLS:EXT, at : at + TOK].astype(F32)
        sums = sums + pair[0:1] + pair[1:2]
    gain[...] = jnp.zeros_like(gain)
    for i in range(4):
        gain[i : i + 1, :] = sums[:, 128 * i : 128 * i + 128]

    lane = lax.broadcasted_iota(jnp.int32, (HALF // 2, 128), 1)
    first = core == 0

    def packed(full):
        col = [full[:, 128 * j : 128 * j + 128] for j in range(4)]
        edge = jnp.where(first, col[3], col[0])
        top, low = edge[: HALF // 2], edge[HALF // 2 :]
        left = jnp.where(first, top, pltpu.roll(top, 64, 1))
        right = jnp.where(first, pltpu.roll(low, 64, 1), low)
        return [jnp.where(first, col[i], col[i + 1]) for i in range(3)] + [
            jnp.where(lane < 64, left, right)
        ]

    def put(ref, parts):
        at = 0
        for part in parts:
            n = part.shape[0]
            ref[at : at + n, :] = part.astype(ref.dtype)
            at += n

    outgoing = []
    for i, (k, e) in enumerate(steps):
        wait_all(incoming[i])
        if i + 2 < len(steps):
            start_all(incoming[i + 2])
        whole = jnp.dot(turned[:COLS, :], tiles[i], preferred_element_type=F32)
        buffer_a = first_a.at[e] if k == 0 else rest_a.at[2 * (k - 1) + e]
        buffer_b = keep_b.at[k] if e == 0 else give_b.at[k]
        put(buffer_a, packed(whole[:HALF]))
        put(buffer_b, packed(whole[HALF:]) + [gain[...]])
        to_a = own_a.at[e] if k == 0 else send_a.at[(z + k) & 3, e]
        to_b = (own_b, send_b)[e].at[(z + k) & 3]
        outgoing.append(pltpu.make_async_copy(buffer_a, to_a, out_sems.at[0, i]))
        outgoing.append(pltpu.make_async_copy(buffer_b, to_b, out_sems.at[1, i]))
        start_all(outgoing[-2:])
    wait_all(outgoing)


def weight_step(hidden, other, grad, grad_other):
    return pl.pallas_call(
        weight_kernel,
        in_specs=[ANYWHERE] * 4,
        out_specs=[ANYWHERE] * 4,
        out_shape=[
            jax.ShapeDtypeStruct((2, ROWS_A, 128), F32),
            jax.ShapeDtypeStruct((4, 2, ROWS_A, 128), BF),
            jax.ShapeDtypeStruct((4, ROWS_B, 128), F32),
            jax.ShapeDtypeStruct((4, ROWS_B, 128), BF),
        ],
        scratch_shapes=[
            pltpu.VMEM((8, 2 * TOK, TILE), BF),
            pltpu.VMEM((EXT, 2 * TOK), BF),
            pltpu.VMEM((2, ROWS_A, 128), F32),
            pltpu.VMEM((6, ROWS_A, 128), BF),
            pltpu.VMEM((4, ROWS_B, 128), F32),
            pltpu.VMEM((4, ROWS_B, 128), BF),
            pltpu.VMEM((16, 128), F32),
            pltpu.SemaphoreType.DMA((2, 8)),
            pltpu.SemaphoreType.DMA((2, 8)),
            pltpu.SemaphoreType.DMA((2,)),
        ],
        compiler_params=params(60),
        cost_estimate=cost(0, 1_000),
        name="weight_grad",
    )(hidden, other, grad, grad_other)


def received_sum(own, parts, z):
    for other in range(4):
        own = own + jnp.where(z == other, 0.0, parts[other].astype(F32))
    return own


def adamw(master, first, second, grad):
    new_first = beta_one * first + (1.0 - beta_one) * grad
    new_second = beta_two * second + (1.0 - beta_two) * grad * grad
    first_hat = new_first / (1.0 - beta_one**adam_count)
    second_hat = new_second / (1.0 - beta_two**adam_count)
    new_master = master - learn_rate * (
        first_hat / (jnp.sqrt(second_hat) + adam_eps) + decay_rate * master
    )
    return (new_master, new_first, new_second)


def adam_kernel(own_a, own_b, far, *rest):
    state, outs, gain_out = rest[:3], rest[3:6], rest[6]
    sum_a, sum_b, sum_far, held, new, grad, gain, sems, out_sems, gain_sem = rest[7:]
    sums = [
        pltpu.make_async_copy(source, target, sems.at[i])
        for i, (source, target) in enumerate(((own_a, sum_a), (own_b, sum_b), (far, sum_far)))
    ]
    loads = [
        pltpu.make_async_copy(ref, held.at[i], sems.at[3 + i]) for i, ref in enumerate(state)
    ]
    start_all(sums + loads)
    wait_all(sums)
    total_a = sum_a[...] + sum_far[:ROWS_A, :].astype(F32)
    total_b = sum_b[...] + sum_far[ROWS_A:, :].astype(F32)
    _, _, core = place()
    gain[...] = total_b[ROWS_A : ROWS_A + 8]
    gain_copy = pltpu.make_async_copy(gain, gain_out, gain_sem)
    gain_copy.start()

    def both(lo, n):
        return [total[lo : lo + n] for total in (total_a, total_b)]

    for i in range(3):
        block = jnp.concatenate(both(i * HALF, HALF), axis=0)
        grad[pl.ds(pl.multiple_of(64 * core + 128 * i, 64), 128), :] = block.T
    edge = []
    for part in both(3 * HALF, HALF // 2):
        edge += [part, pltpu.roll(part, 64, 1)]
    block = jnp.concatenate(edge, axis=0)
    grad[pl.ds(pl.multiple_of(384 * (1 - core), 64), 64), :] = block.T[:64]
    wait_all(loads)
    rows, stores = held.shape[1] // 4, []
    for n in range(4):
        at = slice(n * rows, n * rows + rows)
        values = adamw(held[0, at], held[1, at], held[2, at], grad[at])
        for i, value in enumerate(values):
            new[i, at] = value
            part = pl.ds(n * rows, rows)
            stores.append(
                pltpu.make_async_copy(new.at[i, part], outs[i].at[part], out_sems.at[n, i])
            )
            stores[-1].start()
    wait_all(stores)
    gain_copy.wait()


def adam_step(own_a, own_b, far, master, first, second):
    shape = jax.ShapeDtypeStruct(master.shape, F32)
    return pl.pallas_call(
        adam_kernel,
        in_specs=[LATER] * 6,
        out_specs=[LATER] * 4,
        out_shape=[shape] * 3 + [jax.ShapeDtypeStruct((8, 128), F32)],
        scratch_shapes=[
            pltpu.VMEM(own_a.shape, F32),
            pltpu.VMEM(own_b.shape, F32),
            pltpu.VMEM(far.shape, BF),
            pltpu.VMEM((3, *master.shape), F32),
            pltpu.VMEM((3, *master.shape), F32),
            pltpu.VMEM(master.shape, F32),
            pltpu.VMEM((8, 128), F32),
            pltpu.SemaphoreType.DMA((6,)),
            pltpu.SemaphoreType.DMA((4, 3)),
            pltpu.SemaphoreType.DMA,
        ],
        compiler_params=params(60),
        cost_estimate=cost(0, 9_000_000),
        name="adamw",
    )(own_a, own_b, far, master, first, second)


def input_step(grad, pieces, earlier, begun=None):
    places = [(n, i, dz, e) for n, piece in enumerate(pieces) for i, (dz, e) in enumerate(piece[2])]
    count, arrays = len(places), len(pieces)

    def kernel(grad, *rest):
        halves = rest[: 2 * arrays]
        out, flag, held, blocks, in_sems, out_sems = rest[-6:]
        z, y, core = place()
        incoming = []
        for at, (n, i, _, _) in enumerate(places):
            for half in range(2):
                slot = core ^ half
                rows = pl.ds(pl.multiple_of(slot * HALF, HALF), HALF)
                incoming.append(
                    pltpu.make_async_copy(
                        halves[2 * n + half].at[i], held.at[at, rows], in_sems.at[at, half]
                    )
                )
        start_all(incoming)
        flag[...] = jnp.zeros_like(flag)
        turned = grad[:COLS, :].astype(F32).T.astype(BF)
        outgoing = []
        for at, (_, _, dz, e) in enumerate(places):
            wait_all(incoming[2 * at : 2 * at + 2])
            blocks[at] = jnp.dot(turned, held[at], preferred_element_type=F32).astype(BF)
            block = 2 * ((z + dz) & 3) + (y ^ e)
            cols = pl.ds(pl.multiple_of(block * BLOCK, BLOCK), BLOCK)
            outgoing.append(
                pltpu.make_async_copy(blocks.at[at], out.at[:, cols], out_sems.at[at])
            )
            outgoing[-1].start()
        wait_all(outgoing)

    inside = pl.BlockSpec(memory_space=pltpu.VMEM)
    operands = [grad]
    for own, far, _ in pieces:
        operands += [own, far]
    halves = len(operands) - 1
    operands += earlier + ([] if begun is None else [begun])
    return pl.pallas_call(
        kernel,
        in_specs=[inside]
        + [ANYWHERE] * halves
        + [LATER] * len(earlier)
        + ([] if begun is None else [ANYWHERE]),
        out_specs=[ANYWHERE, inside],
        out_shape=[jax.ShapeDtypeStruct((TOK, WIDTH), BF), FLAG],
        scratch_shapes=[
            pltpu.VMEM((count, COLS, BLOCK), BF),
            pltpu.VMEM((count, TOK, BLOCK), BF),
            pltpu.SemaphoreType.DMA((count, 2)),
            pltpu.SemaphoreType.DMA((count,)),
        ],
        input_output_aliases={} if begun is None else {len(operands) - 1: 0},
        compiler_params=params(60),
        cost_estimate=cost(TOK * WIDTH * COLS, 8_000_000),
        name="input_grad",
    )(*operands)


def rope_step(rope_cot):
    half = ROPE // 2
    position = jnp.arange(TOK).astype(F32)
    freqs = 10000.0 ** (-2.0 * jnp.arange(half).astype(F32) / ROPE)
    angle = freqs[:, None] * position[None, :]
    cosine = jnp.cos(angle)
    sine = jnp.sin(angle)
    rope = rope_cot.T.astype(F32)
    first, second = rope[:half], rope[half:]
    return jnp.concatenate(
        [first * cosine + second * sine, second * cosine - first * sine], axis=0
    ).astype(BF)


def on_device(
    hidden_in,
    weight,
    gain,
    latent_cot,
    rope_cot,
    master_weight,
    first_moment,
    second_moment,
    gain_master,
    gain_first,
    gain_second,
):
    shard = lax.axis_index("dp")
    hidden = hidden_in[0]
    turned = weight[0].T
    other = moved(hidden, to_core)
    groups = [[(0, 0)], [(0, 1), (2, 0), (2, 1)], [(1, 1), (3, 1)]]
    cut_1, cut_2, cut_3 = cut_weight(turned, groups)
    rest_1 = moved(cut_1, to_before_near)
    rope = rope_step(rope_cot[0])
    grad = latent_step(hidden, turned, latent_cot[0], gain, rope, cut_1)
    grad = after(grad, rest_1, mib=62)
    grad_other = moved(grad, to_core)
    grad_next = moved(grad, to_before)

    def both(value, *blocks):
        return value, moved(value, to_core), blocks

    own_a, send_a, own_b, send_b = weight_step(hidden, other, grad, grad_other)
    z = shard >> 2
    along_z = [[4 * z + k for z in range(4)] for k in range(4)]

    def exchanged(value):
        return lax.all_to_all(value, "dp", 0, 0, axis_index_groups=along_z, tiled=True)

    ra = exchanged(send_a)
    rb = moved(after(send_b, grad_next, mib=62), to_ylo)
    rest_2 = moved(after(cut_2, grad_next, mib=62), to_before_near)
    send_b = (own_b + rb.astype(F32)).astype(BF)
    rz = exchanged(send_b)
    send_a = received_sum(own_a[1], ra[:, 1], z).astype(BF)
    ry = moved(send_a, to_ylo)
    rest_2 = after(rest_2, send_a, mib=62)
    piece_2 = both(rest_2, *groups[1])
    rest_3 = moved(after(cut_3, rest_2, mib=62), to_before_near)
    total_a = received_sum(own_a[0], ra[:, 0], z) + ry.astype(F32)
    keep_b = lax.dynamic_index_in_dim(own_b, z, 0, False)
    keep_b += lax.dynamic_index_in_dim(rb, z, 0, False).astype(F32)
    total_b = received_sum(keep_b, rz, z)
    send = jnp.concatenate([total_a, total_b], axis=0).astype(BF)
    far = moved(send, to_mirror)
    here = after(rest_1, total_a, mib=62)
    above, below = moved(here, to_z(-1)), moved(here, to_z(1))
    pieces = [both(here, *groups[0]), piece_2]
    received, is_begun = input_step(grad_next, pieces, [send])
    above = after(above, is_begun, far, mib=62)
    below = after(below, is_begun, far, mib=62)
    rest_3 = after(rest_3, is_begun, mib=62)
    pieces = [both(above, (1, 0)), both(below, (3, 0)), both(rest_3, *groups[2])]
    received, _ = input_step(grad_next, pieces, [], received)
    next_master, next_first, next_second, gain_rows = adam_step(
        total_a, total_b, far, master_weight[0], first_moment[0], second_moment[0]
    )
    gain_total = lax.dynamic_slice(gain_rows[:4].reshape(LAT), (shard * 32,), (32,))
    next_gain = adamw(gain_master[0], gain_first[0], gain_second[0], gain_total)
    return (
        received[None],
        next_master[None],
        next_first[None],
        next_second[None],
        *(value[None] for value in next_gain),
    )


def solution(mesh):
    tokens, shared = P("pipe", "dp", None), P("pipe", None)
    split = P("pipe", "dp")
    return jax.shard_map(
        on_device,
        mesh=mesh,
        in_specs=(tokens, P("pipe", None, None), shared) + (tokens,) * 5 + (split,) * 3,
        out_specs=(tokens,) * 4 + (split,) * 3,
        check_vma=False,
    )
```

```python
import jax
import jax.numpy as jnp
from jax import lax
from jax.experimental import pallas as pl
from jax.experimental.pallas import tpu as pltpu
from jax.sharding import PartitionSpec as P

beta_one = 0.9
beta_two = 0.95
adam_count = 10
learn_rate = 0.00022
adam_eps = 1e-08
decay_rate = 0.1

RANKS, SHARDS = 8, 16
TOK, WIDTH, LAT, ROPE = 512, 7168, 512, 64
COLS = LAT + ROPE
BLOCK = WIDTH // 8
TILE = 512
HALF = COLS // 2
ROWS_A = 3 * HALF + HALF // 2
ROWS_B = ROWS_A + 16
EXT = COLS + 16
BF, F32 = jnp.bfloat16, jnp.float32
MIB = 1 << 20


def params(mib):
    return pltpu.CompilerParams(vmem_limit_bytes=mib * MIB)


def cost(flops, moved):
    return pl.CostEstimate(flops=flops, bytes_accessed=moved, transcendentals=0)


def moved(value, target):
    pairs = []
    for r in range(RANKS):
        for d in range(SHARDS):
            to = target(r, d)
            if 0 <= to[0] < RANKS:
                pairs.append((r * SHARDS + d, to[0] * SHARDS + to[1]))
    return lax.ppermute(value, ("pipe", "dp"), pairs)


def to_core(r, d):
    return r, d ^ 1


def to_ylo(r, d):
    return r, d ^ 2


def to_z(steps):
    return lambda r, d: (r, (d + 4 * steps) % SHARDS)


def to_mirror(r, d):
    return RANKS - 1 - r, d


def to_before(r, d):
    return r - 1, d


def to_before_near(r, d):
    return r - 1, d ^ 2


FLAG = jax.ShapeDtypeStruct((8, 128), F32)
ANYWHERE = pl.BlockSpec(memory_space=pltpu.HBM)
LATER = pl.BlockSpec(memory_space=pl.ANY)


def place():
    shard = lax.axis_index("dp")
    return shard >> 2, (shard >> 1) & 1, shard & 1


def columns(block, core):
    return pl.ds(pl.multiple_of(block * BLOCK + 384 * core, 128), TILE)


def start_all(copies):
    for copy in copies:
        copy.start()


def wait_all(copies):
    for copy in copies:
        copy.wait()


def after(value, *earlier, mib=1):
    def kernel(*refs):
        pass

    return pl.pallas_call(
        kernel,
        in_specs=[ANYWHERE] + [LATER] * len(earlier),
        out_specs=ANYWHERE,
        out_shape=jax.ShapeDtypeStruct(value.shape, value.dtype),
        input_output_aliases={0: 0},
        compiler_params=params(mib),
        cost_estimate=cost(0, 0),
        name="after",
    )(value, *earlier)


def cut_weight(weight, groups):
    def kernel(weight, *rest):
        outs, sems = rest[:-1], rest[-1]
        z, y, core = place()
        rows = pl.ds(pl.multiple_of(core * HALF, HALF), HALF)
        copies = []
        for out, group in zip(outs, groups):
            for i, (dz, e) in enumerate(group):
                block = 2 * ((z + dz) & 3) + ((1 - y) ^ e)
                cols = pl.ds(pl.multiple_of(block * BLOCK, BLOCK), BLOCK)
                sem = sems.at[len(copies)]
                copies.append(pltpu.make_async_copy(weight.at[rows, cols], out.at[i], sem))
        start_all(copies)
        wait_all(copies)

    return pl.pallas_call(
        kernel,
        in_specs=[ANYWHERE],
        out_shape=[jax.ShapeDtypeStruct((len(group), HALF, BLOCK), BF) for group in groups],
        scratch_shapes=[pltpu.SemaphoreType.DMA((sum(len(group) for group in groups),))],
        compiler_params=params(60),
        cost_estimate=cost(0, 1_000),
        name="cut_weight",
    )(weight)


PARTS = 7
PART = WIDTH // PARTS


def latent_kernel(hidden, weight, cot, gain, rope, earlier, out, tokens, matrix, sems):
    copies = []
    for i in range(PARTS):
        cols = pl.ds(i * PART, PART)
        copies.append(
            (
                pltpu.make_async_copy(hidden.at[:, cols], tokens.at[:, cols], sems.at[0, i]),
                pltpu.make_async_copy(
                    weight.at[pl.ds(0, LAT), cols], matrix.at[:, cols], sems.at[1, i]
                ),
            )
        )
    for pair in copies:
        start_all(pair)
    latent = jnp.zeros((TOK, LAT), F32)
    for i in range(PARTS):
        wait_all(copies[i])
        cols = slice(i * PART, i * PART + PART)
        latent += lax.dot_general(
            tokens[:, cols],
            matrix[:, cols],
            (((1,), (1,)), ((), ())),
            preferred_element_type=F32,
        )
    inv = lax.rsqrt(jnp.mean(latent * latent, axis=-1, keepdims=True) + 1e-06)
    normed = latent * inv
    c = cot[...].astype(F32)
    scaled = c * gain[...]
    grad = inv * (scaled - normed * jnp.mean(scaled * normed, axis=-1, keepdims=True))
    gain_part = jnp.sum(c * normed, axis=0, keepdims=True)
    out[0:LAT, :] = grad.T.astype(BF)
    out[LAT:COLS, :] = rope[...]
    high = gain_part.astype(BF)
    low = (gain_part - high.astype(F32)).astype(BF)
    row = lax.broadcasted_iota(jnp.int32, (16, LAT), 0)
    high = jnp.broadcast_to(high.astype(F32), (16, LAT))
    low = jnp.broadcast_to(low.astype(F32), (16, LAT))
    both = jnp.where(row == 0, high, jnp.where(row == 1, low, 0.0))
    out[COLS:EXT, :] = both.astype(BF)


def latent_step(hidden, weight, cot, gain, rope, earlier):
    inside = pl.BlockSpec(memory_space=pltpu.VMEM)
    return pl.pallas_call(
        latent_kernel,
        in_specs=[ANYWHERE, ANYWHERE, inside, inside, inside, LATER],
        out_shape=jax.ShapeDtypeStruct((EXT, TOK), BF),
        scratch_shapes=[
            pltpu.VMEM((TOK, WIDTH), BF),
            pltpu.VMEM((LAT, WIDTH), BF),
            pltpu.SemaphoreType.DMA((2, PARTS)),
        ],
        compiler_params=params(60),
        cost_estimate=cost(0, 1_000),
        name="latent_grad",
    )(hidden, weight, cot, gain, rope, earlier)


def weight_kernel(
    hidden,
    other,
    grad,
    grad_other,
    own_a,
    send_a,
    own_b,
    send_b,
    tiles,
    turned,
    first_a,
    rest_a,
    keep_b,
    give_b,
    gain,
    in_sems,
    out_sems,
    grad_sems,
):
    z, y, core = place()
    steps = [(k, e) for k in (1, 2, 3, 0) for e in (1, 0)]
    incoming = []
    for i, (k, e) in enumerate(steps):
        cols = columns(2 * ((z + k) & 3) + (y ^ e), core)
        incoming.append(
            (
                pltpu.make_async_copy(
                    hidden.at[:, cols], tiles.at[i, pl.ds(0, TOK)], in_sems.at[0, i]
                ),
                pltpu.make_async_copy(
                    other.at[:, cols], tiles.at[i, pl.ds(TOK, TOK)], in_sems.at[1, i]
                ),
            )
        )
    grads = [
        pltpu.make_async_copy(grad, turned.at[:, pl.ds(0, TOK)], grad_sems.at[0]),
        pltpu.make_async_copy(grad_other, turned.at[:, pl.ds(TOK, TOK)], grad_sems.at[1]),
    ]
    start_all(grads)
    for pair in incoming[:2]:
        start_all(pair)
    wait_all(grads)

    sums = jnp.zeros((1, LAT), F32)
    for at in (0, TOK):
        pair = turned[COLS:EXT, at : at + TOK].astype(F32)
        sums = sums + pair[0:1] + pair[1:2]
    gain[...] = jnp.zeros_like(gain)
    for i in range(4):
        gain[i : i + 1, :] = sums[:, 128 * i : 128 * i + 128]

    lane = lax.broadcasted_iota(jnp.int32, (HALF // 2, 128), 1)
    first = core == 0

    def packed(full):
        col = [full[:, 128 * j : 128 * j + 128] for j in range(4)]
        edge = jnp.where(first, col[3], col[0])
        top, low = edge[: HALF // 2], edge[HALF // 2 :]
        left = jnp.where(first, top, pltpu.roll(top, 64, 1))
        right = jnp.where(first, pltpu.roll(low, 64, 1), low)
        return [jnp.where(first, col[i], col[i + 1]) for i in range(3)] + [
            jnp.where(lane < 64, left, right)
        ]

    def put(ref, parts):
        at = 0
        for part in parts:
            n = part.shape[0]
            ref[at : at + n, :] = part.astype(ref.dtype)
            at += n

    outgoing = []
    for i, (k, e) in enumerate(steps):
        wait_all(incoming[i])
        if i + 2 < len(steps):
            start_all(incoming[i + 2])
        whole = jnp.dot(turned[:COLS, :], tiles[i], preferred_element_type=F32)
        buffer_a = first_a.at[e] if k == 0 else rest_a.at[2 * (k - 1) + e]
        buffer_b = keep_b.at[k] if e == 0 else give_b.at[k]
        put(buffer_a, packed(whole[:HALF]))
        put(buffer_b, packed(whole[HALF:]) + [gain[...]])
        to_a = own_a.at[e] if k == 0 else send_a.at[(z + k) & 3, e]
        to_b = (own_b, send_b)[e].at[(z + k) & 3]
        outgoing.append(pltpu.make_async_copy(buffer_a, to_a, out_sems.at[0, i]))
        outgoing.append(pltpu.make_async_copy(buffer_b, to_b, out_sems.at[1, i]))
        start_all(outgoing[-2:])
    wait_all(outgoing)


def weight_step(hidden, other, grad, grad_other):
    return pl.pallas_call(
        weight_kernel,
        in_specs=[ANYWHERE] * 4,
        out_specs=[ANYWHERE] * 4,
        out_shape=[
            jax.ShapeDtypeStruct((2, ROWS_A, 128), F32),
            jax.ShapeDtypeStruct((4, 2, ROWS_A, 128), BF),
            jax.ShapeDtypeStruct((4, ROWS_B, 128), F32),
            jax.ShapeDtypeStruct((4, ROWS_B, 128), BF),
        ],
        scratch_shapes=[
            pltpu.VMEM((8, 2 * TOK, TILE), BF),
            pltpu.VMEM((EXT, 2 * TOK), BF),
            pltpu.VMEM((2, ROWS_A, 128), F32),
            pltpu.VMEM((6, ROWS_A, 128), BF),
            pltpu.VMEM((4, ROWS_B, 128), F32),
            pltpu.VMEM((4, ROWS_B, 128), BF),
            pltpu.VMEM((16, 128), F32),
            pltpu.SemaphoreType.DMA((2, 8)),
            pltpu.SemaphoreType.DMA((2, 8)),
            pltpu.SemaphoreType.DMA((2,)),
        ],
        compiler_params=params(60),
        cost_estimate=cost(0, 1_000),
        name="weight_grad",
    )(hidden, other, grad, grad_other)


def received_sum(own, parts, z):
    for other in range(4):
        own = own + jnp.where(z == other, 0.0, parts[other].astype(F32))
    return own


def adamw(master, first, second, grad):
    new_first = beta_one * first + (1.0 - beta_one) * grad
    new_second = beta_two * second + (1.0 - beta_two) * grad * grad
    first_hat = new_first / (1.0 - beta_one**adam_count)
    second_hat = new_second / (1.0 - beta_two**adam_count)
    new_master = master - learn_rate * (
        first_hat / (jnp.sqrt(second_hat) + adam_eps) + decay_rate * master
    )
    return (new_master, new_first, new_second)


def adam_kernel(own_a, own_b, far, *rest):
    state, outs, gain_out = rest[:3], rest[4:7], rest[7]
    sum_a, sum_b, sum_far, held, new, grad, gain, sems, out_sems, gain_sem = rest[8:]
    sums = [
        pltpu.make_async_copy(source, target, sems.at[i])
        for i, (source, target) in enumerate(((own_a, sum_a), (own_b, sum_b), (far, sum_far)))
    ]
    loads = [
        pltpu.make_async_copy(ref, held.at[i], sems.at[3 + i]) for i, ref in enumerate(state)
    ]
    start_all(sums + loads)
    wait_all(sums)
    total_a = sum_a[...] + sum_far[:ROWS_A, :].astype(F32)
    total_b = sum_b[...] + sum_far[ROWS_A:, :].astype(F32)
    _, _, core = place()
    gain[...] = total_b[ROWS_A : ROWS_A + 8]
    gain_copy = pltpu.make_async_copy(gain, gain_out, gain_sem)
    gain_copy.start()

    def both(lo, n):
        return [total[lo : lo + n] for total in (total_a, total_b)]

    for i in range(3):
        block = jnp.concatenate(both(i * HALF, HALF), axis=0)
        grad[pl.ds(pl.multiple_of(64 * core + 128 * i, 64), 128), :] = block.T
    edge = []
    for part in both(3 * HALF, HALF // 2):
        edge += [part, pltpu.roll(part, 64, 1)]
    block = jnp.concatenate(edge, axis=0)
    grad[pl.ds(pl.multiple_of(384 * (1 - core), 64), 64), :] = block.T[:64]
    wait_all(loads)
    rows, stores = held.shape[1] // 4, []
    for n in range(4):
        at = slice(n * rows, n * rows + rows)
        values = adamw(held[0, at], held[1, at], held[2, at], grad[at])
        for i, value in enumerate(values):
            new[i, at] = value
            part = pl.ds(n * rows, rows)
            stores.append(
                pltpu.make_async_copy(new.at[i, part], outs[i].at[part], out_sems.at[n, i])
            )
            stores[-1].start()
    wait_all(stores)
    gain_copy.wait()


def adam_step(own_a, own_b, far, master, first, second, earlier):
    shape = jax.ShapeDtypeStruct(master.shape, F32)
    return pl.pallas_call(
        adam_kernel,
        in_specs=[LATER] * 7,
        out_specs=[LATER] * 4,
        out_shape=[shape] * 3 + [jax.ShapeDtypeStruct((8, 128), F32)],
        scratch_shapes=[
            pltpu.VMEM(own_a.shape, F32),
            pltpu.VMEM(own_b.shape, F32),
            pltpu.VMEM(far.shape, BF),
            pltpu.VMEM((3, *master.shape), F32),
            pltpu.VMEM((3, *master.shape), F32),
            pltpu.VMEM(master.shape, F32),
            pltpu.VMEM((8, 128), F32),
            pltpu.SemaphoreType.DMA((6,)),
            pltpu.SemaphoreType.DMA((4, 3)),
            pltpu.SemaphoreType.DMA,
        ],
        compiler_params=params(60),
        cost_estimate=cost(0, 9_000_000),
        name="adamw",
    )(own_a, own_b, far, master, first, second, earlier)


def input_step(grad, pieces, earlier, begun=None):
    places = [(n, i, dz, e) for n, piece in enumerate(pieces) for i, (dz, e) in enumerate(piece[2])]
    count, arrays = len(places), len(pieces)

    def kernel(grad, *rest):
        halves = rest[: 2 * arrays]
        out, flag, held, blocks, in_sems, out_sems = rest[-6:]
        z, y, core = place()
        incoming = []
        for at, (n, i, _, _) in enumerate(places):
            for half in range(2):
                slot = core ^ half
                rows = pl.ds(pl.multiple_of(slot * HALF, HALF), HALF)
                incoming.append(
                    pltpu.make_async_copy(
                        halves[2 * n + half].at[i], held.at[at, rows], in_sems.at[at, half]
                    )
                )
        start_all(incoming)
        flag[...] = jnp.zeros_like(flag)
        turned = grad[:COLS, :].astype(F32).T.astype(BF)
        outgoing = []
        for at, (_, _, dz, e) in enumerate(places):
            wait_all(incoming[2 * at : 2 * at + 2])
            blocks[at] = jnp.dot(turned, held[at], preferred_element_type=F32).astype(BF)
            block = 2 * ((z + dz) & 3) + (y ^ e)
            cols = pl.ds(pl.multiple_of(block * BLOCK, BLOCK), BLOCK)
            outgoing.append(
                pltpu.make_async_copy(blocks.at[at], out.at[:, cols], out_sems.at[at])
            )
            outgoing[-1].start()
        wait_all(outgoing)

    inside = pl.BlockSpec(memory_space=pltpu.VMEM)
    operands = [grad]
    for own, far, _ in pieces:
        operands += [own, far]
    halves = len(operands) - 1
    operands += earlier + ([] if begun is None else [begun])
    return pl.pallas_call(
        kernel,
        in_specs=[inside]
        + [ANYWHERE] * halves
        + [LATER] * len(earlier)
        + ([] if begun is None else [ANYWHERE]),
        out_specs=[ANYWHERE, inside],
        out_shape=[jax.ShapeDtypeStruct((TOK, WIDTH), BF), FLAG],
        scratch_shapes=[
            pltpu.VMEM((count, COLS, BLOCK), BF),
            pltpu.VMEM((count, TOK, BLOCK), BF),
            pltpu.SemaphoreType.DMA((count, 2)),
            pltpu.SemaphoreType.DMA((count,)),
        ],
        input_output_aliases={} if begun is None else {len(operands) - 1: 0},
        compiler_params=params(60),
        cost_estimate=cost(TOK * WIDTH * COLS, 8_000_000),
        name="input_grad",
    )(*operands)


def rope_step(rope_cot):
    half = ROPE // 2
    position = jnp.arange(TOK).astype(F32)
    freqs = 10000.0 ** (-2.0 * jnp.arange(half).astype(F32) / ROPE)
    angle = freqs[:, None] * position[None, :]
    cosine = jnp.cos(angle)
    sine = jnp.sin(angle)
    rope = rope_cot.T.astype(F32)
    first, second = rope[:half], rope[half:]
    return jnp.concatenate(
        [first * cosine + second * sine, second * cosine - first * sine], axis=0
    ).astype(BF)


def on_device(
    hidden_in,
    weight,
    gain,
    latent_cot,
    rope_cot,
    master_weight,
    first_moment,
    second_moment,
    gain_master,
    gain_first,
    gain_second,
):
    shard = lax.axis_index("dp")
    hidden = hidden_in[0]
    turned = weight[0].T
    other = moved(hidden, to_core)
    groups = [[(0, 0), (0, 1)], [(2, 0), (2, 1)]]
    cut_1, cut_2 = cut_weight(turned, groups)
    rest_1 = moved(cut_1, to_before_near)
    rope = rope_step(rope_cot[0])
    grad = latent_step(hidden, turned, latent_cot[0], gain, rope, cut_1)
    grad_other = moved(grad, to_core)

    def both(value, *blocks):
        return value, moved(value, to_core), blocks

    own_a, send_a, own_b, send_b = weight_step(hidden, other, grad, grad_other)
    z = shard >> 2
    along_z = [[4 * z + k for z in range(4)] for k in range(4)]

    def exchanged(value):
        return lax.all_to_all(value, "dp", 0, 0, axis_index_groups=along_z, tiled=True)

    ra = exchanged(send_a)
    rb = moved(after(send_b, rest_1, mib=62), to_ylo)
    rest_2 = moved(after(cut_2, own_a, mib=62), to_before_near)
    piece_2 = both(rest_2, *groups[1])
    send_b = (own_b + rb.astype(F32)).astype(BF)
    grad_next = moved(after(grad, rb, mib=1), to_before)
    rz = exchanged(send_b)
    send_a = received_sum(own_a[1], ra[:, 1], z).astype(BF)
    ry = after(moved(send_a, to_ylo), grad_next)
    total_a = received_sum(own_a[0], ra[:, 0], z) + ry.astype(F32)
    keep_b = lax.dynamic_index_in_dim(own_b, z, 0, False)
    keep_b += lax.dynamic_index_in_dim(rb, z, 0, False).astype(F32)
    total_b = received_sum(keep_b, rz, z)
    send = jnp.concatenate([total_a, total_b], axis=0).astype(BF)
    far = moved(send, to_mirror)
    here = after(rest_1, grad_next, mib=62)
    above, below = moved(here, to_z(-1)), moved(here, to_z(1))
    pieces = [both(here, *groups[0]), piece_2]
    received, is_begun = input_step(grad_next, pieces, [send])
    next_master, next_first, next_second, gain_rows = adam_step(
        total_a, total_b, far, master_weight[0], first_moment[0], second_moment[0], is_begun
    )
    above = after(above, is_begun, gain_rows, mib=62)
    below = after(below, is_begun, gain_rows, mib=62)
    pieces = [both(above, (1, 0), (1, 1)), both(below, (3, 0), (3, 1))]
    received, _ = input_step(grad_next, pieces, [], received)
    gain_total = lax.dynamic_slice(gain_rows[:4].reshape(LAT), (shard * 32,), (32,))
    next_gain = adamw(gain_master[0], gain_first[0], gain_second[0], gain_total)
    return (
        received[None],
        next_master[None],
        next_first[None],
        next_second[None],
        *(value[None] for value in next_gain),
    )


def solution(mesh):
    tokens, shared = P("pipe", "dp", None), P("pipe", None)
    split = P("pipe", "dp")
    return jax.shard_map(
        on_device,
        mesh=mesh,
        in_specs=(tokens, P("pipe", None, None), shared) + (tokens,) * 5 + (split,) * 3,
        out_specs=(tokens,) * 4 + (split,) * 3,
        check_vma=False,
    )
```

```python
import jax
import jax.numpy as jnp
from jax import lax
from jax.experimental import pallas as pl
from jax.experimental.pallas import tpu as pltpu
from jax.sharding import PartitionSpec as P

beta_one = 0.9
beta_two = 0.95
adam_count = 10
learn_rate = 0.00022
adam_eps = 1e-08
decay_rate = 0.1

RANKS, SHARDS = 8, 16
TOK, WIDTH, LAT, ROPE = 512, 7168, 512, 64
COLS = LAT + ROPE
BLOCK = WIDTH // 8
TILE = 512
HALF = COLS // 2
ROWS_A = 3 * HALF + HALF // 2
ROWS_B = ROWS_A + 16
EXT = COLS + 16
BF, F32 = jnp.bfloat16, jnp.float32
MIB = 1 << 20


def params(mib):
    return pltpu.CompilerParams(vmem_limit_bytes=mib * MIB)


def cost(flops, moved):
    return pl.CostEstimate(flops=flops, bytes_accessed=moved, transcendentals=0)


def moved(value, target):
    pairs = []
    for r in range(RANKS):
        for d in range(SHARDS):
            to = target(r, d)
            if 0 <= to[0] < RANKS:
                pairs.append((r * SHARDS + d, to[0] * SHARDS + to[1]))
    return lax.ppermute(value, ("pipe", "dp"), pairs)


def to_core(r, d):
    return r, d ^ 1


def to_ylo(r, d):
    return r, d ^ 2


def to_z(steps):
    return lambda r, d: (r, (d + 4 * steps) % SHARDS)


def to_mirror(r, d):
    return RANKS - 1 - r, d


def to_before(r, d):
    return r - 1, d


def to_before_near(r, d):
    return r - 1, d ^ 2


FLAG = jax.ShapeDtypeStruct((8, 128), F32)
ANYWHERE = pl.BlockSpec(memory_space=pltpu.HBM)
LATER = pl.BlockSpec(memory_space=pl.ANY)


def place():
    shard = lax.axis_index("dp")
    return shard >> 2, (shard >> 1) & 1, shard & 1


def columns(block, core):
    return pl.ds(pl.multiple_of(block * BLOCK + 384 * core, 128), TILE)


def start_all(copies):
    for copy in copies:
        copy.start()


def wait_all(copies):
    for copy in copies:
        copy.wait()


def after(value, *earlier, mib=1):
    def kernel(*refs):
        pass

    return pl.pallas_call(
        kernel,
        in_specs=[ANYWHERE] + [LATER] * len(earlier),
        out_specs=ANYWHERE,
        out_shape=jax.ShapeDtypeStruct(value.shape, value.dtype),
        input_output_aliases={0: 0},
        compiler_params=params(mib),
        cost_estimate=cost(0, 0),
        name="after",
    )(value, *earlier)


def cut_weight(weight, groups):
    def kernel(weight, *rest):
        outs, sems = rest[:-1], rest[-1]
        z, y, core = place()
        rows = pl.ds(pl.multiple_of(core * HALF, HALF), HALF)
        copies = []
        for out, group in zip(outs, groups):
            for i, (dz, e) in enumerate(group):
                block = 2 * ((z + dz) & 3) + ((1 - y) ^ e)
                cols = pl.ds(pl.multiple_of(block * BLOCK, BLOCK), BLOCK)
                sem = sems.at[len(copies)]
                copies.append(pltpu.make_async_copy(weight.at[rows, cols], out.at[i], sem))
        start_all(copies)
        wait_all(copies)

    return pl.pallas_call(
        kernel,
        in_specs=[ANYWHERE],
        out_shape=[jax.ShapeDtypeStruct((len(group), HALF, BLOCK), BF) for group in groups],
        scratch_shapes=[pltpu.SemaphoreType.DMA((sum(len(group) for group in groups),))],
        compiler_params=params(60),
        cost_estimate=cost(0, 1_000),
        name="cut_weight",
    )(weight)


PARTS = 7
PART = WIDTH // PARTS


def latent_kernel(hidden, weight, cot, gain, rope, earlier, out, tokens, matrix, sems):
    copies = []
    for i in range(PARTS):
        cols = pl.ds(i * PART, PART)
        copies.append(
            (
                pltpu.make_async_copy(hidden.at[:, cols], tokens.at[:, cols], sems.at[0, i]),
                pltpu.make_async_copy(
                    weight.at[pl.ds(0, LAT), cols], matrix.at[:, cols], sems.at[1, i]
                ),
            )
        )
    for pair in copies:
        start_all(pair)
    latent = jnp.zeros((TOK, LAT), F32)
    for i in range(PARTS):
        wait_all(copies[i])
        cols = slice(i * PART, i * PART + PART)
        latent += lax.dot_general(
            tokens[:, cols],
            matrix[:, cols],
            (((1,), (1,)), ((), ())),
            preferred_element_type=F32,
        )
    inv = lax.rsqrt(jnp.mean(latent * latent, axis=-1, keepdims=True) + 1e-06)
    normed = latent * inv
    c = cot[...].astype(F32)
    scaled = c * gain[...]
    grad = inv * (scaled - normed * jnp.mean(scaled * normed, axis=-1, keepdims=True))
    gain_part = jnp.sum(c * normed, axis=0, keepdims=True)
    out[0:LAT, :] = grad.T.astype(BF)
    out[LAT:COLS, :] = rope[...]
    high = gain_part.astype(BF)
    low = (gain_part - high.astype(F32)).astype(BF)
    row = lax.broadcasted_iota(jnp.int32, (16, LAT), 0)
    high = jnp.broadcast_to(high.astype(F32), (16, LAT))
    low = jnp.broadcast_to(low.astype(F32), (16, LAT))
    both = jnp.where(row == 0, high, jnp.where(row == 1, low, 0.0))
    out[COLS:EXT, :] = both.astype(BF)


def latent_step(hidden, weight, cot, gain, rope, earlier):
    inside = pl.BlockSpec(memory_space=pltpu.VMEM)
    return pl.pallas_call(
        latent_kernel,
        in_specs=[ANYWHERE, ANYWHERE, inside, inside, inside, LATER],
        out_shape=jax.ShapeDtypeStruct((EXT, TOK), BF),
        scratch_shapes=[
            pltpu.VMEM((TOK, WIDTH), BF),
            pltpu.VMEM((LAT, WIDTH), BF),
            pltpu.SemaphoreType.DMA((2, PARTS)),
        ],
        compiler_params=params(60),
        cost_estimate=cost(0, 1_000),
        name="latent_grad",
    )(hidden, weight, cot, gain, rope, earlier)


def weight_kernel(
    hidden,
    other,
    grad,
    grad_other,
    own_a,
    send_a,
    own_b,
    send_b,
    tiles,
    turned,
    first_a,
    rest_a,
    keep_b,
    give_b,
    gain,
    in_sems,
    out_sems,
    grad_sems,
):
    z, y, core = place()
    steps = [(k, e) for k in (1, 2, 3, 0) for e in (1, 0)]
    incoming = []
    for i, (k, e) in enumerate(steps):
        cols = columns(2 * ((z + k) & 3) + (y ^ e), core)
        incoming.append(
            (
                pltpu.make_async_copy(
                    hidden.at[:, cols], tiles.at[i, pl.ds(0, TOK)], in_sems.at[0, i]
                ),
                pltpu.make_async_copy(
                    other.at[:, cols], tiles.at[i, pl.ds(TOK, TOK)], in_sems.at[1, i]
                ),
            )
        )
    grads = [
        pltpu.make_async_copy(grad, turned.at[:, pl.ds(0, TOK)], grad_sems.at[0]),
        pltpu.make_async_copy(grad_other, turned.at[:, pl.ds(TOK, TOK)], grad_sems.at[1]),
    ]
    start_all(grads)
    for pair in incoming[:2]:
        start_all(pair)
    wait_all(grads)

    sums = jnp.zeros((1, LAT), F32)
    for at in (0, TOK):
        pair = turned[COLS:EXT, at : at + TOK].astype(F32)
        sums = sums + pair[0:1] + pair[1:2]
    gain[...] = jnp.zeros_like(gain)
    for i in range(4):
        gain[i : i + 1, :] = sums[:, 128 * i : 128 * i + 128]

    lane = lax.broadcasted_iota(jnp.int32, (HALF // 2, 128), 1)
    first = core == 0

    def packed(full):
        col = [full[:, 128 * j : 128 * j + 128] for j in range(4)]
        edge = jnp.where(first, col[3], col[0])
        top, low = edge[: HALF // 2], edge[HALF // 2 :]
        left = jnp.where(first, top, pltpu.roll(top, 64, 1))
        right = jnp.where(first, pltpu.roll(low, 64, 1), low)
        return [jnp.where(first, col[i], col[i + 1]) for i in range(3)] + [
            jnp.where(lane < 64, left, right)
        ]

    def put(ref, parts):
        at = 0
        for part in parts:
            n = part.shape[0]
            ref[at : at + n, :] = part.astype(ref.dtype)
            at += n

    outgoing = []
    for i, (k, e) in enumerate(steps):
        wait_all(incoming[i])
        if i + 2 < len(steps):
            start_all(incoming[i + 2])
        whole = jnp.dot(turned[:COLS, :], tiles[i], preferred_element_type=F32)
        buffer_a = first_a.at[e] if k == 0 else rest_a.at[2 * (k - 1) + e]
        buffer_b = keep_b.at[k] if e == 0 else give_b.at[k]
        put(buffer_a, packed(whole[:HALF]))
        put(buffer_b, packed(whole[HALF:]) + [gain[...]])
        to_a = own_a.at[e] if k == 0 else send_a.at[(z + k) & 3, e]
        to_b = (own_b, send_b)[e].at[(z + k) & 3]
        outgoing.append(pltpu.make_async_copy(buffer_a, to_a, out_sems.at[0, i]))
        outgoing.append(pltpu.make_async_copy(buffer_b, to_b, out_sems.at[1, i]))
        start_all(outgoing[-2:])
    wait_all(outgoing)


def weight_step(hidden, other, grad, grad_other):
    return pl.pallas_call(
        weight_kernel,
        in_specs=[ANYWHERE] * 4,
        out_specs=[ANYWHERE] * 4,
        out_shape=[
            jax.ShapeDtypeStruct((2, ROWS_A, 128), F32),
            jax.ShapeDtypeStruct((4, 2, ROWS_A, 128), BF),
            jax.ShapeDtypeStruct((4, ROWS_B, 128), F32),
            jax.ShapeDtypeStruct((4, ROWS_B, 128), BF),
        ],
        scratch_shapes=[
            pltpu.VMEM((8, 2 * TOK, TILE), BF),
            pltpu.VMEM((EXT, 2 * TOK), BF),
            pltpu.VMEM((2, ROWS_A, 128), F32),
            pltpu.VMEM((6, ROWS_A, 128), BF),
            pltpu.VMEM((4, ROWS_B, 128), F32),
            pltpu.VMEM((4, ROWS_B, 128), BF),
            pltpu.VMEM((16, 128), F32),
            pltpu.SemaphoreType.DMA((2, 8)),
            pltpu.SemaphoreType.DMA((2, 8)),
            pltpu.SemaphoreType.DMA((2,)),
        ],
        compiler_params=params(60),
        cost_estimate=cost(0, 1_000),
        name="weight_grad",
    )(hidden, other, grad, grad_other)


def received_sum(own, parts, z):
    for other in range(4):
        own = own + jnp.where(z == other, 0.0, parts[other].astype(F32))
    return own


def adamw(master, first, second, grad):
    new_first = beta_one * first + (1.0 - beta_one) * grad
    new_second = beta_two * second + (1.0 - beta_two) * grad * grad
    first_hat = new_first / (1.0 - beta_one**adam_count)
    second_hat = new_second / (1.0 - beta_two**adam_count)
    new_master = master - learn_rate * (
        first_hat / (jnp.sqrt(second_hat) + adam_eps) + decay_rate * master
    )
    return (new_master, new_first, new_second)


def adam_kernel(own_a, own_b, far, *rest):
    state, outs, gain_out = rest[:3], rest[4:7], rest[7]
    sum_a, sum_b, sum_far, held, new, grad, gain, sems, out_sems, gain_sem = rest[8:]
    sums = [
        pltpu.make_async_copy(source, target, sems.at[i])
        for i, (source, target) in enumerate(((own_a, sum_a), (own_b, sum_b), (far, sum_far)))
    ]
    loads = [
        pltpu.make_async_copy(ref, held.at[i], sems.at[3 + i]) for i, ref in enumerate(state)
    ]
    start_all(sums + loads)
    wait_all(sums)
    total_a = sum_a[...] + sum_far[:ROWS_A, :].astype(F32)
    total_b = sum_b[...] + sum_far[ROWS_A:, :].astype(F32)
    _, _, core = place()
    gain[...] = total_b[ROWS_A : ROWS_A + 8]
    gain_copy = pltpu.make_async_copy(gain, gain_out, gain_sem)
    gain_copy.start()

    def both(lo, n):
        return [total[lo : lo + n] for total in (total_a, total_b)]

    for i in range(3):
        block = jnp.concatenate(both(i * HALF, HALF), axis=0)
        grad[pl.ds(pl.multiple_of(64 * core + 128 * i, 64), 128), :] = block.T
    edge = []
    for part in both(3 * HALF, HALF // 2):
        edge += [part, pltpu.roll(part, 64, 1)]
    block = jnp.concatenate(edge, axis=0)
    grad[pl.ds(pl.multiple_of(384 * (1 - core), 64), 64), :] = block.T[:64]
    wait_all(loads)
    rows, stores = held.shape[1] // 4, []
    for n in range(4):
        at = slice(n * rows, n * rows + rows)
        values = adamw(held[0, at], held[1, at], held[2, at], grad[at])
        for i, value in enumerate(values):
            new[i, at] = value
            part = pl.ds(n * rows, rows)
            stores.append(
                pltpu.make_async_copy(new.at[i, part], outs[i].at[part], out_sems.at[n, i])
            )
            stores[-1].start()
    wait_all(stores)
    gain_copy.wait()


def adam_step(own_a, own_b, far, master, first, second, earlier):
    shape = jax.ShapeDtypeStruct(master.shape, F32)
    return pl.pallas_call(
        adam_kernel,
        in_specs=[LATER] * 7,
        out_specs=[LATER] * 4,
        out_shape=[shape] * 3 + [jax.ShapeDtypeStruct((8, 128), F32)],
        scratch_shapes=[
            pltpu.VMEM(own_a.shape, F32),
            pltpu.VMEM(own_b.shape, F32),
            pltpu.VMEM(far.shape, BF),
            pltpu.VMEM((3, *master.shape), F32),
            pltpu.VMEM((3, *master.shape), F32),
            pltpu.VMEM(master.shape, F32),
            pltpu.VMEM((8, 128), F32),
            pltpu.SemaphoreType.DMA((6,)),
            pltpu.SemaphoreType.DMA((4, 3)),
            pltpu.SemaphoreType.DMA,
        ],
        compiler_params=params(60),
        cost_estimate=cost(0, 9_000_000),
        name="adamw",
    )(own_a, own_b, far, master, first, second, earlier)


def input_step(grad, pieces, earlier, begun=None):
    places = [(n, i, dz, e) for n, piece in enumerate(pieces) for i, (dz, e) in enumerate(piece[2])]
    count, arrays = len(places), len(pieces)

    def kernel(grad, *rest):
        halves = rest[: 2 * arrays]
        out, flag, held, blocks, in_sems, out_sems = rest[-6:]
        z, y, core = place()
        incoming = []
        for at, (n, i, _, _) in enumerate(places):
            for half in range(2):
                slot = core ^ half
                rows = pl.ds(pl.multiple_of(slot * HALF, HALF), HALF)
                incoming.append(
                    pltpu.make_async_copy(
                        halves[2 * n + half].at[i], held.at[at, rows], in_sems.at[at, half]
                    )
                )
        start_all(incoming)
        flag[...] = jnp.zeros_like(flag)
        turned = grad[:COLS, :].astype(F32).T.astype(BF)
        outgoing = []
        for at, (_, _, dz, e) in enumerate(places):
            wait_all(incoming[2 * at : 2 * at + 2])
            blocks[at] = jnp.dot(turned, held[at], preferred_element_type=F32).astype(BF)
            block = 2 * ((z + dz) & 3) + (y ^ e)
            cols = pl.ds(pl.multiple_of(block * BLOCK, BLOCK), BLOCK)
            outgoing.append(
                pltpu.make_async_copy(blocks.at[at], out.at[:, cols], out_sems.at[at])
            )
            outgoing[-1].start()
        wait_all(outgoing)

    inside = pl.BlockSpec(memory_space=pltpu.VMEM)
    operands = [grad]
    for own, far, _ in pieces:
        operands += [own, far]
    halves = len(operands) - 1
    operands += earlier + ([] if begun is None else [begun])
    return pl.pallas_call(
        kernel,
        in_specs=[inside]
        + [ANYWHERE] * halves
        + [LATER] * len(earlier)
        + ([] if begun is None else [ANYWHERE]),
        out_specs=[ANYWHERE, inside],
        out_shape=[jax.ShapeDtypeStruct((TOK, WIDTH), BF), FLAG],
        scratch_shapes=[
            pltpu.VMEM((count, COLS, BLOCK), BF),
            pltpu.VMEM((count, TOK, BLOCK), BF),
            pltpu.SemaphoreType.DMA((count, 2)),
            pltpu.SemaphoreType.DMA((count,)),
        ],
        input_output_aliases={} if begun is None else {len(operands) - 1: 0},
        compiler_params=params(60 if begun is None else 36),
        cost_estimate=cost(TOK * WIDTH * COLS, 8_000_000),
        name="input_grad",
    )(*operands)


def rope_step(rope_cot):
    half = ROPE // 2
    position = jnp.arange(TOK).astype(F32)
    freqs = 10000.0 ** (-2.0 * jnp.arange(half).astype(F32) / ROPE)
    angle = freqs[:, None] * position[None, :]
    cosine = jnp.cos(angle)
    sine = jnp.sin(angle)
    rope = rope_cot.T.astype(F32)
    first, second = rope[:half], rope[half:]
    return jnp.concatenate(
        [first * cosine + second * sine, second * cosine - first * sine], axis=0
    ).astype(BF)


def on_device(
    hidden_in,
    weight,
    gain,
    latent_cot,
    rope_cot,
    master_weight,
    first_moment,
    second_moment,
    gain_master,
    gain_first,
    gain_second,
):
    shard = lax.axis_index("dp")
    hidden = hidden_in[0]
    turned = weight[0].T
    other = moved(hidden, to_core)
    groups = [[(0, 0), (0, 1)], [(2, 0), (2, 1)]]
    cut_1, cut_2 = cut_weight(turned, groups)
    rest_1 = moved(cut_1, to_before_near)
    rope = rope_step(rope_cot[0])
    grad = latent_step(hidden, turned, latent_cot[0], gain, rope, cut_1)
    grad_other = moved(grad, to_core)

    def both(value, *blocks):
        return value, moved(value, to_core), blocks

    own_a, send_a, own_b, send_b = weight_step(hidden, other, grad, grad_other)
    z = shard >> 2
    along_z = [[4 * z + k for z in range(4)] for k in range(4)]

    def exchanged(value):
        return lax.all_to_all(value, "dp", 0, 0, axis_index_groups=along_z, tiled=True)

    ra = exchanged(send_a)
    rb = moved(after(send_b, rest_1, mib=62), to_ylo)
    rest_2 = moved(after(cut_2, own_a, mib=62), to_before_near)
    piece_2 = both(rest_2, *groups[1])
    send_b = (own_b + rb.astype(F32)).astype(BF)
    grad_next = moved(after(grad, rb, mib=1), to_before)
    rz = exchanged(send_b)
    send_a = received_sum(own_a[1], ra[:, 1], z).astype(BF)
    ry = after(moved(send_a, to_ylo), grad_next)
    total_a = received_sum(own_a[0], ra[:, 0], z) + ry.astype(F32)
    keep_b = lax.dynamic_index_in_dim(own_b, z, 0, False)
    keep_b += lax.dynamic_index_in_dim(rb, z, 0, False).astype(F32)
    total_b = received_sum(keep_b, rz, z)
    send = jnp.concatenate([total_a, total_b], axis=0).astype(BF)
    far = moved(send, to_mirror)
    here = after(rest_1, grad_next, mib=62)
    above, below = moved(here, to_z(-1)), moved(here, to_z(1))
    pieces = [both(here, *groups[0]), piece_2]
    received, is_begun = input_step(grad_next, pieces, [send])
    next_master, next_first, next_second, gain_rows = adam_step(
        total_a, total_b, far, master_weight[0], first_moment[0], second_moment[0], is_begun
    )
    above = after(above, is_begun, gain_rows, mib=62)
    below = after(below, is_begun, gain_rows, mib=62)
    pieces = [both(above, (1, 0), (1, 1)), both(below, (3, 0), (3, 1))]
    received, _ = input_step(grad_next, pieces, [], received)
    gain_total = lax.dynamic_slice(gain_rows[:4].reshape(LAT), (shard * 32,), (32,))
    next_gain = adamw(gain_master[0], gain_first[0], gain_second[0], gain_total)
    return (
        received[None],
        next_master[None],
        next_first[None],
        next_second[None],
        *(value[None] for value in next_gain),
    )


def solution(mesh):
    tokens, shared = P("pipe", "dp", None), P("pipe", None)
    split = P("pipe", "dp")
    return jax.shard_map(
        on_device,
        mesh=mesh,
        in_specs=(tokens, P("pipe", None, None), shared) + (tokens,) * 5 + (split,) * 3,
        out_specs=(tokens,) * 4 + (split,) * 3,
        check_vma=False,
    )
```
